128 devices in a mesh: bx: 8 (over y, core), by: 16 (over z, x).
Axes of the slice: x: 4, y: 4, z: 4, core: 2. Of those that a mesh axis runs over, the one named last changes fastest.
Arguments:
- features: bfloat16 [256, 8, 8, 8, 128], P(('bx', 'by')), may hold values from -6 to 6
- weight: bfloat16 [27, 128, 128], replicated, may hold values from -0.109375 to 0.109375
- down_weight: bfloat16 [8, 128, 128], replicated, may hold values from -0.1875 to 0.1875
- grad_out: bfloat16 [256, 8, 8, 8, 128], P(('bx', 'by')), may hold values from -6 to 6
- grad_coarse: bfloat16 [256, 64, 128], P(('bx', 'by')), may hold values from -6 to 6
- neighbours: int32 [256, 27], P(('bx', 'by')), may hold values from 0 to 20, as said below
- send_list: int32 [1152, 2], P(('bx', 'by')), may hold values from -1 to 1, as said below
- coarse_dest: int32 [256], P(('bx', 'by')), may hold values from 0 to 15, as said below
- coarse_from: int32 [256], P(('bx', 'by')), may hold values from 0 to 15, as said below
Outputs:
- hidden: bfloat16 [256, 8, 8, 8, 128], P(('bx', 'by'))
- coarse: bfloat16 [256, 64, 128], P(('bx', 'by'))
- grad_features: bfloat16 [256, 8, 8, 8, 128], P(('bx', 'by'))
- grad_weight: float32 [27, 128, 128], replicated
- grad_down: float32 [8, 128, 128], replicated
The draws below stay inside these ranges and needn't reach their ends.
Inputs may be any that keep to these rules, and one draw needn't show every extreme that they name: `neighbours`: entry 13 of a row is the block's own slot. Values under 2 are blocks of the same device; values 2 + 2 e + j name the j-th block that the device at bx offset e div 3 - 1 and by offset e mod 3 - 1 lists toward this device; the value 2 + 9 * 2 means no neighbour. Neighbourhood is symmetric. `send_list`: row 9 d + e lists, in rising order and then -1, exactly the slots of device d that are neighbours of some block of the device at bx offset e div 3 - 1, by offset e mod 3 - 1; row e = 4 is all -1. Some device fills all 2 slots of a row. Slot s of a device goes to coarse slot s of the device in the same bx row with by index coarse_dest; one device sends at most 1 block to one owner, and every device sends exactly 1 to some owner. `coarse_from`: coarse slot m of a device holds slot m of the device in the same bx row with this by index; together with coarse_dest each block reaches exactly one coarse slot.
All inputs are finite; a program needn't handle non-finite values.
Results may differ from the reference program's by a relative error of at most 0.0049.
Values may be sent and summed in bfloat16 or wider, within the bound.
A program may use at most 128 MiB of HBM per device.

```python
import jax
import jax.numpy as jnp
import numpy as np
from jax import lax

C = 128
BE = 8
RUN = 1
BLK_DEV = 2
CAP = 2
CV = 64
NBLK = 256
N_BX = 8
N_BY = 16


def geometry(key):
    key_a, key_b = jax.random.split(key)
    cols_x = 2 * N_BX
    height_span = 3 * RUN + 1
    device_total = N_BX * N_BY
    block_total = BLK_DEV * device_total
    steps_a = jax.random.randint(key_a, (cols_x,), -2, 3)
    steps_b = jax.random.randint(key_b, (N_BY,), -2, 3).at[1].set(0)
    heights = jnp.mod(jnp.cumsum(steps_a)[:, None] + jnp.cumsum(steps_b)[None, :], height_span)
    block_index = jnp.arange(block_total, dtype=jnp.int32)
    device = block_index // BLK_DEV
    slot_ids = block_index % BLK_DEV
    grid_row = device // N_BY
    column = device % N_BY
    pos_x = 2 * grid_row + slot_ids // RUN
    pos_y = column
    pos_z = heights[pos_x, pos_y] + slot_ids % RUN
    table = np.array([(p, q, w) for p in (-1, 0, 1) for q in (-1, 0, 1) for w in (-1, 0, 1)], dtype=np.int32)
    target_x = pos_x[:, None] + jnp.asarray(table[:, 0])[None, :]
    target_y = pos_y[:, None] + jnp.asarray(table[:, 1])[None, :]
    target_z = pos_z[:, None] + jnp.asarray(table[:, 2])[None, :]
    inside = (target_x >= 0) & (target_x < cols_x) & (target_y >= 0) & (target_y < N_BY)
    clip_x = jnp.clip(target_x, 0, cols_x - 1)
    clip_y = jnp.clip(target_y, 0, N_BY - 1)
    start_z = heights[clip_x, clip_y]
    active = inside & (target_z >= start_z) & (target_z < start_z + RUN)
    nb_dev = clip_x // 2 * N_BY + clip_y
    nb_slot = jnp.clip(clip_x % 2 * RUN + target_z - start_z, 0, BLK_DEV - 1)
    row_step = clip_x // 2 - grid_row[:, None]
    col_step = clip_y - column[:, None]
    direction = jnp.clip((row_step + 1) * 3 + col_step + 1, 0, 8)
    remote = active & (nb_dev != device[:, None])
    sender_id = nb_dev * BLK_DEV + nb_slot
    marked = jnp.zeros((block_total, 9), jnp.int32).at[jnp.where(remote, sender_id, block_total), jnp.where(remote, 8 - direction, 0)].set(1, mode='drop')
    marked_dev = marked.reshape(device_total, BLK_DEV, 9)
    rank = (jnp.cumsum(marked_dev, axis=1) - marked_dev).reshape(block_total, 9)
    send_list = jnp.full((device_total, 9, CAP), -1, jnp.int32).at[jnp.broadcast_to(device[:, None], (block_total, 9)), jnp.broadcast_to(jnp.arange(9, dtype=jnp.int32)[None, :], (block_total, 9)), jnp.where(marked == 1, rank, CAP)].set(jnp.broadcast_to(slot_ids[:, None], (block_total, 9)), mode='drop')
    far_rank = rank[jnp.clip(sender_id, 0, block_total - 1), 8 - direction]
    pool_index = jnp.where(remote, BLK_DEV + direction * CAP + far_rank, jnp.where(active, nb_slot, BLK_DEV + 9 * CAP))
    return (pool_index.astype(jnp.int32), send_list.reshape(device_total * 9, CAP).astype(jnp.int32))


def coarse_maps(key):
    device_total = N_BX * N_BY
    block_total = BLK_DEV * device_total
    shuffles = jax.vmap(lambda subkey: jax.random.permutation(subkey, N_BY))(jax.random.split(key, N_BX)).astype(jnp.int32)
    block_index = jnp.arange(block_total, dtype=jnp.int32)
    device = block_index // BLK_DEV
    slot_ids = block_index % BLK_DEV
    grid_row = device // N_BY
    column = device % N_BY
    moves = shuffles[grid_row, slot_ids % N_BY]
    dest = jnp.mod(column + moves, N_BY).astype(jnp.int32)
    source = jnp.mod(column - moves, N_BY).astype(jnp.int32)
    return (dest, source)


def draw_neighbours(key, part):
    shared = geometry(key)
    return shared[0]


def draw_send_list(key, part):
    shared = geometry(key)
    return shared[1]


def draw_coarse_dest(key, part):
    key = jax.random.fold_in(key, 13)
    return coarse_maps(key)[0]


def draw_coarse_from(key, part):
    key = jax.random.fold_in(key, 13)
    return coarse_maps(key)[1]


def steps_of(own_key, extent, pieces, least, high):
    loudness, own = 1.0, jax.random.fold_in(own_key, 6)
    for dim, parts in pieces:
        steps = jnp.exp(jax.random.uniform(jax.random.fold_in(own, dim), (parts,), jnp.float32, least / len(pieces), high / len(pieces)))
        loudness = loudness * jnp.repeat(steps, extent[dim] // parts).reshape([-1 if axis == dim else 1 for axis in range(len(extent))])
    return loudness


def scatter_about(own_key, shape, spread, bound, pieces=(), kind=jnp.bfloat16):
    values = jax.random.normal(own_key, shape, jnp.float32) * spread
    if len(pieces) > 0:
        values = steps_of(own_key, shape, pieces, -0.22, 0.18) * values
    return jnp.clip(values, min=-bound, max=bound).astype(kind)


def setup_inputs(seed: int = 0) -> dict:
    keys = jax.random.split(jax.random.key(seed), 10)
    return {
        "features": scatter_about(keys[0], (NBLK, BE, BE, BE, C), 1.0, 6.0, ((0, 128),)),
        "weight": scatter_about(keys[1], (27, C, C), (27 * C) ** -0.5, 0.109375),
        "down_weight": scatter_about(keys[2], (8, C, C), (8 * C) ** -0.5, 0.1875),
        "grad_out": scatter_about(keys[3], (NBLK, BE, BE, BE, C), 1.0, 6.0, ((0, 128),)),
        "grad_coarse": scatter_about(keys[4], (NBLK, CV, C), 1.0, 6.0, ((0, 128),)),
        "neighbours": draw_neighbours(jax.random.fold_in(keys[9], 71), 0),
        "send_list": draw_send_list(jax.random.fold_in(keys[9], 71), 0),
        "coarse_dest": draw_coarse_dest(jax.random.fold_in(keys[9], 71), 0),
        "coarse_from": draw_coarse_from(jax.random.fold_in(keys[9], 71), 0),
    }


OFFSETS = [(p, q, w) for p in (-1, 0, 1) for q in (-1, 0, 1) for w in (-1, 0, 1)]


def offset_index(offset):
    return (offset[0] + 1) * 9 + (offset[1] + 1) * 3 + offset[2] + 1


def span_of(step, edge_len):
    if step == -1:
        return slice(edge_len - 1, edge_len)
    if step == 1:
        return slice(0, 1)
    return slice(0, edge_len)


def assemble(piece_at):
    planes = []
    for step_x in (-1, 0, 1):
        lines = []
        for step_y in (-1, 0, 1):
            cells = [piece_at((step_x, step_y, step_z)) for step_z in (-1, 0, 1)]
            lines.append(jnp.concatenate(cells, axis=3))
        planes.append(jnp.concatenate(lines, axis=2))
    return jnp.concatenate(planes, axis=1)


def padded_full(extended, block_ids):
    edge_len = extended.shape[1]

    def piece_at(offset):
        whole = jnp.take(extended, block_ids[:, offset_index(offset)], axis=0)
        return whole[:, span_of(offset[0], edge_len), span_of(offset[1], edge_len), span_of(offset[2], edge_len)]

    return assemble(piece_at)


def window(padded, offset, sign):
    edge_len = padded.shape[1] - 2
    starts = [1 + sign * offset[axis_id] for axis_id in range(3)]
    return padded[:, starts[0]:starts[0] + edge_len, starts[1]:starts[1] + edge_len, starts[2]:starts[2] + edge_len]


def conv_rows(padded, weight, sign):
    channels = padded.shape[-1]
    running = None
    for offset in OFFSETS:
        shifted = window(padded, offset, sign).reshape(-1, channels)
        matrix = weight[offset_index(offset)]
        if sign < 0:
            matrix = matrix.T
        term = jnp.dot(shifted, matrix, preferred_element_type=jnp.float32)
        running = term if running is None else running + term
    return running


def contract(left, right):
    return lax.dot_general(left, right, (((0,), (0,)), ((), ())), preferred_element_type=jnp.float32)


def children(hidden):
    block_count, edge_len, channels = hidden.shape[0], hidden.shape[1], hidden.shape[-1]
    half_edge = edge_len // 2
    parted = hidden.reshape(block_count, half_edge, 2, half_edge, 2, half_edge, 2, channels)
    return [parted[:, :, i, :, j, :, l, :].reshape(-1, channels) for i in (0, 1) for j in (0, 1) for l in (0, 1)]


def down_blocks(hidden, down_weight):
    block_count, channels = hidden.shape[0], hidden.shape[-1]
    running = None
    for child_id, rows_in in enumerate(children(hidden)):
        term = jnp.dot(rows_in, down_weight[child_id], preferred_element_type=jnp.float32)
        running = term if running is None else running + term
    return running.reshape(block_count, -1, channels)


def up_blocks(coarse_grad, down_weight, edge_len):
    block_count, channels = coarse_grad.shape[0], coarse_grad.shape[-1]
    half_edge = edge_len // 2
    flat_grad = coarse_grad.reshape(-1, channels)
    parts_list = [jnp.dot(flat_grad, down_weight[child_id].T, preferred_element_type=jnp.float32) for child_id in range(8)]
    stacked = jnp.stack(parts_list).reshape(2, 2, 2, block_count, half_edge, half_edge, half_edge, channels)
    return stacked.transpose(3, 4, 0, 5, 1, 6, 2, 7).reshape(block_count, edge_len, edge_len, edge_len, channels)


def child_products(hidden, coarse_grad):
    channels = hidden.shape[-1]
    flat_grad = coarse_grad.reshape(-1, channels)
    return jnp.stack([contract(rows_in, flat_grad) for rows_in in children(hidden)])


def neighbour_ids(neighbours, send_list):
    block_total = neighbours.shape[0]
    block_index = jnp.arange(block_total, dtype=jnp.int32)
    device = block_index // BLK_DEV
    grid_row = (device // N_BY)[:, None]
    column = (device % N_BY)[:, None]
    is_local = neighbours < BLK_DEV
    remote_index = neighbours - BLK_DEV
    remote = (neighbours >= BLK_DEV) & (neighbours < BLK_DEV + 9 * CAP)
    direction = jnp.clip(remote_index // CAP, 0, 8)
    position = jnp.clip(remote_index % CAP, 0, CAP - 1)
    source_row = jnp.clip(grid_row + direction // 3 - 1, 0, N_BX - 1)
    source_col = jnp.clip(column + direction % 3 - 1, 0, N_BY - 1)
    source_dev = source_row * N_BY + source_col
    source_slot = send_list[source_dev * 9 + 8 - direction, position]
    own_id = device[:, None] * BLK_DEV + neighbours
    far_id = source_dev * BLK_DEV + source_slot
    return jnp.where(is_local, own_id, jnp.where(remote, far_id, -1)).astype(jnp.int32)


def reference(features, weight, down_weight, grad_out, grad_coarse, neighbours, send_list, coarse_dest, coarse_from):
    block_total, edge_len, channels = features.shape[0], features.shape[1], features.shape[-1]
    device_total = N_BX * N_BY
    block_ids = neighbour_ids(neighbours, send_list)
    lookup = jnp.where(block_ids < 0, block_total, block_ids).astype(jnp.int32)
    zero_block = jnp.zeros((1,) + features.shape[1:], features.dtype)
    feat_ext = jnp.concatenate([features, zero_block], axis=0)

    def local_ids(device):
        return lax.dynamic_slice(lookup, (device * BLK_DEV, jnp.int32(0)), (BLK_DEV, 27))

    def forward_one(device):
        return conv_rows(padded_full(feat_ext, local_ids(device)), weight, 1)

    preact = lax.map(forward_one, jnp.arange(device_total, dtype=jnp.int32)).reshape(features.shape)
    hidden = jax.nn.silu(preact).astype(jnp.bfloat16)
    reduced = down_blocks(hidden, down_weight).astype(jnp.bfloat16)
    block_index = jnp.arange(block_total, dtype=jnp.int32)
    slot_ids = block_index % BLK_DEV
    grid_row = (block_index // BLK_DEV) // N_BY
    coarse = reduced[(grid_row * N_BY + coarse_from) * BLK_DEV + slot_ids]
    coarse_grad_here = grad_coarse[(grid_row * N_BY + coarse_dest) * BLK_DEV + slot_ids]
    grad_down = child_products(hidden, coarse_grad_here) / device_total
    sigmoid_pre = jax.nn.sigmoid(preact)
    grad_pre = ((grad_out.astype(jnp.float32) + up_blocks(coarse_grad_here, down_weight, edge_len))
                * sigmoid_pre * (1.0 + preact * (1.0 - sigmoid_pre))).astype(jnp.bfloat16)
    grad_ext = jnp.concatenate([grad_pre, zero_block], axis=0)

    def backward_one(carry, device):
        ids_here = local_ids(device)
        padded_in = padded_full(feat_ext, ids_here)
        padded_grad = padded_full(grad_ext, ids_here)
        own_rows = lax.dynamic_slice_in_dim(grad_pre, device * BLK_DEV, BLK_DEV, 0).reshape(-1, channels)
        grad_here = conv_rows(padded_grad, weight, -1).astype(jnp.bfloat16)
        weight_terms = jnp.stack([contract(window(padded_in, offset, 1).reshape(-1, channels), own_rows) for offset in OFFSETS])
        return carry + weight_terms, grad_here

    start = jnp.zeros((27, channels, channels), jnp.float32)
    grad_weight, grad_features = lax.scan(backward_one, start, jnp.arange(device_total, dtype=jnp.int32))
    grad_weight = grad_weight / device_total
    return hidden, coarse, grad_features.reshape(features.shape), grad_weight, grad_down
```

```python
import functools

import jax
import jax.numpy as jnp
from jax import lax
from jax.experimental import pallas as pl
from jax.experimental.pallas import tpu as pltpu
from jax.sharding import PartitionSpec as P

OFFSETS = [(p, q, w) for p in (-1, 0, 1) for q in (-1, 0, 1) for w in (-1, 0, 1)]


def with_halo(cells, sides, width):
    for axis, dim in sides:
        count = lax.axis_size(axis)
        ends = count - 1
        head = lax.slice_in_dim(cells, 0, width, axis=dim)
        tail = lax.slice_in_dim(cells, cells.shape[dim] - width, cells.shape[dim], axis=dim)
        cells = jnp.concatenate(
            [
                lax.ppermute(tail, axis, [(i, (i + 1) % count) for i in range(ends)]),
                cells,
                lax.ppermute(head, axis, [((i + 1) % count, i) for i in range(ends)]),
            ],
            axis=dim,
        )
    return cells


def offset_index(offset):
    return (offset[0] + 1) * 9 + (offset[1] + 1) * 3 + offset[2] + 1


def span_of(step, edge_len):
    if step == -1:
        return slice(edge_len - 1, edge_len)
    if step == 1:
        return slice(0, 1)
    return slice(0, edge_len)


def assemble(piece_at):
    planes = []
    for step_x in (-1, 0, 1):
        lines = []
        for step_y in (-1, 0, 1):
            cells = [piece_at((step_x, step_y, step_z)) for step_z in (-1, 0, 1)]
            lines.append(jnp.concatenate(cells, axis=3))
        planes.append(jnp.concatenate(lines, axis=2))
    return jnp.concatenate(planes, axis=1)


def window(padded, offset, sign):
    edge_len = padded.shape[1] - 2
    starts = [1 + sign * offset[axis_id] for axis_id in range(3)]
    return padded[
        :,
        starts[0] : starts[0] + edge_len,
        starts[1] : starts[1] + edge_len,
        starts[2] : starts[2] + edge_len,
    ]


def conv_rows(padded, weight, sign):
    channels = padded.shape[-1]
    running = None
    for offset in OFFSETS:
        shifted = window(padded, offset, sign).reshape(-1, channels)
        matrix = weight[offset_index(offset)]
        if sign < 0:
            matrix = matrix.T
        term = jnp.dot(shifted, matrix, preferred_element_type=jnp.float32)
        running = term if running is None else running + term
    return running


def contract(left, right):
    return lax.dot_general(
        left, right, (((0,), (0,)), ((), ())), preferred_element_type=jnp.float32
    )


def children(hidden):
    block_count, edge_len, channels = (hidden.shape[0], hidden.shape[1], hidden.shape[-1])
    half_edge = edge_len // 2
    parted = hidden.reshape(block_count, half_edge, 2, half_edge, 2, half_edge, 2, channels)
    return [
        parted[:, :, i, :, j, :, l, :].reshape(-1, channels)
        for i in (0, 1)
        for j in (0, 1)
        for l in (0, 1)
    ]


def down_blocks(hidden, down_weight):
    block_count, channels = (hidden.shape[0], hidden.shape[-1])
    running = None
    for child_id, rows_in in enumerate(children(hidden)):
        term = jnp.dot(rows_in, down_weight[child_id], preferred_element_type=jnp.float32)
        running = term if running is None else running + term
    return running.reshape(block_count, -1, channels)


def up_blocks(coarse_grad, down_weight, edge_len):
    block_count, channels = (coarse_grad.shape[0], coarse_grad.shape[-1])
    half_edge = edge_len // 2
    flat_grad = coarse_grad.reshape(-1, channels)
    parts_list = [
        jnp.dot(flat_grad, down_weight[child_id].T, preferred_element_type=jnp.float32)
        for child_id in range(8)
    ]
    stacked = jnp.stack(parts_list).reshape(
        2, 2, 2, block_count, half_edge, half_edge, half_edge, channels
    )
    return stacked.transpose(3, 4, 0, 5, 1, 6, 2, 7).reshape(
        block_count, edge_len, edge_len, edge_len, channels
    )


def face_stack(blocks):
    return jnp.stack(
        [
            blocks[:, 0],
            blocks[:, -1],
            blocks[:, :, 0],
            blocks[:, :, -1],
            blocks[:, :, :, 0],
            blocks[:, :, :, -1],
        ],
        axis=1,
    )


def listed_faces(blocks, send_list):
    block_count = blocks.shape[0]
    all_faces = face_stack(blocks)
    zero_face = jnp.zeros((1,) + all_faces.shape[1:], all_faces.dtype)
    extended = jnp.concatenate([all_faces, zero_face], axis=0)
    picked = jnp.take(extended, jnp.where(send_list < 0, block_count, send_list), axis=0)
    return (all_faces, zero_face, picked)


def build_padded(blocks, face_pool, neighbours):
    edge_len = blocks.shape[1]

    def piece_at(offset):
        if offset == (0, 0, 0):
            return blocks
        axis_lead = [axis_id for axis_id in range(3) if offset[axis_id] != 0][0]
        face_id = 2 * axis_lead + (0 if offset[axis_lead] == 1 else 1)
        face_rows = jnp.take(face_pool, neighbours[:, offset_index(offset)] * 6 + face_id, axis=0)
        others = [axis_id for axis_id in range(3) if axis_id != axis_lead]
        face_rows = face_rows[
            :, span_of(offset[others[0]], edge_len), span_of(offset[others[1]], edge_len)
        ]
        return jnp.expand_dims(face_rows, 1 + axis_lead)

    return assemble(piece_at)


def padded_for(blocks, send_list, neighbours):
    slot_cap = send_list.shape[1]
    all_faces, zero_face, picked = listed_faces(blocks, send_list)
    outgoing = picked.reshape((3, 3) + picked.shape[1:])
    padded = with_halo(outgoing, (("bx", 0), ("by", 1)), 1)
    received = padded[::2, ::2]
    face_pool = jnp.concatenate(
        [all_faces, received.reshape((9 * slot_cap,) + all_faces.shape[1:]), zero_face], axis=0
    )
    return build_padded(blocks, face_pool.reshape((-1,) + all_faces.shape[2:]), neighbours)


def prior_count(owners, columns):
    onehot = (owners[:, None] == jnp.arange(columns, dtype=jnp.int32)[None, :]).astype(jnp.int32)
    before = jnp.cumsum(onehot, axis=0) - onehot
    return jnp.sum(before * onehot, axis=1)


def general_path(
    features,
    weight,
    down_weight,
    grad_out,
    grad_coarse,
    neighbours,
    send_list,
    coarse_dest,
    coarse_from,
):
    block_count, edge_len, channels = (features.shape[0], features.shape[1], features.shape[-1])
    device_total = lax.axis_size("bx") * lax.axis_size("by")
    padded_in = padded_for(features, send_list, neighbours)
    preact = conv_rows(padded_in, weight, 1).reshape(features.shape)
    hidden = jax.nn.silu(preact).astype(jnp.bfloat16)
    reduced = down_blocks(hidden, down_weight).astype(jnp.bfloat16)
    columns = lax.axis_size("by")
    per_peer = -(-block_count // columns)
    send_rank = prior_count(coarse_dest, columns)
    recv_rank = prior_count(coarse_from, columns)
    outgoing = jnp.zeros((columns * per_peer,) + reduced.shape[1:], jnp.bfloat16)
    outgoing = outgoing.at[coarse_dest * per_peer + send_rank].set(reduced)
    arrived = lax.all_to_all(outgoing, "by", split_axis=0, concat_axis=0, tiled=True)
    coarse = arrived[coarse_from * per_peer + recv_rank]
    returning = jnp.zeros((columns * per_peer,) + grad_coarse.shape[1:], jnp.bfloat16)
    returning = returning.at[coarse_from * per_peer + recv_rank].set(grad_coarse)
    came_back = lax.all_to_all(returning, "by", split_axis=0, concat_axis=0, tiled=True)
    coarse_grad_here = came_back[coarse_dest * per_peer + send_rank]
    flat_grad = coarse_grad_here.reshape(-1, channels)
    down_terms = jnp.stack([contract(rows_in, flat_grad) for rows_in in children(hidden)])
    sigmoid_pre = jax.nn.sigmoid(preact)
    grad_pre = (
        (grad_out.astype(jnp.float32) + up_blocks(coarse_grad_here, down_weight, edge_len))
        * sigmoid_pre
        * (1.0 + preact * (1.0 - sigmoid_pre))
    ).astype(jnp.bfloat16)
    padded_grad = padded_for(grad_pre, send_list, neighbours)
    grad_features = conv_rows(padded_grad, weight, -1).reshape(features.shape).astype(jnp.bfloat16)
    own_rows = grad_pre.reshape(-1, channels)
    weight_terms = jnp.stack(
        [
            contract(window(padded_in, offset, 1).reshape(-1, channels), own_rows)
            for offset in OFFSETS
        ]
    )
    weight_total, down_total = lax.psum((weight_terms, down_terms), ("bx", "by"))
    return (hidden, coarse, grad_features, weight_total / device_total, down_total / device_total)


F32, BF16 = jnp.float32, jnp.bfloat16
MESH = pl.DeviceIdType.MESH
NONE = 20
LISTS = 9
ROUTES = (("x", "y", "z"), ("y", "z", "x"), ("z", "x", "y"))
PART_ROWS = 1536
HALF_ROWS = 768


def fits_grid(p, o1, o2):
    half = p // 2
    good = (half == 0) | (half == NONE // 2)
    for dr in {0, o1}:
        for dc in {0, o2}:
            if (dr, dc) != (0, 0):
                good = good | (half == (dr + 1) * 3 + dc + 2)
    return good


def section_kernel(
    sizes,
    nb, sl, cdest, cfrom,
    feat, weight, down, gout, gcoarse,
    hid_out, coarse_out, gfeat_out, gw_out, gd_out, flag_out,
    pad, col, colg, xpool, ypool, cpool,
    xs, ys, cs, xr, yr, cr,
    gsend, gpool, rsend, rpool,
    wback, wdcat, slope, hpart, wide, cgx, up, gbf,
    arf, s0, r0, hf, s1, r1, t1f, s2, r2, r3, fin,
    halo_send, halo_recv, g_send, g_recv, c_send, c_recv, ar_send, ar_recv, core_send, core_recv,
):
    nx, ny, nz = sizes
    nby, nbx = nx * nz, 2 * ny
    r, c = lax.axis_index("bx"), lax.axis_index("by")
    core, at = lax.rem(r, 2), {"x": lax.rem(c, nx), "y": r // 2, "z": c // nx}
    size = {"x": nx, "y": ny, "z": nz}

    def moved(axis, step):
        to = dict(at)
        to[axis] = lax.rem(at[axis] + step, size[axis])
        return (to["y"] * 2 + core, to["z"] * nx + to["x"])

    other_core = (r + 1 - 2 * core, c)

    def beside(dr, dc):
        return (lax.rem(r + dr + nbx, nbx), lax.rem(c + dc + nby, nby))

    around = [(dr, dc) for dr in (-1, 0, 1) for dc in (-1, 0, 1) if (dr, dc) != (0, 0)]

    barrier = pltpu.get_barrier_semaphore()

    def greet(step, carry):
        pl.semaphore_signal(barrier, inc=1, device_id=(r, lax.rem(c + step, nby)), device_id_type=MESH)
        return carry

    lax.fori_loop(1, nby, greet, 0)
    met = nby - 1
    for dr, dc in around:
        if dr != 0:
            pl.semaphore_signal(barrier, inc=1, device_id=beside(dr, dc), device_id_type=MESH)
            met += 1
    for step in range(1, ny):
        pl.semaphore_signal(barrier, inc=1, device_id=moved("y", step), device_id_type=MESH)
        met += 1

    def fill_interior(i, carry):
        b, x = i // 8, lax.rem(i, 8)
        pad[b, x + 1, 1:9, 1:9, :] = feat[b, x].astype(F32).reshape(8, 8, 128)
        return carry

    lax.fori_loop(0, 16, fill_interior, 0)
    pad[2, 1:9, 1:9] = jnp.zeros((8, 8, 16, 128), F32)
    for side in (0, 1):
        xpool[side, NONE] = jnp.zeros((8, 8, 128), F32)
        ypool[side, NONE] = jnp.zeros((8, 8, 128), F32)
    for corner in range(4):
        cpool[corner, NONE] = jnp.zeros((8, 128), F32)

    near = (8, 1)
    edge = (1, 8)

    def stage_faces(t):
        for side in (0, 1):
            step = 2 * side - 1
            for j in (0, 1):
                bx_block = jnp.maximum(sl[(step + 1) * 3 + 1, j], 0)
                face = pad[bx_block, edge[side], 1:9, 1:9, :]
                xs[t, side, 64 * j : 64 * j + 64] = face.reshape(64, 128).astype(BF16)
                by_block = jnp.maximum(sl[3 + step + 1, j], 0)
                face = pad[by_block, 1:9, edge[side], 1:9, :]
                ys[t, side, 64 * j : 64 * j + 64] = face.reshape(64, 128).astype(BF16)
        for sx in (0, 1):
            for sy in (0, 1):
                row = 2 * sx * 3 + 2 * sy
                lines = [pad[jnp.maximum(sl[row, j], 0), edge[sx], edge[sy], 1:9, :] for j in (0, 1)]
                cs[t, 2 * sx + sy] = jnp.concatenate(lines, axis=0).astype(BF16)

    def halo_copies(t):
        out = []
        for side in (0, 1):
            out.append((xs.at[t, side], xr.at[t, 1 - side], beside(2 * side - 1, 0)))
        for side in (0, 1):
            out.append((ys.at[t, side], yr.at[t, 1 - side], beside(0, 2 * side - 1)))
        for sx in (0, 1):
            for sy in (0, 1):
                out.append((cs.at[t, 2 * sx + sy], cr.at[t, 3 - 2 * sx - sy], beside(2 * sx - 1, 2 * sy - 1)))
        return [
            pltpu.make_async_remote_copy(
                src_ref=src, dst_ref=dst, send_sem=halo_send.at[t, n], recv_sem=halo_recv.at[t, n],
                device_id=to, device_id_type=MESH,
            )
            for n, (src, dst, to) in enumerate(out)
        ]

    def local_pools():
        for side in (0, 1):
            for b in (0, 1):
                xpool[side, b] = pad[b, near[side], 1:9, 1:9, :]
                ypool[side, b] = pad[b, 1:9, near[side], 1:9, :]
        for sx in (0, 1):
            for sy in (0, 1):
                for b in (0, 1):
                    cpool[2 * sx + sy, b] = pad[b, near[sx], near[sy], 1:9, :]

    def remote_pools(t):
        for side in (0, 1):
            for j in (0, 1):
                ex, ey = 2 * side * 3 + 1, 3 + 2 * side
                xpool[side, 2 + 2 * ex + j] = xr[t, side, 64 * j : 64 * j + 64].astype(F32).reshape(8, 8, 128)
                ypool[side, 2 + 2 * ey + j] = yr[t, side, 64 * j : 64 * j + 64].astype(F32).reshape(8, 8, 128)
        for sx in (0, 1):
            for sy in (0, 1):
                lines = cr[t, 2 * sx + sy].astype(F32).reshape(2, 8, 128)
                for j in (0, 1):
                    ex, ey, ec = 2 * sx * 3 + 1, 3 + 2 * sy, 2 * sx * 3 + 2 * sy
                    cpool[2 * sx + sy, 2 + 2 * ex + j] = xpool[sx, 2 + 2 * ex + j, near[sy] - 1]
                    cpool[2 * sx + sy, 2 + 2 * ey + j] = ypool[sy, 2 + 2 * ey + j, near[sx] - 1]
                    cpool[2 * sx + sy, 2 + 2 * ec + j] = lines[j]

    def rims():
        def one(b, carry):
            for o1 in (-1, 0, 1):
                for o2 in (-1, 0, 1):
                    for o3 in (-1, 0, 1):
                        if (o1, o2, o3) == (0, 0, 0):
                            continue
                        p = nb[b, offset_index((o1, o2, o3))]
                        x, y, z = [(0, None, 9)[o + 1] for o in (o1, o2, o3)]
                        zs = (8, None, 1)[o3 + 1]
                        if o1 == 0 and o2 == 0:
                            pad[b, 1:9, 1:9, z : z + 1, :] = pad[jnp.minimum(p, 2), 1:9, 1:9, zs : zs + 1, :]
                        elif o2 == 0:
                            s = (o1 + 1) // 2
                            if o3 == 0:
                                pad[b, x, 1:9, 1:9, :] = xpool[s, p]
                            else:
                                pad[b, x, 1:9, z : z + 1, :] = xpool[s, p, :, zs - 1 : zs, :]
                        elif o1 == 0:
                            s = (o2 + 1) // 2
                            if o3 == 0:
                                pad[b, 1:9, y, 1:9, :] = ypool[s, p]
                            else:
                                pad[b, 1:9, y, z : z + 1, :] = ypool[s, p, :, zs - 1 : zs, :]
                        else:
                            s = (o1 + 1) + (o2 + 1) // 2
                            if o3 == 0:
                                pad[b, x, y, 1:9, :] = cpool[s, p]
                            else:
                                pad[b, x, y, z : z + 1, :] = cpool[s, p, zs - 1 : zs, :]
            return carry

        lax.fori_loop(0, 2, one, 0)

    def columns(dst):
        def one(i, carry):
            b, x = i // 10, lax.rem(i, 10)
            for m in range(9):
                o2, o3 = m // 3, m % 3
                cells = pad[b, x, o2 : o2 + 8, o3 : o3 + 8, :]
                dst[i, :, 128 * m : 128 * m + 128] = cells.reshape(64, 128).astype(BF16)
            return carry

        lax.fori_loop(0, 20, one, 0)

    stage_faces(0)

    def stage_gcoarse(step, carry):
        to = lax.rem(c + step, nby)
        gsend[step] = gcoarse[jnp.where(cfrom[1] == to, 1, 0)]
        return carry

    lax.fori_loop(0, nby, stage_gcoarse, 0)
    gpool[0] = gsend[0]

    pl.semaphore_wait(barrier, met)
    first = halo_copies(0)
    for copy in first:
        copy.start()

    def row_copy(src, dst, send, recv, step):
        return pltpu.make_async_remote_copy(
            src_ref=src.at[step], dst_ref=dst.at[step], send_sem=send.at[step], recv_sem=recv.at[step],
            device_id=(r, lax.rem(c + step, nby)), device_id_type=MESH,
        )

    def start_row(src, dst, send, recv):
        def one(step, carry):
            row_copy(src, dst, send, recv, step).start()
            return carry

        lax.fori_loop(1, nby, one, 0)

    def wait_row_recv(src, dst, send, recv):
        def one(step, carry):
            row_copy(src, dst, send, recv, step).wait_recv()
            return carry

        lax.fori_loop(1, nby, one, 0)

    def wait_row_send(src, dst, send, recv):
        def one(step, carry):
            row_copy(src, dst, send, recv, step).wait_send()
            return carry

        lax.fori_loop(1, nby, one, 0)

    start_row(gsend, gpool, g_send, g_recv)

    for k in range(27):
        wback[k // 9, :, 128 * (k % 9) : 128 * (k % 9) + 128] = weight[26 - k]
    for q in range(8):
        wdcat[q // 2, :, 128 * (q % 2) : 128 * (q % 2) + 128] = down[q]
    local_pools()
    for copy in first:
        copy.wait_recv()
    remote_pools(0)
    rims()
    columns(col)

    def forward(b, carry):
        total = None
        for o1 in range(3):
            rows = col[pl.ds(b * 10 + o1, 8)].reshape(512, 1152)
            term = jnp.dot(rows, weight[9 * o1 : 9 * o1 + 9].reshape(1152, 128), preferred_element_type=F32)
            total = term if total is None else total + term
        slope[b] = total.reshape(8, 64, 128)
        return carry

    lax.fori_loop(0, 2, forward, 0)

    def activate(i, carry):
        b, a1 = i // 4, lax.rem(i, 4)
        for p1 in (0, 1):
            x = 2 * a1 + p1
            pre = slope[b, x]
            g = jax.nn.sigmoid(pre)
            act = (pre * g).astype(BF16)
            hid_out[b, x] = act
            lines = act.astype(F32).reshape(4, 2, 8, 128)
            for p2 in (0, 1):
                at_row = pl.multiple_of(b * 128 + a1 * 32, 32)
                hpart[2 * p1 + p2, pl.ds(at_row, 32), :] = lines[:, p2].reshape(32, 128).astype(BF16)
            slope[b, x] = g * (1.0 + pre * (1.0 - g))
        return carry

    lax.fori_loop(0, 8, activate, 0)

    total = None
    for q in range(4):
        term = jnp.dot(hpart[q], wdcat[q], preferred_element_type=F32)
        total = term if total is None else total + term
    wide[0] = total[:, :128]
    wide[1] = total[:, 128:]
    reduced = wide[0, pl.ds(0, 128, stride=2), :] + wide[1, pl.ds(1, 128, stride=2), :]
    reduced = reduced.astype(BF16).reshape(2, 64, 128)

    for step in range(nby):
        to = lax.rem(c + step, nby)
        second = jnp.full((64, 128), cdest[1], jnp.int32) == to
        block = jnp.where(second, reduced[1].astype(F32), reduced[0].astype(F32)).astype(BF16)
        if step == 0:
            rpool[0] = block
        else:
            rsend[step] = block
    start_row(rsend, rpool, c_send, c_recv)

    wait_row_recv(gsend, gpool, g_send, g_recv)
    wide[...] = jnp.zeros((2, 256, 128), F32)
    for b in (0, 1):
        block = gpool[lax.rem(c - cdest[b] + nby, nby)].astype(F32)
        wide[0, pl.ds(128 * b, 64, stride=2), :] = block
        wide[1, pl.ds(128 * b + 1, 64, stride=2), :] = block
    cgx[:, :128] = wide[0].astype(BF16)
    cgx[:, 128:] = wide[1].astype(BF16)
    for q in range(4):
        up[q] = lax.dot_general(cgx[...], wdcat[q], (((1,), (1,)), ((), ())), preferred_element_type=F32)

    def pre_grad(i, carry):
        b, a1 = i // 4, lax.rem(i, 4)
        for p1 in (0, 1):
            x = 2 * a1 + p1
            at_row = pl.multiple_of(b * 128 + a1 * 32, 32)
            parts = [up[2 * p1 + p2, pl.ds(at_row, 32), :].reshape(4, 8, 128) for p2 in (0, 1)]
            back = jnp.stack(parts, axis=1).reshape(64, 128)
            grad = ((gout[b, x].astype(F32) + back) * slope[b, x]).astype(BF16)
            gbf[b, x] = grad
            pad[b, x + 1, 1:9, 1:9, :] = grad.astype(F32).reshape(8, 8, 128)
        return carry

    lax.fori_loop(0, 8, pre_grad, 0)
    stage_faces(1)
    second_halo = halo_copies(1)
    for copy in second_halo:
        copy.start()

    def contracted(left, right):
        return lax.dot_general(left, right, (((0,), (0,)), ((), ())), preferred_element_type=F32)

    for q in range(4):
        both = contracted(hpart[q], cgx[...])
        for l in (0, 1):
            n = 2 * q + l
            arf[n // 3, 1152 + 128 * (n % 3) : 1280 + 128 * (n % 3)] = both[:, 128 * l : 128 * l + 128]
    misfits = jnp.int32(0)
    for b in (0, 1):
        for offset in OFFSETS:
            good = fits_grid(nb[b, offset_index(offset)], offset[0], offset[1])
            misfits = misfits + jnp.where(good, 0, 1)
    arf[2, 1408:1536] = jnp.full((128, 128), misfits, jnp.int32).astype(F32)

    my_half = pl.multiple_of(core * HALF_ROWS, HALF_ROWS)
    your_half = pl.multiple_of((1 - core) * HALF_ROWS, HALF_ROWS)

    def core_copy(part):
        return pltpu.make_async_remote_copy(
            src_ref=s0.at[part], dst_ref=r0.at[part], send_sem=core_send.at[0, part], recv_sem=core_recv.at[0, part],
            device_id=other_core, device_id_type=MESH,
        )

    def core_back(part):
        return pltpu.make_async_remote_copy(
            src_ref=fin.at[core, part], dst_ref=fin.at[core, part], send_sem=core_send.at[1, part],
            recv_sem=core_recv.at[1, part], device_id=other_core, device_id_type=MESH,
        )

    def hop(phase, part, src, dst, axis, step):
        return pltpu.make_async_remote_copy(
            src_ref=src, dst_ref=dst, send_sem=ar_send.at[phase, part, step], recv_sem=ar_recv.at[phase, part, step],
            device_id=moved(axis, step), device_id_type=MESH,
        )

    def hops(phase, part):
        a1, a2, a3 = ROUTES[part]
        out = []
        for step in range(1, size[(a1, a2, a3, a2, a1)[phase]]):
            if phase == 0:
                to = lax.rem(at[a1] + step, size[a1])
                out.append(hop(0, part, s1.at[part, to], r1.at[part, step], a1, step))
            elif phase == 1:
                to = lax.rem(at[a2] + step, size[a2])
                out.append(hop(1, part, s2.at[part, to], r2.at[part, step], a2, step))
            elif phase == 2:
                out.append(hop(2, part, r3.at[part, 0], r3.at[part, step], a3, step))
            elif phase == 3:
                place = fin.at[core, part, at[a1], at[a2]]
                out.append(hop(3, part, place, place, a2, step))
            else:
                place = fin.at[core, part, at[a1]]
                out.append(hop(4, part, place, place, a1, step))
        return out

    def run_hops(phase, part):
        for copy in hops(phase, part):
            copy.start()

    def land_hops(phase, part):
        for copy in hops(phase, part):
            copy.wait_recv()

    n1, n2 = nx, nx
    rows1, rows2 = HALF_ROWS // n1, HALF_ROWS // (n1 * n2)

    for part in range(3):
        def weight_grad(m, carry, part=part):
            lanes = pl.ds(pl.multiple_of(m * 128, 128), 128)
            total = None
            for b in (0, 1):
                rows = col[10 * b + part : 10 * b + part + 8, :, lanes].reshape(512, 128)
                term = contracted(rows, gbf[b].reshape(512, 128))
                total = term if total is None else total + term
            arf[part, pl.ds(pl.multiple_of(m * 128, 128), 128), :] = total
            return carry

        lax.fori_loop(0, 9, weight_grad, 0)
        s0[part] = arf[part, pl.ds(your_half, HALF_ROWS), :].astype(BF16)
        core_copy(part).start()

    for part in range(3):
        core_copy(part).wait_recv()
        hf[part] = arf[part, pl.ds(my_half, HALF_ROWS), :] + r0[part].astype(F32)
        s1[part] = hf[part].astype(BF16).reshape(n1, rows1, 128)
        run_hops(0, part)

    local_pools()
    for copy in second_halo:
        copy.wait_recv()
    remote_pools(1)
    rims()

    for part in range(3):
        land_hops(0, part)
        mine = hf[part, pl.ds(pl.multiple_of(at[ROUTES[part][0]] * rows1, rows1), rows1), :]
        for step in range(1, n1):
            mine = mine + r1[part, step].astype(F32)
        t1f[part] = mine.reshape(n2, rows2, 128)
        s2[part] = mine.astype(BF16).reshape(n2, rows2, 128)
        run_hops(1, part)

    columns(colg)

    for part in range(3):
        land_hops(1, part)
        mine = t1f[part, at[ROUTES[part][1]]]
        for step in range(1, n2):
            mine = mine + r2[part, step].astype(F32)
        r3[part, 0] = mine.astype(BF16)
        run_hops(2, part)

    def backward(b, carry):
        total = None
        for o1 in range(3):
            rows = colg[pl.ds(b * 10 + o1, 8)].reshape(512, 1152)
            term = lax.dot_general(rows, wback[o1], (((1,), (1,)), ((), ())), preferred_element_type=F32)
            total = term if total is None else total + term
        gfeat_out[b] = total.astype(BF16).reshape(8, 64, 128)
        return carry

    backward(0, 0)

    for part in range(3):
        a1, a2, a3 = ROUTES[part]
        land_hops(2, part)
        whole = None
        for place in range(size[a3]):
            term = r3[part, lax.rem(at[a3] - place + size[a3], size[a3])].astype(F32)
            whole = term if whole is None else whole + term
        fin[core, part, at[a1], at[a2]] = (whole * (1.0 / (nbx * nby))).astype(BF16)
        run_hops(3, part)

    backward(1, 0)

    for part in range(3):
        land_hops(3, part)
        run_hops(4, part)

    wait_row_recv(rsend, rpool, c_send, c_recv)
    for m in (0, 1):
        coarse_out[m] = rpool[lax.rem(c - cfrom[m] + nby, nby)]

    for part in range(3):
        land_hops(4, part)
        core_back(part).start()
    for part in range(3):
        core_back(part).wait_recv()
        low = fin[0, part].reshape(HALF_ROWS, 128).astype(F32).reshape(6, 128, 128)
        high = fin[1, part].reshape(HALF_ROWS, 128).astype(F32).reshape(6, 128, 128)
        gw_out[9 * part : 9 * part + 6] = low
        gw_out[9 * part + 6 : 9 * part + 9] = high[:3]
        if part < 2:
            gd_out[3 * part : 3 * part + 3] = high[3:]
        else:
            gd_out[6:8] = high[3:5]
            flag_out[...] = high[5, :8]

    for copy in first + second_halo:
        copy.wait_send()
    wait_row_send(gsend, gpool, g_send, g_recv)
    wait_row_send(rsend, rpool, c_send, c_recv)
    for part in range(3):
        core_copy(part).wait_send()
        core_back(part).wait_send()
        for phase in range(5):
            for copy in hops(phase, part):
                copy.wait_send()


def grid_path(
    sizes, features, weight, down_weight, grad_out, grad_coarse, neighbours, send_list, coarse_dest, coarse_from
):
    nx, ny, nz = sizes
    nby = nx * nz
    rows1, rows2 = HALF_ROWS // nx, HALF_ROWS // (nx * nx)
    vmem, smem = pl.BlockSpec(memory_space=pltpu.VMEM), pl.BlockSpec(memory_space=pltpu.SMEM)
    hidden, coarse, grad_features, grad_weight, grad_down, flag = pl.pallas_call(
        functools.partial(section_kernel, sizes),
        out_shape=[
            jax.ShapeDtypeStruct((2, 8, 64, 128), BF16),
            jax.ShapeDtypeStruct((2, 64, 128), BF16),
            jax.ShapeDtypeStruct((2, 8, 64, 128), BF16),
            jax.ShapeDtypeStruct((27, 128, 128), F32),
            jax.ShapeDtypeStruct((8, 128, 128), F32),
            jax.ShapeDtypeStruct((8, 128), F32),
        ],
        in_specs=[smem] * 4 + [vmem] * 5,
        out_specs=[vmem] * 6,
        scratch_shapes=[
            pltpu.VMEM((3, 10, 10, 16, 128), F32),
            pltpu.VMEM((20, 64, 1152), BF16),
            pltpu.VMEM((20, 64, 1152), BF16),
            pltpu.VMEM((2, 21, 8, 8, 128), F32),
            pltpu.VMEM((2, 21, 8, 8, 128), F32),
            pltpu.VMEM((4, 21, 8, 128), F32),
            pltpu.VMEM((2, 2, 128, 128), BF16),
            pltpu.VMEM((2, 2, 128, 128), BF16),
            pltpu.VMEM((2, 4, 16, 128), BF16),
            pltpu.VMEM((2, 2, 128, 128), BF16),
            pltpu.VMEM((2, 2, 128, 128), BF16),
            pltpu.VMEM((2, 4, 16, 128), BF16),
            pltpu.VMEM((nby, 64, 128), BF16),
            pltpu.VMEM((nby, 64, 128), BF16),
            pltpu.VMEM((nby, 64, 128), BF16),
            pltpu.VMEM((nby, 64, 128), BF16),
            pltpu.VMEM((3, 128, 1152), BF16),
            pltpu.VMEM((4, 128, 256), BF16),
            pltpu.VMEM((2, 8, 64, 128), F32),
            pltpu.VMEM((4, 256, 128), BF16),
            pltpu.VMEM((2, 256, 128), F32),
            pltpu.VMEM((256, 256), BF16),
            pltpu.VMEM((4, 256, 128), F32),
            pltpu.VMEM((2, 8, 64, 128), BF16),
            pltpu.VMEM((3, PART_ROWS, 128), F32),
            pltpu.VMEM((3, HALF_ROWS, 128), BF16),
            pltpu.VMEM((3, HALF_ROWS, 128), BF16),
            pltpu.VMEM((3, HALF_ROWS, 128), F32),
            pltpu.VMEM((3, nx, rows1, 128), BF16),
            pltpu.VMEM((3, nx, rows1, 128), BF16),
            pltpu.VMEM((3, nx, rows2, 128), F32),
            pltpu.VMEM((3, nx, rows2, 128), BF16),
            pltpu.VMEM((3, nx, rows2, 128), BF16),
            pltpu.VMEM((3, nx, rows2, 128), BF16),
            pltpu.VMEM((2, 3, nx, nx, rows2, 128), BF16),
            pltpu.SemaphoreType.DMA((2, 8)),
            pltpu.SemaphoreType.DMA((2, 8)),
            pltpu.SemaphoreType.DMA((nby,)),
            pltpu.SemaphoreType.DMA((nby,)),
            pltpu.SemaphoreType.DMA((nby,)),
            pltpu.SemaphoreType.DMA((nby,)),
            pltpu.SemaphoreType.DMA((5, 3, nx)),
            pltpu.SemaphoreType.DMA((5, 3, nx)),
            pltpu.SemaphoreType.DMA((2, 3)),
            pltpu.SemaphoreType.DMA((2, 3)),
        ],
        compiler_params=pltpu.CompilerParams(
            collective_id=0, has_side_effects=True, vmem_limit_bytes=48 * 2**20
        ),
        cost_estimate=pl.CostEstimate(flops=3 * 10**9, bytes_accessed=6 * 10**6, transcendentals=2**17),
    )(
        neighbours, send_list, coarse_dest, coarse_from,
        features.reshape(2, 8, 64, 128), weight, down_weight, grad_out.reshape(2, 8, 64, 128), grad_coarse,
    )
    return (
        (hidden.reshape(features.shape), coarse, grad_features.reshape(features.shape), grad_weight, grad_down),
        flag[0, 0],
    )


def per_device(sizes, *operands):
    results, misfits = grid_path(sizes, *operands)
    return lax.cond(misfits > 0, lambda: general_path(*operands), lambda: results)


def solution(mesh):
    nby = mesh.shape["by"]
    nx = {16: 4, 4: 2}[nby]
    sizes = (nx, mesh.shape["bx"] // 2, nby // nx)
    in_specs = (
        P(("bx", "by"), None, None, None, None),
        P(),
        P(),
        P(("bx", "by"), None, None, None, None),
        P(("bx", "by"), None, None),
        P(("bx", "by"), None),
        P(("bx", "by"), None),
        P(("bx", "by")),
        P(("bx", "by")),
    )
    out_specs = (
        P(("bx", "by"), None, None, None, None),
        P(("bx", "by"), None, None),
        P(("bx", "by"), None, None, None, None),
        P(),
        P(),
    )
    return jax.shard_map(
        functools.partial(per_device, sizes), mesh=mesh, in_specs=in_specs, out_specs=out_specs, check_vma=False
    )
```

```python
import functools

import jax
import jax.numpy as jnp
from jax import lax
from jax.experimental import pallas as pl
from jax.experimental.pallas import tpu as pltpu
from jax.sharding import PartitionSpec as P

OFFSETS = [(p, q, w) for p in (-1, 0, 1) for q in (-1, 0, 1) for w in (-1, 0, 1)]


def with_halo(cells, sides, width):
    for axis, dim in sides:
        count = lax.axis_size(axis)
        ends = count - 1
        head = lax.slice_in_dim(cells, 0, width, axis=dim)
        tail = lax.slice_in_dim(cells, cells.shape[dim] - width, cells.shape[dim], axis=dim)
        cells = jnp.concatenate(
            [
                lax.ppermute(tail, axis, [(i, (i + 1) % count) for i in range(ends)]),
                cells,
                lax.ppermute(head, axis, [((i + 1) % count, i) for i in range(ends)]),
            ],
            axis=dim,
        )
    return cells


def offset_index(offset):
    return (offset[0] + 1) * 9 + (offset[1] + 1) * 3 + offset[2] + 1


def span_of(step, edge_len):
    if step == -1:
        return slice(edge_len - 1, edge_len)
    if step == 1:
        return slice(0, 1)
    return slice(0, edge_len)


def assemble(piece_at):
    planes = []
    for step_x in (-1, 0, 1):
        lines = []
        for step_y in (-1, 0, 1):
            cells = [piece_at((step_x, step_y, step_z)) for step_z in (-1, 0, 1)]
            lines.append(jnp.concatenate(cells, axis=3))
        planes.append(jnp.concatenate(lines, axis=2))
    return jnp.concatenate(planes, axis=1)


def window(padded, offset, sign):
    edge_len = padded.shape[1] - 2
    starts = [1 + sign * offset[axis_id] for axis_id in range(3)]
    return padded[
        :,
        starts[0] : starts[0] + edge_len,
        starts[1] : starts[1] + edge_len,
        starts[2] : starts[2] + edge_len,
    ]


def conv_rows(padded, weight, sign):
    channels = padded.shape[-1]
    running = None
    for offset in OFFSETS:
        shifted = window(padded, offset, sign).reshape(-1, channels)
        matrix = weight[offset_index(offset)]
        if sign < 0:
            matrix = matrix.T
        term = jnp.dot(shifted, matrix, preferred_element_type=jnp.float32)
        running = term if running is None else running + term
    return running


def contract(left, right):
    return lax.dot_general(
        left, right, (((0,), (0,)), ((), ())), preferred_element_type=jnp.float32
    )


def children(hidden):
    block_count, edge_len, channels = (hidden.shape[0], hidden.shape[1], hidden.shape[-1])
    half_edge = edge_len // 2
    parted = hidden.reshape(block_count, half_edge, 2, half_edge, 2, half_edge, 2, channels)
    return [
        parted[:, :, i, :, j, :, l, :].reshape(-1, channels)
        for i in (0, 1)
        for j in (0, 1)
        for l in (0, 1)
    ]


def down_blocks(hidden, down_weight):
    block_count, channels = (hidden.shape[0], hidden.shape[-1])
    running = None
    for child_id, rows_in in enumerate(children(hidden)):
        term = jnp.dot(rows_in, down_weight[child_id], preferred_element_type=jnp.float32)
        running = term if running is None else running + term
    return running.reshape(block_count, -1, channels)


def up_blocks(coarse_grad, down_weight, edge_len):
    block_count, channels = (coarse_grad.shape[0], coarse_grad.shape[-1])
    half_edge = edge_len // 2
    flat_grad = coarse_grad.reshape(-1, channels)
    parts_list = [
        jnp.dot(flat_grad, down_weight[child_id].T, preferred_element_type=jnp.float32)
        for child_id in range(8)
    ]
    stacked = jnp.stack(parts_list).reshape(
        2, 2, 2, block_count, half_edge, half_edge, half_edge, channels
    )
    return stacked.transpose(3, 4, 0, 5, 1, 6, 2, 7).reshape(
        block_count, edge_len, edge_len, edge_len, channels
    )


def face_stack(blocks):
    return jnp.stack(
        [
            blocks[:, 0],
            blocks[:, -1],
            blocks[:, :, 0],
            blocks[:, :, -1],
            blocks[:, :, :, 0],
            blocks[:, :, :, -1],
        ],
        axis=1,
    )


def listed_faces(blocks, send_list):
    block_count = blocks.shape[0]
    all_faces = face_stack(blocks)
    zero_face = jnp.zeros((1,) + all_faces.shape[1:], all_faces.dtype)
    extended = jnp.concatenate([all_faces, zero_face], axis=0)
    picked = jnp.take(extended, jnp.where(send_list < 0, block_count, send_list), axis=0)
    return (all_faces, zero_face, picked)


def build_padded(blocks, face_pool, neighbours):
    edge_len = blocks.shape[1]

    def piece_at(offset):
        if offset == (0, 0, 0):
            return blocks
        axis_lead = [axis_id for axis_id in range(3) if offset[axis_id] != 0][0]
        face_id = 2 * axis_lead + (0 if offset[axis_lead] == 1 else 1)
        face_rows = jnp.take(face_pool, neighbours[:, offset_index(offset)] * 6 + face_id, axis=0)
        others = [axis_id for axis_id in range(3) if axis_id != axis_lead]
        face_rows = face_rows[
            :, span_of(offset[others[0]], edge_len), span_of(offset[others[1]], edge_len)
        ]
        return jnp.expand_dims(face_rows, 1 + axis_lead)

    return assemble(piece_at)


def padded_for(blocks, send_list, neighbours):
    slot_cap = send_list.shape[1]
    all_faces, zero_face, picked = listed_faces(blocks, send_list)
    outgoing = picked.reshape((3, 3) + picked.shape[1:])
    padded = with_halo(outgoing, (("bx", 0), ("by", 1)), 1)
    received = padded[::2, ::2]
    face_pool = jnp.concatenate(
        [all_faces, received.reshape((9 * slot_cap,) + all_faces.shape[1:]), zero_face], axis=0
    )
    return build_padded(blocks, face_pool.reshape((-1,) + all_faces.shape[2:]), neighbours)


def row_gathered(blocks):
    count = lax.axis_size("by")
    me = lax.axis_index("by")

    def one(step, state):
        held, gathered = state
        held = lax.ppermute(held, "by", [(i, (i + 1) % count) for i in range(count)])
        return held, gathered.at[lax.rem(me - step + count, count)].set(held)

    gathered = jnp.zeros((count,) + blocks.shape, blocks.dtype).at[me].set(blocks)
    return lax.fori_loop(1, count, one, (blocks, gathered))[1]


def summed(terms):
    for axis in ("bx", "by"):
        count, distance = lax.axis_size(axis), 1
        while distance < count:
            pairs = [(i, i ^ distance) for i in range(count)]
            terms = [term + lax.ppermute(term, axis, pairs) for term in terms]
            distance *= 2
    return terms


def general_path(
    features,
    weight,
    down_weight,
    grad_out,
    grad_coarse,
    neighbours,
    send_list,
    coarse_dest,
    coarse_from,
):
    send_list = send_list.T
    block_count, edge_len, channels = (features.shape[0], features.shape[1], features.shape[-1])
    device_total = lax.axis_size("bx") * lax.axis_size("by")
    padded_in = padded_for(features, send_list, neighbours)
    preact = conv_rows(padded_in, weight, 1).reshape(features.shape)
    hidden = jax.nn.silu(preact).astype(jnp.bfloat16)
    reduced = down_blocks(hidden, down_weight).astype(jnp.bfloat16)
    slots = jnp.arange(block_count)
    coarse = row_gathered(reduced)[coarse_from, slots]
    coarse_grad_here = row_gathered(grad_coarse)[coarse_dest, slots]
    flat_grad = coarse_grad_here.reshape(-1, channels)
    down_terms = jnp.stack([contract(rows_in, flat_grad) for rows_in in children(hidden)])
    sigmoid_pre = jax.nn.sigmoid(preact)
    grad_pre = (
        (grad_out.astype(jnp.float32) + up_blocks(coarse_grad_here, down_weight, edge_len))
        * sigmoid_pre
        * (1.0 + preact * (1.0 - sigmoid_pre))
    ).astype(jnp.bfloat16)
    padded_grad = padded_for(grad_pre, send_list, neighbours)
    grad_features = conv_rows(padded_grad, weight, -1).reshape(features.shape).astype(jnp.bfloat16)
    own_rows = grad_pre.reshape(-1, channels)
    weight_terms = jnp.stack(
        [
            contract(window(padded_in, offset, 1).reshape(-1, channels), own_rows)
            for offset in OFFSETS
        ]
    )
    weight_total, down_total = summed([weight_terms, down_terms])
    return (hidden, coarse, grad_features, weight_total / device_total, down_total / device_total)


F32, BF16 = jnp.float32, jnp.bfloat16
MESH = pl.DeviceIdType.MESH
NONE = 20
LISTS = 9
ROUTES = (("x", "y", "z"), ("y", "z", "x"), ("z", "x", "y"))
PART_ROWS = 1536
HALF_ROWS = 768


def fits_grid(p, o1, o2):
    half = p // 2
    good = (half == 0) | (half == NONE // 2)
    for dr in {0, o1}:
        for dc in {0, o2}:
            if (dr, dc) != (0, 0):
                good = good | (half == (dr + 1) * 3 + dc + 2)
    return good


def section_kernel(
    sizes,
    nb_in, sl_in, cdest_in, cfrom_in, feat_in, weight_in, down_in, gout_in, gcoarse_in,
    hid_out, coarse_out, gfeat_out, fin,
    nb, sl, cdest, cfrom, feat, weight, down, gout, gcoarse, in_sem,
    pad, col, colg, xpool, ypool, cpool,
    xs, ys, cs, xr, yr, cr,
    gsend, gpool, rsend, rpool,
    wback, wdcat, slope, hpart, wide, cgx, up, gcat,
    arf, s0, r0, hf, s1, r1, t1f, s2, r2, r3,
    halo_send, halo_recv, g_send, g_recv, c_send, c_recv, ar_send, ar_recv, core_send, core_recv,
):
    nx, ny, nz = sizes
    nby, nbx = nx * nz, 2 * ny
    r, c = lax.axis_index("bx"), lax.axis_index("by")
    core, at = lax.rem(r, 2), {"x": lax.rem(c, nx), "y": r // 2, "z": c // nx}
    size = {"x": nx, "y": ny, "z": nz}

    def moved(axis, step):
        to = dict(at)
        to[axis] = lax.rem(at[axis] + step, size[axis])
        return (to["y"] * 2 + core, to["z"] * nx + to["x"])

    other_core = (r + 1 - 2 * core, c)

    def beside(dr, dc):
        return (lax.rem(r + dr + nbx, nbx), lax.rem(c + dc + nby, nby))

    around = [(dr, dc) for dr in (-1, 0, 1) for dc in (-1, 0, 1) if (dr, dc) != (0, 0)]

    staged = {}
    pairs = (
        ("sl", sl_in, sl), ("feat", feat_in, feat), ("cfrom", cfrom_in, cfrom), ("gcoarse", gcoarse_in, gcoarse),
        ("nb", nb_in, nb), ("down", down_in, down), ("weight", weight_in, weight), ("cdest", cdest_in, cdest),
        ("gout", gout_in, gout),
    )
    for n, (name, src, dst) in enumerate(pairs):
        staged[name] = pltpu.make_async_copy(src, dst, in_sem.at[n])
        staged[name].start()

    barrier = pltpu.get_barrier_semaphore()

    def greet(step, carry):
        pl.semaphore_signal(barrier, inc=1, device_id=(r, lax.rem(c + step, nby)), device_id_type=MESH)
        return carry

    lax.fori_loop(1, nby, greet, 0)
    met = nby - 1
    for dr, dc in around:
        if dr != 0:
            pl.semaphore_signal(barrier, inc=1, device_id=beside(dr, dc), device_id_type=MESH)
            met += 1
    for step in range(1, ny):
        pl.semaphore_signal(barrier, inc=1, device_id=moved("y", step), device_id_type=MESH)
        met += 1

    def fill_interior(i, carry):
        b, x = i // 8, lax.rem(i, 8)
        pad[b, x + 1, 1:9, 1:9, :] = feat[b, x].astype(F32).reshape(8, 8, 128)
        return carry

    pad[2, 1:9, 1:9] = jnp.zeros((8, 8, 16, 128), F32)
    for side in (0, 1):
        xpool[side, NONE] = jnp.zeros((8, 8, 128), F32)
        ypool[side, NONE] = jnp.zeros((8, 8, 128), F32)
    for corner in range(4):
        cpool[corner, NONE] = jnp.zeros((8, 128), F32)

    near = (8, 1)
    edge = (1, 8)

    def stage_faces(t):
        for side in (0, 1):
            step = 2 * side - 1
            for j in (0, 1):
                bx_block = jnp.maximum(sl[j, (step + 1) * 3 + 1], 0)
                face = pad[bx_block, edge[side], 1:9, 1:9, :]
                xs[t, side, 64 * j : 64 * j + 64] = face.reshape(64, 128).astype(BF16)
                by_block = jnp.maximum(sl[j, 3 + step + 1], 0)
                face = pad[by_block, 1:9, edge[side], 1:9, :]
                ys[t, side, 64 * j : 64 * j + 64] = face.reshape(64, 128).astype(BF16)
        for sx in (0, 1):
            for sy in (0, 1):
                row = 2 * sx * 3 + 2 * sy
                lines = [pad[jnp.maximum(sl[j, row], 0), edge[sx], edge[sy], 1:9, :] for j in (0, 1)]
                cs[t, 2 * sx + sy] = jnp.concatenate(lines, axis=0).astype(BF16)

    def halo_copies(t):
        out = []
        for side in (0, 1):
            out.append((xs.at[t, side], xr.at[t, 1 - side], beside(2 * side - 1, 0)))
        for side in (0, 1):
            out.append((ys.at[t, side], yr.at[t, 1 - side], beside(0, 2 * side - 1)))
        for sx in (0, 1):
            for sy in (0, 1):
                out.append((cs.at[t, 2 * sx + sy], cr.at[t, 3 - 2 * sx - sy], beside(2 * sx - 1, 2 * sy - 1)))
        return [
            pltpu.make_async_remote_copy(
                src_ref=src, dst_ref=dst, send_sem=halo_send.at[t, n], recv_sem=halo_recv.at[t, n],
                device_id=to, device_id_type=MESH,
            )
            for n, (src, dst, to) in enumerate(out)
        ]

    def local_pools():
        for side in (0, 1):
            for b in (0, 1):
                xpool[side, b] = pad[b, near[side], 1:9, 1:9, :]
                ypool[side, b] = pad[b, 1:9, near[side], 1:9, :]
        for sx in (0, 1):
            for sy in (0, 1):
                for b in (0, 1):
                    cpool[2 * sx + sy, b] = pad[b, near[sx], near[sy], 1:9, :]

    def remote_pools(t):
        for side in (0, 1):
            for j in (0, 1):
                ex, ey = 2 * side * 3 + 1, 3 + 2 * side
                xpool[side, 2 + 2 * ex + j] = xr[t, side, 64 * j : 64 * j + 64].astype(F32).reshape(8, 8, 128)
                ypool[side, 2 + 2 * ey + j] = yr[t, side, 64 * j : 64 * j + 64].astype(F32).reshape(8, 8, 128)
        for sx in (0, 1):
            for sy in (0, 1):
                lines = cr[t, 2 * sx + sy].astype(F32).reshape(2, 8, 128)
                for j in (0, 1):
                    ex, ey, ec = 2 * sx * 3 + 1, 3 + 2 * sy, 2 * sx * 3 + 2 * sy
                    cpool[2 * sx + sy, 2 + 2 * ex + j] = xpool[sx, 2 + 2 * ex + j, near[sy] - 1]
                    cpool[2 * sx + sy, 2 + 2 * ey + j] = ypool[sy, 2 + 2 * ey + j, near[sx] - 1]
                    cpool[2 * sx + sy, 2 + 2 * ec + j] = lines[j]

    def rims():
        def one(b, carry):
            for o1 in (-1, 0, 1):
                for o2 in (-1, 0, 1):
                    for o3 in (-1, 0, 1):
                        if (o1, o2, o3) == (0, 0, 0):
                            continue
                        p = nb[b, offset_index((o1, o2, o3))]
                        x, y, z = [(0, None, 9)[o + 1] for o in (o1, o2, o3)]
                        zs = (8, None, 1)[o3 + 1]
                        if o1 == 0 and o2 == 0:
                            pad[b, 1:9, 1:9, z : z + 1, :] = pad[jnp.minimum(p, 2), 1:9, 1:9, zs : zs + 1, :]
                        elif o2 == 0:
                            s = (o1 + 1) // 2
                            if o3 == 0:
                                pad[b, x, 1:9, 1:9, :] = xpool[s, p]
                            else:
                                pad[b, x, 1:9, z : z + 1, :] = xpool[s, p, :, zs - 1 : zs, :]
                        elif o1 == 0:
                            s = (o2 + 1) // 2
                            if o3 == 0:
                                pad[b, 1:9, y, 1:9, :] = ypool[s, p]
                            else:
                                pad[b, 1:9, y, z : z + 1, :] = ypool[s, p, :, zs - 1 : zs, :]
                        else:
                            s = (o1 + 1) + (o2 + 1) // 2
                            if o3 == 0:
                                pad[b, x, y, 1:9, :] = cpool[s, p]
                            else:
                                pad[b, x, y, z : z + 1, :] = cpool[s, p, zs - 1 : zs, :]
            return carry

        lax.fori_loop(0, 2, one, 0)

    def columns(dst):
        def one(i, carry):
            b, x = i // 10, lax.rem(i, 10)
            for m in range(9):
                o2, o3 = m // 3, m % 3
                cells = pad[b, x, o2 : o2 + 8, o3 : o3 + 8, :]
                dst[i, :, 128 * m : 128 * m + 128] = cells.reshape(64, 128).astype(BF16)
            return carry

        lax.fori_loop(0, 20, one, 0)

    for b in (0, 1):
        for o1 in range(3):
            for x in (8, 9):
                gcat[10 * b + (x + o1) % 10, :, 128 * o1 : 128 * o1 + 128] = jnp.zeros((64, 128), BF16)
    staged["feat"].wait()
    lax.fori_loop(0, 16, fill_interior, 0)
    staged["sl"].wait()
    stage_faces(0)
    staged["cfrom"].wait()
    staged["gcoarse"].wait()

    def stage_gcoarse(step, carry):
        to = lax.rem(c + step, nby)
        gsend[step] = gcoarse[jnp.where(cfrom[1] == to, 1, 0)]
        return carry

    lax.fori_loop(0, nby, stage_gcoarse, 0)
    gpool[0] = gsend[0]

    pl.semaphore_wait(barrier, met)
    first = halo_copies(0)
    for copy in first:
        copy.start()

    def row_copy(src, dst, send, recv, step):
        return pltpu.make_async_remote_copy(
            src_ref=src.at[step], dst_ref=dst.at[step], send_sem=send.at[step], recv_sem=recv.at[step],
            device_id=(r, lax.rem(c + step, nby)), device_id_type=MESH,
        )

    def start_row(src, dst, send, recv):
        def one(step, carry):
            row_copy(src, dst, send, recv, step).start()
            return carry

        lax.fori_loop(1, nby, one, 0)

    def wait_row_recv(src, dst, send, recv):
        def one(step, carry):
            row_copy(src, dst, send, recv, step).wait_recv()
            return carry

        lax.fori_loop(1, nby, one, 0)

    def wait_row_send(src, dst, send, recv):
        def one(step, carry):
            row_copy(src, dst, send, recv, step).wait_send()
            return carry

        lax.fori_loop(1, nby, one, 0)

    start_row(gsend, gpool, g_send, g_recv)
    staged["weight"].wait()
    for k in range(27):
        wback[k // 9, :, 128 * (k % 9) : 128 * (k % 9) + 128] = weight[26 - k]
    staged["down"].wait()
    for q in range(8):
        wdcat[q // 2, :, 128 * (q % 2) : 128 * (q % 2) + 128] = down[q]
    local_pools()
    staged["nb"].wait()
    for copy in first:
        copy.wait_recv()
    remote_pools(0)
    rims()
    columns(col)

    def forward(b, carry):
        total = None
        for o1 in range(3):
            rows = col[pl.ds(b * 10 + o1, 8)].reshape(512, 1152)
            term = jnp.dot(rows, weight[9 * o1 : 9 * o1 + 9].reshape(1152, 128), preferred_element_type=F32)
            total = term if total is None else total + term
        slope[b] = total.reshape(8, 64, 128)
        return carry

    lax.fori_loop(0, 2, forward, 0)

    def activate(i, carry):
        b, a1 = i // 4, lax.rem(i, 4)
        for p1 in (0, 1):
            x = 2 * a1 + p1
            pre = slope[b, x]
            g = jax.nn.sigmoid(pre)
            act = (pre * g).astype(BF16)
            hid_out[b, x] = act
            lines = act.astype(F32).reshape(4, 2, 8, 128)
            for p2 in (0, 1):
                at_row = pl.multiple_of(b * 128 + a1 * 32, 32)
                hpart[2 * p1 + p2, pl.ds(at_row, 32), :] = lines[:, p2].reshape(32, 128).astype(BF16)
            slope[b, x] = g * (1.0 + pre * (1.0 - g))
        return carry

    lax.fori_loop(0, 8, activate, 0)

    staged["cdest"].wait()
    staged["gout"].wait()
    wait_row_recv(gsend, gpool, g_send, g_recv)
    wide[...] = jnp.zeros((2, 256, 128), F32)
    for b in (0, 1):
        block = gpool[lax.rem(c - cdest[b] + nby, nby)].astype(F32)
        wide[0, pl.ds(128 * b, 64, stride=2), :] = block
        wide[1, pl.ds(128 * b + 1, 64, stride=2), :] = block
    cgx[:, :128] = wide[0].astype(BF16)
    cgx[:, 128:] = wide[1].astype(BF16)
    for q in range(4):
        up[q] = lax.dot_general(cgx[...], wdcat[q], (((1,), (1,)), ((), ())), preferred_element_type=F32)

    def pre_grad(i, carry):
        b, a1 = i // 4, lax.rem(i, 4)
        for p1 in (0, 1):
            x = 2 * a1 + p1
            at_row = pl.multiple_of(b * 128 + a1 * 32, 32)
            parts = [up[2 * p1 + p2, pl.ds(at_row, 32), :].reshape(4, 8, 128) for p2 in (0, 1)]
            back = jnp.stack(parts, axis=1).reshape(64, 128)
            grad = ((gout[b, x].astype(F32) + back) * slope[b, x]).astype(BF16)
            for o1 in range(3):
                gcat[b * 10 + x + o1, :, 128 * o1 : 128 * o1 + 128] = grad
            pad[b, x + 1, 1:9, 1:9, :] = grad.astype(F32).reshape(8, 8, 128)
        return carry

    lax.fori_loop(0, 8, pre_grad, 0)
    stage_faces(1)
    second_halo = halo_copies(1)
    for copy in second_halo:
        copy.start()

    def contracted(left, right):
        return lax.dot_general(left, right, (((0,), (0,)), ((), ())), preferred_element_type=F32)

    for q in range(4):
        both = contracted(hpart[q], cgx[...])
        for l in (0, 1):
            n = 2 * q + l
            arf[n // 3, 1152 + 128 * (n % 3) : 1280 + 128 * (n % 3)] = both[:, 128 * l : 128 * l + 128]
    misfits = jnp.int32(0)
    for b in (0, 1):
        for offset in OFFSETS:
            good = fits_grid(nb[b, offset_index(offset)], offset[0], offset[1])
            misfits = misfits + jnp.where(good, 0, 1)
    arf[2, 1408:1536] = jnp.full((128, 128), misfits, jnp.int32).astype(F32)

    my_half = pl.multiple_of(core * HALF_ROWS, HALF_ROWS)
    your_half = pl.multiple_of((1 - core) * HALF_ROWS, HALF_ROWS)

    def core_copy(part):
        return pltpu.make_async_remote_copy(
            src_ref=s0.at[part], dst_ref=r0.at[part], send_sem=core_send.at[0, part], recv_sem=core_recv.at[0, part],
            device_id=other_core, device_id_type=MESH,
        )

    def core_back(part):
        return pltpu.make_async_remote_copy(
            src_ref=fin.at[core, part], dst_ref=fin.at[core, part], send_sem=core_send.at[1, part],
            recv_sem=core_recv.at[1, part], device_id=other_core, device_id_type=MESH,
        )

    def hop(phase, part, src, dst, axis, step):
        return pltpu.make_async_remote_copy(
            src_ref=src, dst_ref=dst, send_sem=ar_send.at[phase, part, step], recv_sem=ar_recv.at[phase, part, step],
            device_id=moved(axis, step), device_id_type=MESH,
        )

    def hops(phase, part):
        a1, a2, a3 = ROUTES[part]
        out = []
        for step in range(1, size[(a1, a2, a3, a2, a1)[phase]]):
            if phase == 0:
                to = lax.rem(at[a1] + step, size[a1])
                out.append(hop(0, part, s1.at[part, to], r1.at[part, step], a1, step))
            elif phase == 1:
                to = lax.rem(at[a2] + step, size[a2])
                out.append(hop(1, part, s2.at[part, to], r2.at[part, step], a2, step))
            elif phase == 2:
                out.append(hop(2, part, r3.at[part, 0], r3.at[part, step], a3, step))
            elif phase == 3:
                place = fin.at[core, part, at[a1], at[a2]]
                out.append(hop(3, part, place, place, a2, step))
            else:
                place = fin.at[core, part, at[a1]]
                out.append(hop(4, part, place, place, a1, step))
        return out

    def run_hops(phase, part):
        for copy in hops(phase, part):
            copy.start()

    def land_hops(phase, part):
        for copy in hops(phase, part):
            copy.wait_recv()

    n1, n2 = nx, nx
    rows1, rows2 = HALF_ROWS // n1, HALF_ROWS // (n1 * n2)

    def weight_grad(part):
        for mm in range(3):
            m = 3 * part + mm
            rows = col[:, :, 128 * m : 128 * m + 128].reshape(1280, 128)
            three = contracted(rows, gcat[...].reshape(1280, 384))
            for o1 in range(3):
                arf[part, 128 * (3 * o1 + mm) : 128 * (3 * o1 + mm) + 128] = three[:, 128 * o1 : 128 * o1 + 128]
        s0[part] = arf[part, pl.ds(your_half, HALF_ROWS), :].astype(BF16)
        core_copy(part).start()

    def start_axes(part):
        core_copy(part).wait_recv()
        hf[part] = arf[part, pl.ds(my_half, HALF_ROWS), :] + r0[part].astype(F32)
        s1[part] = hf[part].astype(BF16).reshape(n1, rows1, 128)
        run_hops(0, part)

    weight_grad(0)

    total = None
    for q in range(4):
        term = jnp.dot(hpart[q], wdcat[q], preferred_element_type=F32)
        total = term if total is None else total + term
    wide[0] = total[:, :128]
    wide[1] = total[:, 128:]
    reduced = wide[0, pl.ds(0, 128, stride=2), :] + wide[1, pl.ds(1, 128, stride=2), :]
    reduced = reduced.astype(BF16).reshape(2, 64, 128)

    for step in range(nby):
        to = lax.rem(c + step, nby)
        second = jnp.full((64, 128), cdest[1], jnp.int32) == to
        block = jnp.where(second, reduced[1].astype(F32), reduced[0].astype(F32)).astype(BF16)
        if step == 0:
            rpool[0] = block
        else:
            rsend[step] = block
    start_row(rsend, rpool, c_send, c_recv)

    weight_grad(1)
    start_axes(0)
    weight_grad(2)
    start_axes(1)
    start_axes(2)

    local_pools()
    for copy in second_halo:
        copy.wait_recv()
    remote_pools(1)
    rims()

    for part in range(3):
        land_hops(0, part)
        mine = hf[part, pl.ds(pl.multiple_of(at[ROUTES[part][0]] * rows1, rows1), rows1), :]
        for step in range(1, n1):
            mine = mine + r1[part, step].astype(F32)
        t1f[part] = mine.reshape(n2, rows2, 128)
        s2[part] = mine.astype(BF16).reshape(n2, rows2, 128)
        run_hops(1, part)

    columns(colg)

    for part in range(3):
        land_hops(1, part)
        mine = t1f[part, at[ROUTES[part][1]]]
        for step in range(1, n2):
            mine = mine + r2[part, step].astype(F32)
        r3[part, 0] = mine.astype(BF16)
        run_hops(2, part)

    def backward(b, carry):
        total = None
        for o1 in range(3):
            rows = colg[pl.ds(b * 10 + o1, 8)].reshape(512, 1152)
            term = lax.dot_general(rows, wback[o1], (((1,), (1,)), ((), ())), preferred_element_type=F32)
            total = term if total is None else total + term
        gfeat_out[b] = total.astype(BF16).reshape(8, 64, 128)
        return carry

    backward(0, 0)

    for part in range(3):
        a1, a2, a3 = ROUTES[part]
        land_hops(2, part)
        whole = None
        for place in range(size[a3]):
            term = r3[part, lax.rem(at[a3] - place + size[a3], size[a3])].astype(F32)
            whole = term if whole is None else whole + term
        fin[core, part, at[a1], at[a2]] = (whole * (1.0 / (nbx * nby))).astype(BF16)
        run_hops(3, part)

    backward(1, 0)

    for part in range(3):
        land_hops(3, part)
        run_hops(4, part)

    wait_row_recv(rsend, rpool, c_send, c_recv)
    for m in (0, 1):
        coarse_out[m] = rpool[lax.rem(c - cfrom[m] + nby, nby)]

    for part in range(3):
        land_hops(4, part)
        core_back(part).start()
    for part in range(3):
        core_back(part).wait_recv()

    for copy in first + second_halo:
        copy.wait_send()
    wait_row_send(gsend, gpool, g_send, g_recv)
    wait_row_send(rsend, rpool, c_send, c_recv)
    for part in range(3):
        core_copy(part).wait_send()
        core_back(part).wait_send()
        for phase in range(5):
            for copy in hops(phase, part):
                copy.wait_send()


def finish_kernel(hid, coarse, gfeat, fin, hid_out, coarse_out, gfeat_out, gw_out, gd_out, misfits, gw, gd, sem):
    copies = []

    def leave(src, dst):
        copies.append(pltpu.make_async_copy(src, dst, sem.at[len(copies)]))
        copies[-1].start()

    leave(hid, hid_out)
    leave(coarse, coarse_out)
    leave(gfeat, gfeat_out)
    for part in range(3):
        low = fin[0, part].reshape(HALF_ROWS, 128).astype(F32).reshape(6, 128, 128)
        high = fin[1, part].reshape(HALF_ROWS, 128).astype(F32).reshape(6, 128, 128)
        for o1, three in enumerate((low[:3], low[3:], high[:3])):
            at = pl.ds(9 * o1 + 3 * part, 3)
            gw[at] = three
            leave(gw.at[at], gw_out.at[at])
        kept = 3 if part < 2 else 2
        gd[3 * part : 3 * part + kept] = high[3 : 3 + kept]
        leave(gd.at[pl.ds(3 * part, kept)], gd_out.at[pl.ds(3 * part, kept)])
    count = fin[1, 2].reshape(HALF_ROWS, 128)[640:656].astype(F32)
    misfits[0] = (jnp.max(count) > 0).astype(jnp.int32)
    for copy in copies:
        copy.wait()


def grid_path(
    sizes, features, weight, down_weight, grad_out, grad_coarse, neighbours, send_list, coarse_dest, coarse_from
):
    nx, ny, nz = sizes
    nby = nx * nz
    rows1, rows2 = HALF_ROWS // nx, HALF_ROWS // (nx * nx)
    vmem = pl.BlockSpec(memory_space=pltpu.VMEM)
    hbm, smem = pl.BlockSpec(memory_space=pltpu.HBM), pl.BlockSpec(memory_space=pltpu.SMEM)
    hidden, coarse, grad_features, grads = pl.pallas_call(
        functools.partial(section_kernel, sizes),
        out_shape=[
            jax.ShapeDtypeStruct((2, 8, 64, 128), BF16),
            jax.ShapeDtypeStruct((2, 64, 128), BF16),
            jax.ShapeDtypeStruct((2, 8, 64, 128), BF16),
            jax.ShapeDtypeStruct((2, 3, nx, nx, rows2, 128), BF16),
        ],
        in_specs=[hbm] * 9,
        out_specs=[vmem] * 4,
        scratch_shapes=[
            pltpu.SMEM((2, 27), jnp.int32),
            pltpu.SMEM((2, LISTS), jnp.int32),
            pltpu.SMEM((2,), jnp.int32),
            pltpu.SMEM((2,), jnp.int32),
            pltpu.VMEM((2, 8, 64, 128), BF16),
            pltpu.VMEM((27, 128, 128), BF16),
            pltpu.VMEM((8, 128, 128), BF16),
            pltpu.VMEM((2, 8, 64, 128), BF16),
            pltpu.VMEM((2, 64, 128), BF16),
            pltpu.SemaphoreType.DMA((9,)),
            pltpu.VMEM((3, 10, 10, 16, 128), F32),
            pltpu.VMEM((20, 64, 1152), BF16),
            pltpu.VMEM((20, 64, 1152), BF16),
            pltpu.VMEM((2, 21, 8, 8, 128), F32),
            pltpu.VMEM((2, 21, 8, 8, 128), F32),
            pltpu.VMEM((4, 21, 8, 128), F32),
            pltpu.VMEM((2, 2, 128, 128), BF16),
            pltpu.VMEM((2, 2, 128, 128), BF16),
            pltpu.VMEM((2, 4, 16, 128), BF16),
            pltpu.VMEM((2, 2, 128, 128), BF16),
            pltpu.VMEM((2, 2, 128, 128), BF16),
            pltpu.VMEM((2, 4, 16, 128), BF16),
            pltpu.VMEM((nby, 64, 128), BF16),
            pltpu.VMEM((nby, 64, 128), BF16),
            pltpu.VMEM((nby, 64, 128), BF16),
            pltpu.VMEM((nby, 64, 128), BF16),
            pltpu.VMEM((3, 128, 1152), BF16),
            pltpu.VMEM((4, 128, 256), BF16),
            pltpu.VMEM((2, 8, 64, 128), F32),
            pltpu.VMEM((4, 256, 128), BF16),
            pltpu.VMEM((2, 256, 128), F32),
            pltpu.VMEM((256, 256), BF16),
            pltpu.VMEM((4, 256, 128), F32),
            pltpu.VMEM((20, 64, 384), BF16),
            pltpu.VMEM((3, PART_ROWS, 128), F32),
            pltpu.VMEM((3, HALF_ROWS, 128), BF16),
            pltpu.VMEM((3, HALF_ROWS, 128), BF16),
            pltpu.VMEM((3, HALF_ROWS, 128), F32),
            pltpu.VMEM((3, nx, rows1, 128), BF16),
            pltpu.VMEM((3, nx, rows1, 128), BF16),
            pltpu.VMEM((3, nx, rows2, 128), F32),
            pltpu.VMEM((3, nx, rows2, 128), BF16),
            pltpu.VMEM((3, nx, rows2, 128), BF16),
            pltpu.VMEM((3, nx, rows2, 128), BF16),
            pltpu.SemaphoreType.DMA((2, 8)),
            pltpu.SemaphoreType.DMA((2, 8)),
            pltpu.SemaphoreType.DMA((nby,)),
            pltpu.SemaphoreType.DMA((nby,)),
            pltpu.SemaphoreType.DMA((nby,)),
            pltpu.SemaphoreType.DMA((nby,)),
            pltpu.SemaphoreType.DMA((5, 3, nx)),
            pltpu.SemaphoreType.DMA((5, 3, nx)),
            pltpu.SemaphoreType.DMA((2, 3)),
            pltpu.SemaphoreType.DMA((2, 3)),
        ],
        compiler_params=pltpu.CompilerParams(
            collective_id=0, has_side_effects=True, vmem_limit_bytes=48 * 2**20
        ),
        cost_estimate=pl.CostEstimate(flops=3 * 10**9, bytes_accessed=6 * 10**6, transcendentals=2**17),
    )(
        neighbours, send_list, coarse_dest, coarse_from,
        features.reshape(2, 8, 64, 128), weight, down_weight, grad_out.reshape(2, 8, 64, 128), grad_coarse,
    )
    hidden, coarse, grad_features, grad_weight, grad_down, misfits = pl.pallas_call(
        finish_kernel,
        out_shape=[
            jax.ShapeDtypeStruct((2, 8, 64, 128), BF16),
            jax.ShapeDtypeStruct((2, 64, 128), BF16),
            jax.ShapeDtypeStruct((2, 8, 64, 128), BF16),
            jax.ShapeDtypeStruct((27, 128, 128), F32),
            jax.ShapeDtypeStruct((8, 128, 128), F32),
            jax.ShapeDtypeStruct((1,), jnp.int32),
        ],
        in_specs=[vmem] * 4,
        out_specs=[hbm] * 5 + [smem],
        scratch_shapes=[
            pltpu.VMEM((27, 128, 128), F32),
            pltpu.VMEM((8, 128, 128), F32),
            pltpu.SemaphoreType.DMA((15,)),
        ],
        compiler_params=pltpu.CompilerParams(vmem_limit_bytes=16 * 2**20),
    )(hidden, coarse, grad_features, grads)
    return (
        (hidden.reshape(features.shape), coarse, grad_features.reshape(features.shape), grad_weight, grad_down),
        misfits[0],
    )


def duplicate_kernel(count, *refs):
    sources, targets, sem = refs[:count], refs[count : 2 * count], refs[2 * count]
    for n in range(count):
        copy = pltpu.make_async_copy(sources[n], targets[n], sem.at[n])
        copy.start()
        copy.wait()


def duplicates(arrays):
    count = len(arrays)
    hbm = pl.BlockSpec(memory_space=pltpu.HBM)
    return pl.pallas_call(
        functools.partial(duplicate_kernel, count),
        out_shape=[jax.ShapeDtypeStruct(array.shape, array.dtype) for array in arrays],
        in_specs=[hbm] * count,
        out_specs=[hbm] * count,
        scratch_shapes=[pltpu.SemaphoreType.DMA((count,))],
        compiler_params=pltpu.CompilerParams(has_side_effects=True),
    )(*arrays)


def per_device(sizes, *operands):
    operands = operands[:6] + (operands[6].T,) + operands[7:]
    results, misfits = grid_path(sizes, *operands)
    _, results = lax.while_loop(
        lambda state: state[0] > 0,
        lambda state: (jnp.zeros((), jnp.int32), tuple(duplicates(general_path(*duplicates(operands))))),
        (misfits, results),
    )
    return results


def solution(mesh):
    nby = mesh.shape["by"]
    nx = {16: 4, 4: 2}[nby]
    sizes = (nx, mesh.shape["bx"] // 2, nby // nx)
    in_specs = (
        P(("bx", "by"), None, None, None, None),
        P(),
        P(),
        P(("bx", "by"), None, None, None, None),
        P(("bx", "by"), None, None),
        P(("bx", "by"), None),
        P(("bx", "by"), None),
        P(("bx", "by")),
        P(("bx", "by")),
    )
    out_specs = (
        P(("bx", "by"), None, None, None, None),
        P(("bx", "by"), None, None),
        P(("bx", "by"), None, None, None, None),
        P(),
        P(),
    )
    return jax.shard_map(
        functools.partial(per_device, sizes), mesh=mesh, in_specs=in_specs, out_specs=out_specs, check_vma=False
    )
```

```python
import functools

import jax
import jax.numpy as jnp
from jax import lax
from jax.experimental import pallas as pl
from jax.experimental.pallas import tpu as pltpu
from jax.sharding import PartitionSpec as P

OFFSETS = [(p, q, w) for p in (-1, 0, 1) for q in (-1, 0, 1) for w in (-1, 0, 1)]


def with_halo(cells, sides, width):
    for axis, dim in sides:
        count = lax.axis_size(axis)
        ends = count - 1
        head = lax.slice_in_dim(cells, 0, width, axis=dim)
        tail = lax.slice_in_dim(cells, cells.shape[dim] - width, cells.shape[dim], axis=dim)
        cells = jnp.concatenate(
            [
                lax.ppermute(tail, axis, [(i, (i + 1) % count) for i in range(ends)]),
                cells,
                lax.ppermute(head, axis, [((i + 1) % count, i) for i in range(ends)]),
            ],
            axis=dim,
        )
    return cells


def offset_index(offset):
    return (offset[0] + 1) * 9 + (offset[1] + 1) * 3 + offset[2] + 1


def span_of(step, edge_len):
    if step == -1:
        return slice(edge_len - 1, edge_len)
    if step == 1:
        return slice(0, 1)
    return slice(0, edge_len)


def assemble(piece_at):
    planes = []
    for step_x in (-1, 0, 1):
        lines = []
        for step_y in (-1, 0, 1):
            cells = [piece_at((step_x, step_y, step_z)) for step_z in (-1, 0, 1)]
            lines.append(jnp.concatenate(cells, axis=3))
        planes.append(jnp.concatenate(lines, axis=2))
    return jnp.concatenate(planes, axis=1)


def window(padded, offset, sign):
    edge_len = padded.shape[1] - 2
    starts = [1 + sign * offset[axis_id] for axis_id in range(3)]
    return padded[
        :,
        starts[0] : starts[0] + edge_len,
        starts[1] : starts[1] + edge_len,
        starts[2] : starts[2] + edge_len,
    ]


def conv_rows(padded, weight, sign):
    channels = padded.shape[-1]
    running = None
    for offset in OFFSETS:
        shifted = window(padded, offset, sign).reshape(-1, channels)
        matrix = weight[offset_index(offset)]
        if sign < 0:
            matrix = matrix.T
        term = jnp.dot(shifted, matrix, preferred_element_type=jnp.float32)
        running = term if running is None else running + term
    return running


def contract(left, right):
    return lax.dot_general(
        left, right, (((0,), (0,)), ((), ())), preferred_element_type=jnp.float32
    )


def children(hidden):
    block_count, edge_len, channels = (hidden.shape[0], hidden.shape[1], hidden.shape[-1])
    half_edge = edge_len // 2
    parted = hidden.reshape(block_count, half_edge, 2, half_edge, 2, half_edge, 2, channels)
    return [
        parted[:, :, i, :, j, :, l, :].reshape(-1, channels)
        for i in (0, 1)
        for j in (0, 1)
        for l in (0, 1)
    ]


def down_blocks(hidden, down_weight):
    block_count, channels = (hidden.shape[0], hidden.shape[-1])
    running = None
    for child_id, rows_in in enumerate(children(hidden)):
        term = jnp.dot(rows_in, down_weight[child_id], preferred_element_type=jnp.float32)
        running = term if running is None else running + term
    return running.reshape(block_count, -1, channels)


def up_blocks(coarse_grad, down_weight, edge_len):
    block_count, channels = (coarse_grad.shape[0], coarse_grad.shape[-1])
    half_edge = edge_len // 2
    flat_grad = coarse_grad.reshape(-1, channels)
    parts_list = [
        jnp.dot(flat_grad, down_weight[child_id].T, preferred_element_type=jnp.float32)
        for child_id in range(8)
    ]
    stacked = jnp.stack(parts_list).reshape(
        2, 2, 2, block_count, half_edge, half_edge, half_edge, channels
    )
    return stacked.transpose(3, 4, 0, 5, 1, 6, 2, 7).reshape(
        block_count, edge_len, edge_len, edge_len, channels
    )


def face_stack(blocks):
    return jnp.stack(
        [
            blocks[:, 0],
            blocks[:, -1],
            blocks[:, :, 0],
            blocks[:, :, -1],
            blocks[:, :, :, 0],
            blocks[:, :, :, -1],
        ],
        axis=1,
    )


def listed_faces(blocks, send_list):
    block_count = blocks.shape[0]
    all_faces = face_stack(blocks)
    zero_face = jnp.zeros((1,) + all_faces.shape[1:], all_faces.dtype)
    extended = jnp.concatenate([all_faces, zero_face], axis=0)
    picked = jnp.take(extended, jnp.where(send_list < 0, block_count, send_list), axis=0)
    return (all_faces, zero_face, picked)


def build_padded(blocks, face_pool, neighbours):
    edge_len = blocks.shape[1]

    def piece_at(offset):
        if offset == (0, 0, 0):
            return blocks
        axis_lead = [axis_id for axis_id in range(3) if offset[axis_id] != 0][0]
        face_id = 2 * axis_lead + (0 if offset[axis_lead] == 1 else 1)
        face_rows = jnp.take(face_pool, neighbours[:, offset_index(offset)] * 6 + face_id, axis=0)
        others = [axis_id for axis_id in range(3) if axis_id != axis_lead]
        face_rows = face_rows[
            :, span_of(offset[others[0]], edge_len), span_of(offset[others[1]], edge_len)
        ]
        return jnp.expand_dims(face_rows, 1 + axis_lead)

    return assemble(piece_at)


def padded_for(blocks, send_list, neighbours):
    slot_cap = send_list.shape[1]
    all_faces, zero_face, picked = listed_faces(blocks, send_list)
    outgoing = picked.reshape((3, 3) + picked.shape[1:])
    padded = with_halo(outgoing, (("bx", 0), ("by", 1)), 1)
    received = padded[::2, ::2]
    face_pool = jnp.concatenate(
        [all_faces, received.reshape((9 * slot_cap,) + all_faces.shape[1:]), zero_face], axis=0
    )
    return build_padded(blocks, face_pool.reshape((-1,) + all_faces.shape[2:]), neighbours)


def row_gathered(blocks):
    count = lax.axis_size("by")
    me = lax.axis_index("by")

    def one(step, state):
        held, gathered = state
        held = lax.ppermute(held, "by", [(i, (i + 1) % count) for i in range(count)])
        return held, gathered.at[lax.rem(me - step + count, count)].set(held)

    gathered = jnp.zeros((count,) + blocks.shape, blocks.dtype).at[me].set(blocks)
    return lax.fori_loop(1, count, one, (blocks, gathered))[1]


def summed(terms):
    for axis in ("bx", "by"):
        count, distance = lax.axis_size(axis), 1
        while distance < count:
            pairs = [(i, i ^ distance) for i in range(count)]
            terms = [term + lax.ppermute(term, axis, pairs) for term in terms]
            distance *= 2
    return terms


def general_path(
    features,
    weight,
    down_weight,
    grad_out,
    grad_coarse,
    neighbours,
    send_list,
    coarse_dest,
    coarse_from,
):
    send_list = send_list.T
    block_count, edge_len, channels = (features.shape[0], features.shape[1], features.shape[-1])
    device_total = lax.axis_size("bx") * lax.axis_size("by")
    padded_in = padded_for(features, send_list, neighbours)
    preact = conv_rows(padded_in, weight, 1).reshape(features.shape)
    hidden = jax.nn.silu(preact).astype(jnp.bfloat16)
    reduced = down_blocks(hidden, down_weight).astype(jnp.bfloat16)
    slots = jnp.arange(block_count)
    coarse = row_gathered(reduced)[coarse_from, slots]
    coarse_grad_here = row_gathered(grad_coarse)[coarse_dest, slots]
    flat_grad = coarse_grad_here.reshape(-1, channels)
    down_terms = jnp.stack([contract(rows_in, flat_grad) for rows_in in children(hidden)])
    sigmoid_pre = jax.nn.sigmoid(preact)
    grad_pre = (
        (grad_out.astype(jnp.float32) + up_blocks(coarse_grad_here, down_weight, edge_len))
        * sigmoid_pre
        * (1.0 + preact * (1.0 - sigmoid_pre))
    ).astype(jnp.bfloat16)
    padded_grad = padded_for(grad_pre, send_list, neighbours)
    grad_features = conv_rows(padded_grad, weight, -1).reshape(features.shape).astype(jnp.bfloat16)
    own_rows = grad_pre.reshape(-1, channels)
    weight_terms = jnp.stack(
        [
            contract(window(padded_in, offset, 1).reshape(-1, channels), own_rows)
            for offset in OFFSETS
        ]
    )
    weight_total, down_total = summed([weight_terms, down_terms])
    return (hidden, coarse, grad_features, weight_total / device_total, down_total / device_total)


F32, BF16 = jnp.float32, jnp.bfloat16
MESH = pl.DeviceIdType.MESH
NONE = 20
LISTS = 9
ROUTES = (("x", "y", "z"), ("y", "z", "x"), ("z", "x", "y"))
PART_ROWS = 1536
HALF_ROWS = 768


def fits_grid(p, o1, o2):
    half = p // 2
    good = (half == 0) | (half == NONE // 2)
    for dr in {0, o1}:
        for dc in {0, o2}:
            if (dr, dc) != (0, 0):
                good = good | (half == (dr + 1) * 3 + dc + 2)
    return good


def section_kernel(
    sizes,
    nb_in, sl_in, cdest_in, cfrom_in, feat_in, weight_in, down_in, gout_in, gcoarse_in,
    hid_out, coarse_out, gfeat_out, fin,
    nb, sl, cdest, cfrom, feat, weight, down, gout, gcoarse, in_sem,
    pad, col, colg, xpool, ypool, cpool,
    xs, ys, cs, xr, yr, cr,
    gsend, gpool, rsend, rpool,
    wback, wdcat, small, slope, hpart, wide, cgx, up, gcat,
    arf, s0, r0, hf, s1, r1, r3,
    halo_send, halo_recv, g_send, g_recv, c_send, c_recv, plane_send, plane_recv, axis_send, axis_recv, core_send, core_recv,
):
    nx, ny, nz = sizes
    nby, nbx = nx * nz, 2 * ny
    ring = nx
    r, c = lax.axis_index("bx"), lax.axis_index("by")
    core, at = lax.rem(r, 2), {"x": lax.rem(c, nx), "y": r // 2, "z": c // nx}
    size = {"x": nx, "y": ny, "z": nz}

    def moved(axis, step):
        to = dict(at)
        to[axis] = lax.rem(at[axis] + step, size[axis])
        return (to["y"] * 2 + core, to["z"] * nx + to["x"])

    other_core = (r + 1 - 2 * core, c)

    def beside(dr, dc):
        return (lax.rem(r + dr + nbx, nbx), lax.rem(c + dc + nby, nby))

    around = [(dr, dc) for dr in (-1, 0, 1) for dc in (-1, 0, 1) if (dr, dc) != (0, 0)]

    barrier = pltpu.get_barrier_semaphore()

    met = nby - 1
    for dr, dc in around:
        if dr != 0:
            pl.semaphore_signal(barrier, inc=1, device_id=beside(dr, dc), device_id_type=MESH)
            met += 1

    def greet(step, carry):
        pl.semaphore_signal(barrier, inc=1, device_id=(r, lax.rem(c + step, nby)), device_id_type=MESH)
        return carry

    lax.fori_loop(1, nby, greet, 0)

    def greet_planes(n, carry):
        y = lax.rem(at["y"] + 1 + n // (ring - 1), ring)
        step = 1 + lax.rem(n, ring - 1)
        x, z = lax.rem(at["x"] + step, ring), lax.rem(at["z"] + step, ring)
        for device in ((y * 2 + core, at["z"] * nx + x), (y * 2 + core, z * nx + at["x"])):
            pl.semaphore_signal(barrier, inc=1, device_id=device, device_id_type=MESH)
        return carry

    lax.fori_loop(0, (ring - 1) ** 2, greet_planes, 0)
    met += 2 * (ring - 1) ** 2
    for step in range(1, ny):
        pl.semaphore_signal(barrier, inc=1, device_id=moved("y", step), device_id_type=MESH)
        met += 1

    staged = {}
    pairs = (
        ("sl", sl_in, sl), ("feat", feat_in, feat), ("cfrom", cfrom_in, cfrom), ("gcoarse", gcoarse_in, gcoarse),
        ("nb", nb_in, nb), ("down", down_in, down), ("weight", weight_in, weight), ("cdest", cdest_in, cdest),
        ("gout", gout_in, gout),
    )
    for n, (name, src, dst) in enumerate(pairs):
        staged[name] = pltpu.make_async_copy(src, dst, in_sem.at[n])
        staged[name].start()

    def fill_interior(i, carry):
        b, x = i // 8, lax.rem(i, 8)
        pad[b, x + 1, 1:9, 1:9, :] = feat[b, x].astype(F32).reshape(8, 8, 128)
        return carry

    pad[2, 1:9, 1:9] = jnp.zeros((8, 8, 16, 128), F32)
    for side in (0, 1):
        xpool[side, NONE] = jnp.zeros((8, 8, 128), F32)
        ypool[side, NONE] = jnp.zeros((8, 8, 128), F32)
    for corner in range(4):
        cpool[corner, NONE] = jnp.zeros((8, 128), F32)

    near = (8, 1)
    edge = (1, 8)

    def stage_faces(t):
        for side in (0, 1):
            step = 2 * side - 1
            for j in (0, 1):
                bx_block = jnp.maximum(sl[j, (step + 1) * 3 + 1], 0)
                face = pad[bx_block, edge[side], 1:9, 1:9, :]
                xs[t, side, 64 * j : 64 * j + 64] = face.reshape(64, 128).astype(BF16)
                by_block = jnp.maximum(sl[j, 3 + step + 1], 0)
                face = pad[by_block, 1:9, edge[side], 1:9, :]
                ys[t, side, 64 * j : 64 * j + 64] = face.reshape(64, 128).astype(BF16)
        for sx in (0, 1):
            for sy in (0, 1):
                row = 2 * sx * 3 + 2 * sy
                lines = [pad[jnp.maximum(sl[j, row], 0), edge[sx], edge[sy], 1:9, :] for j in (0, 1)]
                cs[t, 2 * sx + sy] = jnp.concatenate(lines, axis=0).astype(BF16)

    def halo_copies(t):
        out = []
        for side in (0, 1):
            out.append((xs.at[t, side], xr.at[t, 1 - side], beside(2 * side - 1, 0)))
        for side in (0, 1):
            out.append((ys.at[t, side], yr.at[t, 1 - side], beside(0, 2 * side - 1)))
        for sx in (0, 1):
            for sy in (0, 1):
                out.append((cs.at[t, 2 * sx + sy], cr.at[t, 3 - 2 * sx - sy], beside(2 * sx - 1, 2 * sy - 1)))
        return [
            pltpu.make_async_remote_copy(
                src_ref=src, dst_ref=dst, send_sem=halo_send.at[t, n], recv_sem=halo_recv.at[t, n],
                device_id=to, device_id_type=MESH,
            )
            for n, (src, dst, to) in enumerate(out)
        ]

    def local_pools():
        for side in (0, 1):
            for b in (0, 1):
                xpool[side, b] = pad[b, near[side], 1:9, 1:9, :]
                ypool[side, b] = pad[b, 1:9, near[side], 1:9, :]
        for sx in (0, 1):
            for sy in (0, 1):
                for b in (0, 1):
                    cpool[2 * sx + sy, b] = pad[b, near[sx], near[sy], 1:9, :]

    def remote_pools(t):
        for side in (0, 1):
            for j in (0, 1):
                ex, ey = 2 * side * 3 + 1, 3 + 2 * side
                xpool[side, 2 + 2 * ex + j] = xr[t, side, 64 * j : 64 * j + 64].astype(F32).reshape(8, 8, 128)
                ypool[side, 2 + 2 * ey + j] = yr[t, side, 64 * j : 64 * j + 64].astype(F32).reshape(8, 8, 128)
        for sx in (0, 1):
            for sy in (0, 1):
                lines = cr[t, 2 * sx + sy].astype(F32).reshape(2, 8, 128)
                for j in (0, 1):
                    ex, ey, ec = 2 * sx * 3 + 1, 3 + 2 * sy, 2 * sx * 3 + 2 * sy
                    cpool[2 * sx + sy, 2 + 2 * ex + j] = xpool[sx, 2 + 2 * ex + j, near[sy] - 1]
                    cpool[2 * sx + sy, 2 + 2 * ey + j] = ypool[sy, 2 + 2 * ey + j, near[sx] - 1]
                    cpool[2 * sx + sy, 2 + 2 * ec + j] = lines[j]

    def rims():
        def one(b, carry):
            for o1 in (-1, 0, 1):
                for o2 in (-1, 0, 1):
                    for o3 in (-1, 0, 1):
                        if (o1, o2, o3) == (0, 0, 0):
                            continue
                        p = nb[b, offset_index((o1, o2, o3))]
                        x, y, z = [(0, None, 9)[o + 1] for o in (o1, o2, o3)]
                        zs = (8, None, 1)[o3 + 1]
                        if o1 == 0 and o2 == 0:
                            pad[b, 1:9, 1:9, z : z + 1, :] = pad[jnp.minimum(p, 2), 1:9, 1:9, zs : zs + 1, :]
                        elif o2 == 0:
                            s = (o1 + 1) // 2
                            if o3 == 0:
                                pad[b, x, 1:9, 1:9, :] = xpool[s, p]
                            else:
                                pad[b, x, 1:9, z : z + 1, :] = xpool[s, p, :, zs - 1 : zs, :]
                        elif o1 == 0:
                            s = (o2 + 1) // 2
                            if o3 == 0:
                                pad[b, 1:9, y, 1:9, :] = ypool[s, p]
                            else:
                                pad[b, 1:9, y, z : z + 1, :] = ypool[s, p, :, zs - 1 : zs, :]
                        else:
                            s = (o1 + 1) + (o2 + 1) // 2
                            if o3 == 0:
                                pad[b, x, y, 1:9, :] = cpool[s, p]
                            else:
                                pad[b, x, y, z : z + 1, :] = cpool[s, p, zs - 1 : zs, :]
            return carry

        lax.fori_loop(0, 2, one, 0)

    def columns(dst):
        def one(i, carry):
            b, x = i // 10, lax.rem(i, 10)
            for m in range(9):
                o2, o3 = m // 3, m % 3
                cells = pad[b, x, o2 : o2 + 8, o3 : o3 + 8, :]
                dst[i, :, 128 * m : 128 * m + 128] = cells.reshape(64, 128).astype(BF16)
            return carry

        lax.fori_loop(0, 20, one, 0)

    for b in (0, 1):
        for o1 in range(3):
            for x in (8, 9):
                gcat[10 * b + (x + o1) % 10, :, 128 * o1 : 128 * o1 + 128] = jnp.zeros((64, 128), BF16)
    staged["feat"].wait()
    lax.fori_loop(0, 16, fill_interior, 0)
    staged["sl"].wait()
    stage_faces(0)
    staged["cfrom"].wait()
    staged["gcoarse"].wait()

    def stage_gcoarse(step, carry):
        to = lax.rem(c + step, nby)
        gsend[step] = gcoarse[jnp.where(cfrom[1] == to, 1, 0)]
        return carry

    lax.fori_loop(0, nby, stage_gcoarse, 0)
    gpool[0] = gsend[0]

    pl.semaphore_wait(barrier, met)
    first = halo_copies(0)
    for copy in first:
        copy.start()

    def start_row(src, dst, send, recv):
        def one(step, carry):
            pltpu.make_async_remote_copy(
                src_ref=src.at[step], dst_ref=dst.at[step], send_sem=send, recv_sem=recv,
                device_id=(r, lax.rem(c + step, nby)), device_id_type=MESH,
            ).start()
            return carry

        lax.fori_loop(1, nby, one, 0)

    def all_of(ref, send, recv):
        return pltpu.make_async_remote_copy(
            src_ref=ref, dst_ref=ref, send_sem=send, recv_sem=recv, device_id=other_core, device_id_type=MESH
        )

    def row_waits(buffer, send, recv):
        return all_of(buffer.at[pl.ds(1, nby - 1)], send, recv)

    start_row(gsend, gpool, g_send, g_recv)
    staged["weight"].wait()
    for k in range(27):
        wback[k // 9, :, 128 * (k % 9) : 128 * (k % 9) + 128] = weight[26 - k]
    staged["down"].wait()
    for q in range(8):
        wdcat[q // 2, :, 128 * (q % 2) : 128 * (q % 2) + 128] = down[q]
    local_pools()
    staged["nb"].wait()
    for copy in first:
        copy.wait_recv()
    remote_pools(0)
    rims()
    columns(col)

    def forward(b, carry):
        total = None
        for o1 in range(3):
            rows = col[pl.ds(b * 10 + o1, 8)].reshape(512, 1152)
            term = jnp.dot(rows, weight[9 * o1 : 9 * o1 + 9].reshape(1152, 128), preferred_element_type=F32)
            total = term if total is None else total + term
        slope[b] = total.reshape(8, 64, 128)
        return carry

    lax.fori_loop(0, 2, forward, 0)

    def activate(i, carry):
        b, a1 = i // 4, lax.rem(i, 4)
        for p1 in (0, 1):
            x = 2 * a1 + p1
            pre = slope[b, x]
            g = jax.nn.sigmoid(pre)
            act = (pre * g).astype(BF16)
            hid_out[b, x] = act
            lines = act.astype(F32).reshape(4, 2, 8, 128)
            for p2 in (0, 1):
                at_row = pl.multiple_of(b * 128 + a1 * 32, 32)
                hpart[2 * p1 + p2, pl.ds(at_row, 32), :] = lines[:, p2].reshape(32, 128).astype(BF16)
            slope[b, x] = g * (1.0 + pre * (1.0 - g))
        return carry

    lax.fori_loop(0, 8, activate, 0)

    staged["cdest"].wait()
    staged["gout"].wait()
    row_waits(gpool, g_send, g_recv).wait_recv()
    wide[...] = jnp.zeros((2, 256, 128), F32)
    for b in (0, 1):
        block = gpool[lax.rem(c - cdest[b] + nby, nby)].astype(F32)
        wide[0, pl.ds(128 * b, 64, stride=2), :] = block
        wide[1, pl.ds(128 * b + 1, 64, stride=2), :] = block
    cgx[:, :128] = wide[0].astype(BF16)
    cgx[:, 128:] = wide[1].astype(BF16)
    for q in range(4):
        up[q] = lax.dot_general(cgx[...], wdcat[q], (((1,), (1,)), ((), ())), preferred_element_type=F32)

    def pre_grad(i, carry):
        b, a1 = i // 4, lax.rem(i, 4)
        for p1 in (0, 1):
            x = 2 * a1 + p1
            at_row = pl.multiple_of(b * 128 + a1 * 32, 32)
            parts = [up[2 * p1 + p2, pl.ds(at_row, 32), :].reshape(4, 8, 128) for p2 in (0, 1)]
            back = jnp.stack(parts, axis=1).reshape(64, 128)
            grad = ((gout[b, x].astype(F32) + back) * slope[b, x]).astype(BF16)
            for o1 in range(3):
                gcat[b * 10 + x + o1, :, 128 * o1 : 128 * o1 + 128] = grad
            pad[b, x + 1, 1:9, 1:9, :] = grad.astype(F32).reshape(8, 8, 128)
        return carry

    lax.fori_loop(0, 8, pre_grad, 0)
    def contracted(left, right):
        return lax.dot_general(left, right, (((0,), (0,)), ((), ())), preferred_element_type=F32)

    for q in range(4):
        both = contracted(hpart[q], cgx[...])
        for l in (0, 1):
            n = 2 * q + l
            arf[n // 3, 1152 + 128 * (n % 3) : 1280 + 128 * (n % 3)] = both[:, 128 * l : 128 * l + 128]
    misfits = jnp.int32(0)
    for b in (0, 1):
        for offset in OFFSETS:
            good = fits_grid(nb[b, offset_index(offset)], offset[0], offset[1])
            misfits = misfits + jnp.where(good, 0, 1)
    arf[2, 1408:1536] = jnp.full((128, 128), misfits, jnp.int32).astype(F32)

    my_half = pl.multiple_of(core * HALF_ROWS, HALF_ROWS)
    your_half = pl.multiple_of((1 - core) * HALF_ROWS, HALF_ROWS)

    def core_copy(part):
        return pltpu.make_async_remote_copy(
            src_ref=s0.at[part], dst_ref=r0.at[part], send_sem=core_send.at[0, part], recv_sem=core_recv.at[0, part],
            device_id=other_core, device_id_type=MESH,
        )

    def core_back(part):
        return pltpu.make_async_remote_copy(
            src_ref=fin.at[core, part], dst_ref=fin.at[core, part], send_sem=core_send.at[1, part],
            recv_sem=core_recv.at[1, part], device_id=other_core, device_id_type=MESH,
        )

    plane, chunk = ring * ring, HALF_ROWS // (ring * ring)

    def spot(part):
        a1, a2, _ = ROUTES[part]
        return at[a1] * ring + at[a2]

    def plane_copy(back, part, step):
        a1, a2, _ = ROUTES[part]
        to = dict(at)
        to[a1] = lax.rem(at[a1] + step // ring, ring)
        to[a2] = lax.rem(at[a2] + lax.rem(step, ring), ring)
        if back:
            src = dst = fin.at[core, part, spot(part)]
        else:
            src, dst = s1.at[part, to[a1] * ring + to[a2]], r1.at[part, step]
        return pltpu.make_async_remote_copy(
            src_ref=src, dst_ref=dst, send_sem=plane_send.at[back, part], recv_sem=plane_recv.at[back, part],
            device_id=(to["y"] * 2 + core, to["z"] * nx + to["x"]), device_id_type=MESH,
        )

    def start_copies(back, part):
        def one(step, carry):
            plane_copy(back, part, step).start()
            return carry

        lax.fori_loop(1, plane, one, 0)

    def plane_waits(back, part):
        landed = fin.at[core, part, pl.ds(0, plane - 1)] if back else r1.at[part, pl.ds(1, plane - 1)]
        return all_of(landed, plane_send.at[back, part], plane_recv.at[back, part])

    def axis_copies(part):
        return [
            pltpu.make_async_remote_copy(
                src_ref=r3.at[part, 0], dst_ref=r3.at[part, step], send_sem=axis_send.at[part, step],
                recv_sem=axis_recv.at[part, step], device_id=moved(ROUTES[part][2], step), device_id_type=MESH,
            )
            for step in range(1, ring)
        ]

    def weight_grad(part):
        for mm in range(3):
            m = 3 * part + mm
            rows = col[:, :, 128 * m : 128 * m + 128].reshape(1280, 128)
            three = contracted(rows, gcat[...].reshape(1280, 384))
            for o1 in range(3):
                arf[part, 128 * (3 * o1 + mm) : 128 * (3 * o1 + mm) + 128] = three[:, 128 * o1 : 128 * o1 + 128]
        s0[part] = arf[part, pl.ds(your_half, HALF_ROWS), :].astype(BF16)
        core_copy(part).start()

    def start_plane(part):
        core_copy(part).wait_recv()
        hf[part] = arf[part, pl.ds(my_half, HALF_ROWS), :] + r0[part].astype(F32)
        s1[part] = hf[part].astype(BF16).reshape(plane, chunk, 128)
        start_copies(0, part)

    def start_axis(part):
        plane_waits(0, part).wait_recv()
        mine = hf[part, pl.ds(pl.multiple_of(spot(part) * chunk, chunk), chunk), :]
        for step in range(1, plane):
            mine = mine + r1[part, step].astype(F32)
        r3[part, 0] = mine.astype(BF16)
        for copy in axis_copies(part):
            copy.start()

    def start_back(part):
        a3 = ROUTES[part][2]
        for copy in axis_copies(part):
            copy.wait_recv()
        whole = None
        for place in range(ring):
            term = r3[part, lax.rem(at[a3] - place + ring, ring)].astype(F32)
            whole = term if whole is None else whole + term
        fin[core, part, spot(part)] = (whole * (1.0 / (nbx * nby))).astype(BF16)
        start_copies(1, part)

    weight_grad(0)
    stage_faces(1)
    second_halo = halo_copies(1)
    for copy in second_halo:
        copy.start()
    total = None
    for q in range(4):
        term = jnp.dot(hpart[q], wdcat[q], preferred_element_type=F32)
        total = term if total is None else total + term
    wide[0] = total[:, :128]
    wide[1] = total[:, 128:]
    reduced = wide[0, pl.ds(0, 128, stride=2), :] + wide[1, pl.ds(1, 128, stride=2), :]
    small[...] = reduced.astype(BF16).reshape(2, 64, 128)

    def stage_reduced(step, carry):
        rsend[step] = small[jnp.where(cdest[1] == lax.rem(c + step, nby), 1, 0)]
        return carry

    lax.fori_loop(0, nby, stage_reduced, 0)
    rpool[0] = rsend[0]
    start_row(rsend, rpool, c_send, c_recv)

    weight_grad(1)
    start_plane(0)
    weight_grad(2)
    start_plane(1)
    start_plane(2)

    local_pools()
    for copy in second_halo:
        copy.wait_recv()
    remote_pools(1)
    rims()
    start_axis(0)
    start_axis(1)
    start_axis(2)
    columns(colg)

    def backward(b, carry):
        total = None
        for o1 in range(3):
            rows = colg[pl.ds(b * 10 + o1, 8)].reshape(512, 1152)
            term = lax.dot_general(rows, wback[o1], (((1,), (1,)), ((), ())), preferred_element_type=F32)
            total = term if total is None else total + term
        gfeat_out[b] = total.astype(BF16).reshape(8, 64, 128)
        return carry

    backward(0, 0)
    for part in range(3):
        start_back(part)
    backward(1, 0)

    row_waits(rpool, c_send, c_recv).wait_recv()
    for m in (0, 1):
        coarse_out[m] = rpool[lax.rem(c - cfrom[m] + nby, nby)]

    for part in range(3):
        plane_waits(1, part).wait_recv()
        core_back(part).start()
    for part in range(3):
        core_back(part).wait_recv()

    for copy in first + second_halo:
        copy.wait_send()
    row_waits(gsend, g_send, g_recv).wait_send()
    row_waits(rsend, c_send, c_recv).wait_send()
    for part in range(3):
        core_copy(part).wait_send()
        core_back(part).wait_send()
        plane_waits(0, part).wait_send()
        plane_waits(1, part).wait_send()
        for copy in axis_copies(part):
            copy.wait_send()


def finish_kernel(hid, coarse, gfeat, fin, hid_out, coarse_out, gfeat_out, gw_out, gd_out, misfits, gw, gd, sem):
    copies = []

    def leave(src, dst):
        copies.append(pltpu.make_async_copy(src, dst, sem.at[len(copies)]))
        copies[-1].start()

    leave(hid, hid_out)
    leave(coarse, coarse_out)
    leave(gfeat, gfeat_out)
    for part in range(3):
        low = fin[0, part].reshape(HALF_ROWS, 128).astype(F32).reshape(6, 128, 128)
        high = fin[1, part].reshape(HALF_ROWS, 128).astype(F32).reshape(6, 128, 128)
        for o1, three in enumerate((low[:3], low[3:], high[:3])):
            at = pl.ds(9 * o1 + 3 * part, 3)
            gw[at] = three
            leave(gw.at[at], gw_out.at[at])
        kept = 3 if part < 2 else 2
        gd[3 * part : 3 * part + kept] = high[3 : 3 + kept]
        leave(gd.at[pl.ds(3 * part, kept)], gd_out.at[pl.ds(3 * part, kept)])
    count = fin[1, 2].reshape(HALF_ROWS, 128)[640:656].astype(F32)
    misfits[0] = (jnp.max(count) > 0).astype(jnp.int32)
    for copy in copies:
        copy.wait()


def grid_path(
    sizes, features, weight, down_weight, grad_out, grad_coarse, neighbours, send_list, coarse_dest, coarse_from
):
    nx, ny, nz = sizes
    nby = nx * nz
    plane, chunk = nx * nx, HALF_ROWS // (nx * nx)
    vmem = pl.BlockSpec(memory_space=pltpu.VMEM)
    hbm, smem = pl.BlockSpec(memory_space=pltpu.HBM), pl.BlockSpec(memory_space=pltpu.SMEM)
    hidden, coarse, grad_features, grads = pl.pallas_call(
        functools.partial(section_kernel, sizes),
        out_shape=[
            jax.ShapeDtypeStruct((2, 8, 64, 128), BF16),
            jax.ShapeDtypeStruct((2, 64, 128), BF16),
            jax.ShapeDtypeStruct((2, 8, 64, 128), BF16),
            jax.ShapeDtypeStruct((2, 3, plane, chunk, 128), BF16),
        ],
        in_specs=[hbm] * 9,
        out_specs=[vmem] * 4,
        scratch_shapes=[
            pltpu.SMEM((2, 27), jnp.int32),
            pltpu.SMEM((2, LISTS), jnp.int32),
            pltpu.SMEM((2,), jnp.int32),
            pltpu.SMEM((2,), jnp.int32),
            pltpu.VMEM((2, 8, 64, 128), BF16),
            pltpu.VMEM((27, 128, 128), BF16),
            pltpu.VMEM((8, 128, 128), BF16),
            pltpu.VMEM((2, 8, 64, 128), BF16),
            pltpu.VMEM((2, 64, 128), BF16),
            pltpu.SemaphoreType.DMA((9,)),
            pltpu.VMEM((3, 10, 10, 16, 128), F32),
            pltpu.VMEM((20, 64, 1152), BF16),
            pltpu.VMEM((20, 64, 1152), BF16),
            pltpu.VMEM((2, 21, 8, 8, 128), F32),
            pltpu.VMEM((2, 21, 8, 8, 128), F32),
            pltpu.VMEM((4, 21, 8, 128), F32),
            pltpu.VMEM((2, 2, 128, 128), BF16),
            pltpu.VMEM((2, 2, 128, 128), BF16),
            pltpu.VMEM((2, 4, 16, 128), BF16),
            pltpu.VMEM((2, 2, 128, 128), BF16),
            pltpu.VMEM((2, 2, 128, 128), BF16),
            pltpu.VMEM((2, 4, 16, 128), BF16),
            pltpu.VMEM((nby, 64, 128), BF16),
            pltpu.VMEM((nby, 64, 128), BF16),
            pltpu.VMEM((nby, 64, 128), BF16),
            pltpu.VMEM((nby, 64, 128), BF16),
            pltpu.VMEM((3, 128, 1152), BF16),
            pltpu.VMEM((4, 128, 256), BF16),
            pltpu.VMEM((2, 64, 128), BF16),
            pltpu.VMEM((2, 8, 64, 128), F32),
            pltpu.VMEM((4, 256, 128), BF16),
            pltpu.VMEM((2, 256, 128), F32),
            pltpu.VMEM((256, 256), BF16),
            pltpu.VMEM((4, 256, 128), F32),
            pltpu.VMEM((20, 64, 384), BF16),
            pltpu.VMEM((3, PART_ROWS, 128), F32),
            pltpu.VMEM((3, HALF_ROWS, 128), BF16),
            pltpu.VMEM((3, HALF_ROWS, 128), BF16),
            pltpu.VMEM((3, HALF_ROWS, 128), F32),
            pltpu.VMEM((3, plane, chunk, 128), BF16),
            pltpu.VMEM((3, plane, chunk, 128), BF16),
            pltpu.VMEM((3, nx, chunk, 128), BF16),
            pltpu.SemaphoreType.DMA((2, 8)),
            pltpu.SemaphoreType.DMA((2, 8)),
            pltpu.SemaphoreType.DMA,
            pltpu.SemaphoreType.DMA,
            pltpu.SemaphoreType.DMA,
            pltpu.SemaphoreType.DMA,
            pltpu.SemaphoreType.DMA((2, 3)),
            pltpu.SemaphoreType.DMA((2, 3)),
            pltpu.SemaphoreType.DMA((3, nx)),
            pltpu.SemaphoreType.DMA((3, nx)),
            pltpu.SemaphoreType.DMA((2, 3)),
            pltpu.SemaphoreType.DMA((2, 3)),
        ],
        compiler_params=pltpu.CompilerParams(
            collective_id=0, has_side_effects=True, vmem_limit_bytes=48 * 2**20
        ),
        cost_estimate=pl.CostEstimate(flops=3 * 10**9, bytes_accessed=6 * 10**6, transcendentals=2**17),
    )(
        neighbours, send_list, coarse_dest, coarse_from,
        features.reshape(2, 8, 64, 128), weight, down_weight, grad_out.reshape(2, 8, 64, 128), grad_coarse,
    )
    hidden, coarse, grad_features, grad_weight, grad_down, misfits = pl.pallas_call(
        finish_kernel,
        out_shape=[
            jax.ShapeDtypeStruct((2, 8, 64, 128), BF16),
            jax.ShapeDtypeStruct((2, 64, 128), BF16),
            jax.ShapeDtypeStruct((2, 8, 64, 128), BF16),
            jax.ShapeDtypeStruct((27, 128, 128), F32),
            jax.ShapeDtypeStruct((8, 128, 128), F32),
            jax.ShapeDtypeStruct((1,), jnp.int32),
        ],
        in_specs=[vmem] * 4,
        out_specs=[hbm] * 5 + [smem],
        scratch_shapes=[
            pltpu.VMEM((27, 128, 128), F32),
            pltpu.VMEM((8, 128, 128), F32),
            pltpu.SemaphoreType.DMA((15,)),
        ],
        compiler_params=pltpu.CompilerParams(vmem_limit_bytes=16 * 2**20),
    )(hidden, coarse, grad_features, grads)
    return (
        (hidden.reshape(features.shape), coarse, grad_features.reshape(features.shape), grad_weight, grad_down),
        misfits[0],
    )


def duplicate_kernel(count, *refs):
    sources, targets, sem = refs[:count], refs[count : 2 * count], refs[2 * count]
    for n in range(count):
        copy = pltpu.make_async_copy(sources[n], targets[n], sem.at[n])
        copy.start()
        copy.wait()


def duplicates(arrays):
    count = len(arrays)
    hbm = pl.BlockSpec(memory_space=pltpu.HBM)
    return pl.pallas_call(
        functools.partial(duplicate_kernel, count),
        out_shape=[jax.ShapeDtypeStruct(array.shape, array.dtype) for array in arrays],
        in_specs=[hbm] * count,
        out_specs=[hbm] * count,
        scratch_shapes=[pltpu.SemaphoreType.DMA((count,))],
        compiler_params=pltpu.CompilerParams(has_side_effects=True),
    )(*arrays)


def per_device(sizes, *operands):
    operands = operands[:6] + (operands[6].T,) + operands[7:]
    results, misfits = grid_path(sizes, *operands)
    _, results = lax.while_loop(
        lambda state: state[0] > 0,
        lambda state: (jnp.zeros((), jnp.int32), tuple(duplicates(general_path(*duplicates(operands))))),
        (misfits, results),
    )
    return results


def solution(mesh):
    nby = mesh.shape["by"]
    nx = {16: 4, 4: 2}[nby]
    sizes = (nx, mesh.shape["bx"] // 2, nby // nx)
    in_specs = (
        P(("bx", "by"), None, None, None, None),
        P(),
        P(),
        P(("bx", "by"), None, None, None, None),
        P(("bx", "by"), None, None),
        P(("bx", "by"), None),
        P(("bx", "by"), None),
        P(("bx", "by")),
        P(("bx", "by")),
    )
    out_specs = (
        P(("bx", "by"), None, None, None, None),
        P(("bx", "by"), None, None),
        P(("bx", "by"), None, None, None, None),
        P(),
        P(),
    )
    return jax.shard_map(
        functools.partial(per_device, sizes), mesh=mesh, in_specs=in_specs, out_specs=out_specs, check_vma=False
    )
```

```python
import functools

import jax
import jax.numpy as jnp
from jax import lax
from jax.experimental import pallas as pl
from jax.experimental.pallas import tpu as pltpu
from jax.sharding import PartitionSpec as P

OFFSETS = [(p, q, w) for p in (-1, 0, 1) for q in (-1, 0, 1) for w in (-1, 0, 1)]


def with_halo(cells, sides, width):
    for axis, dim in sides:
        count = lax.axis_size(axis)
        ends = count - 1
        head = lax.slice_in_dim(cells, 0, width, axis=dim)
        tail = lax.slice_in_dim(cells, cells.shape[dim] - width, cells.shape[dim], axis=dim)
        cells = jnp.concatenate(
            [
                lax.ppermute(tail, axis, [(i, (i + 1) % count) for i in range(ends)]),
                cells,
                lax.ppermute(head, axis, [((i + 1) % count, i) for i in range(ends)]),
            ],
            axis=dim,
        )
    return cells


def offset_index(offset):
    return (offset[0] + 1) * 9 + (offset[1] + 1) * 3 + offset[2] + 1


def span_of(step, edge_len):
    if step == -1:
        return slice(edge_len - 1, edge_len)
    if step == 1:
        return slice(0, 1)
    return slice(0, edge_len)


def assemble(piece_at):
    planes = []
    for step_x in (-1, 0, 1):
        lines = []
        for step_y in (-1, 0, 1):
            cells = [piece_at((step_x, step_y, step_z)) for step_z in (-1, 0, 1)]
            lines.append(jnp.concatenate(cells, axis=3))
        planes.append(jnp.concatenate(lines, axis=2))
    return jnp.concatenate(planes, axis=1)


def window(padded, offset, sign):
    edge_len = padded.shape[1] - 2
    starts = [1 + sign * offset[axis_id] for axis_id in range(3)]
    return padded[
        :,
        starts[0] : starts[0] + edge_len,
        starts[1] : starts[1] + edge_len,
        starts[2] : starts[2] + edge_len,
    ]


def conv_rows(padded, weight, sign):
    channels = padded.shape[-1]
    running = None
    for offset in OFFSETS:
        shifted = window(padded, offset, sign).reshape(-1, channels)
        matrix = weight[offset_index(offset)]
        if sign < 0:
            matrix = matrix.T
        term = jnp.dot(shifted, matrix, preferred_element_type=jnp.float32)
        running = term if running is None else running + term
    return running


def contract(left, right):
    return lax.dot_general(
        left, right, (((0,), (0,)), ((), ())), preferred_element_type=jnp.float32
    )


def children(hidden):
    block_count, edge_len, channels = (hidden.shape[0], hidden.shape[1], hidden.shape[-1])
    half_edge = edge_len // 2
    parted = hidden.reshape(block_count, half_edge, 2, half_edge, 2, half_edge, 2, channels)
    return [
        parted[:, :, i, :, j, :, l, :].reshape(-1, channels)
        for i in (0, 1)
        for j in (0, 1)
        for l in (0, 1)
    ]


def down_blocks(hidden, down_weight):
    block_count, channels = (hidden.shape[0], hidden.shape[-1])
    running = None
    for child_id, rows_in in enumerate(children(hidden)):
        term = jnp.dot(rows_in, down_weight[child_id], preferred_element_type=jnp.float32)
        running = term if running is None else running + term
    return running.reshape(block_count, -1, channels)


def up_blocks(coarse_grad, down_weight, edge_len):
    block_count, channels = (coarse_grad.shape[0], coarse_grad.shape[-1])
    half_edge = edge_len // 2
    flat_grad = coarse_grad.reshape(-1, channels)
    parts_list = [
        jnp.dot(flat_grad, down_weight[child_id].T, preferred_element_type=jnp.float32)
        for child_id in range(8)
    ]
    stacked = jnp.stack(parts_list).reshape(
        2, 2, 2, block_count, half_edge, half_edge, half_edge, channels
    )
    return stacked.transpose(3, 4, 0, 5, 1, 6, 2, 7).reshape(
        block_count, edge_len, edge_len, edge_len, channels
    )


def face_stack(blocks):
    return jnp.stack(
        [
            blocks[:, 0],
            blocks[:, -1],
            blocks[:, :, 0],
            blocks[:, :, -1],
            blocks[:, :, :, 0],
            blocks[:, :, :, -1],
        ],
        axis=1,
    )


def listed_faces(blocks, send_list):
    block_count = blocks.shape[0]
    all_faces = face_stack(blocks)
    zero_face = jnp.zeros((1,) + all_faces.shape[1:], all_faces.dtype)
    extended = jnp.concatenate([all_faces, zero_face], axis=0)
    picked = jnp.take(extended, jnp.where(send_list < 0, block_count, send_list), axis=0)
    return (all_faces, zero_face, picked)


def build_padded(blocks, face_pool, neighbours):
    edge_len = blocks.shape[1]

    def piece_at(offset):
        if offset == (0, 0, 0):
            return blocks
        axis_lead = [axis_id for axis_id in range(3) if offset[axis_id] != 0][0]
        face_id = 2 * axis_lead + (0 if offset[axis_lead] == 1 else 1)
        face_rows = jnp.take(face_pool, neighbours[:, offset_index(offset)] * 6 + face_id, axis=0)
        others = [axis_id for axis_id in range(3) if axis_id != axis_lead]
        face_rows = face_rows[
            :, span_of(offset[others[0]], edge_len), span_of(offset[others[1]], edge_len)
        ]
        return jnp.expand_dims(face_rows, 1 + axis_lead)

    return assemble(piece_at)


def padded_for(blocks, send_list, neighbours):
    slot_cap = send_list.shape[1]
    all_faces, zero_face, picked = listed_faces(blocks, send_list)
    outgoing = picked.reshape((3, 3) + picked.shape[1:])
    padded = with_halo(outgoing, (("bx", 0), ("by", 1)), 1)
    received = padded[::2, ::2]
    face_pool = jnp.concatenate(
        [all_faces, received.reshape((9 * slot_cap,) + all_faces.shape[1:]), zero_face], axis=0
    )
    return build_padded(blocks, face_pool.reshape((-1,) + all_faces.shape[2:]), neighbours)


def row_gathered(blocks):
    count = lax.axis_size("by")
    me = lax.axis_index("by")

    def one(step, state):
        held, gathered = state
        held = lax.ppermute(held, "by", [(i, (i + 1) % count) for i in range(count)])
        return held, gathered.at[lax.rem(me - step + count, count)].set(held)

    gathered = jnp.zeros((count,) + blocks.shape, blocks.dtype).at[me].set(blocks)
    return lax.fori_loop(1, count, one, (blocks, gathered))[1]


def summed(terms):
    for axis in ("bx", "by"):
        count, distance = lax.axis_size(axis), 1
        while distance < count:
            pairs = [(i, i ^ distance) for i in range(count)]
            terms = [term + lax.ppermute(term, axis, pairs) for term in terms]
            distance *= 2
    return terms


def general_path(
    features,
    weight,
    down_weight,
    grad_out,
    grad_coarse,
    neighbours,
    send_list,
    coarse_dest,
    coarse_from,
):
    send_list = send_list.T
    block_count, edge_len, channels = (features.shape[0], features.shape[1], features.shape[-1])
    device_total = lax.axis_size("bx") * lax.axis_size("by")
    padded_in = padded_for(features, send_list, neighbours)
    preact = conv_rows(padded_in, weight, 1).reshape(features.shape)
    hidden = jax.nn.silu(preact).astype(jnp.bfloat16)
    reduced = down_blocks(hidden, down_weight).astype(jnp.bfloat16)
    slots = jnp.arange(block_count)
    coarse = row_gathered(reduced)[coarse_from, slots]
    coarse_grad_here = row_gathered(grad_coarse)[coarse_dest, slots]
    flat_grad = coarse_grad_here.reshape(-1, channels)
    down_terms = jnp.stack([contract(rows_in, flat_grad) for rows_in in children(hidden)])
    sigmoid_pre = jax.nn.sigmoid(preact)
    grad_pre = (
        (grad_out.astype(jnp.float32) + up_blocks(coarse_grad_here, down_weight, edge_len))
        * sigmoid_pre
        * (1.0 + preact * (1.0 - sigmoid_pre))
    ).astype(jnp.bfloat16)
    padded_grad = padded_for(grad_pre, send_list, neighbours)
    grad_features = conv_rows(padded_grad, weight, -1).reshape(features.shape).astype(jnp.bfloat16)
    own_rows = grad_pre.reshape(-1, channels)
    weight_terms = jnp.stack(
        [
            contract(window(padded_in, offset, 1).reshape(-1, channels), own_rows)
            for offset in OFFSETS
        ]
    )
    weight_total, down_total = summed([weight_terms, down_terms])
    return (hidden, coarse, grad_features, weight_total / device_total, down_total / device_total)


F32, BF16 = jnp.float32, jnp.bfloat16
MESH = pl.DeviceIdType.MESH
NONE = 20
LISTS = 9
ROUTES = (("x", "y", "z"), ("y", "z", "x"), ("z", "x", "y"))
PART_ROWS = 1536
HALF_ROWS = 768


def farthest_first(ring):
    steps = [(i, j) for i in range(ring) for j in range(ring) if (i, j) != (0, 0)]
    return sorted(steps, key=lambda step: -sum(min(i, ring - i) for i in step))


def fits_grid(p, o1, o2):
    half = p // 2
    good = (half == 0) | (half == NONE // 2)
    for dr in {0, o1}:
        for dc in {0, o2}:
            if (dr, dc) != (0, 0):
                good = good | (half == (dr + 1) * 3 + dc + 2)
    return good


def section_kernel(
    sizes,
    nb_in, sl_in, cdest_in, cfrom_in, feat_in, weight_in, down_in, gout_in, gcoarse_in,
    hid_out, coarse_out, gfeat_out, fin,
    nb, sl, cdest, cfrom, feat, weight, down, gout, gcoarse, in_sem,
    pad, col, colg, xpool, ypool, cpool,
    xs, ys, cs, xr, yr, cr,
    gsend, gpool, rsend, rpool,
    wback, wpair, wdcat, small, slope, hpart, wide, cgx, up, gcat,
    arf, s0, r0, hf, s1, r1, r3,
    halo_send, halo_recv, g_send, g_recv, c_send, c_recv, plane_send, plane_recv, axis_send, axis_recv, core_send, core_recv,
):
    nx, ny, nz = sizes
    nby, nbx = nx * nz, 2 * ny
    ring = nx
    others = farthest_first(ring)
    r, c = lax.axis_index("bx"), lax.axis_index("by")
    core, at = lax.rem(r, 2), {"x": lax.rem(c, nx), "y": r // 2, "z": c // nx}
    size = {"x": nx, "y": ny, "z": nz}

    def stepped(*steps):
        to = dict(at)
        for axis, step in steps:
            to[axis] = lax.rem(at[axis] + step, ring)
        return (to["y"] * 2 + core, to["z"] * nx + to["x"])

    other_core = (r + 1 - 2 * core, c)

    def beside(dr, dc):
        return (lax.rem(r + dr + nbx, nbx), lax.rem(c + dc + nby, nby))

    around = [(dr, dc) for dr in (-1, 0, 1) for dc in (-1, 0, 1) if (dr, dc) != (0, 0)]

    barrier = pltpu.get_barrier_semaphore()

    greeted = []
    for i, j in others:
        greeted.append(stepped(("z", i), ("x", j)))
        if i != 0:
            greeted.append(stepped(("y", i), ("z", j)))
        if i != 0 and j != 0:
            greeted.append(stepped(("x", i), ("y", j)))
    greeted += [beside(dr, dc) for dr, dc in around if dr != 0]
    for device in greeted:
        pl.semaphore_signal(barrier, inc=1, device_id=device, device_id_type=MESH)

    staged = {}
    pairs = (
        ("sl", sl_in, sl), ("feat", feat_in, feat), ("cfrom", cfrom_in, cfrom), ("gcoarse", gcoarse_in, gcoarse),
        ("nb", nb_in, nb), ("down", down_in, down), ("weight", weight_in, weight), ("cdest", cdest_in, cdest),
        ("gout", gout_in, gout),
    )
    for n, (name, src, dst) in enumerate(pairs):
        staged[name] = pltpu.make_async_copy(src, dst, in_sem.at[n])
        staged[name].start()

    def fill_interior(i, carry):
        b, x = i // 8, lax.rem(i, 8)
        pad[b, x + 1, 1:9, 1:9, :] = feat[b, x].astype(F32).reshape(8, 8, 128)
        return carry

    pad[2, 1:9, 1:9] = jnp.zeros((8, 8, 16, 128), F32)
    for side in (0, 1):
        xpool[side, NONE] = jnp.zeros((8, 8, 128), F32)
        ypool[side, NONE] = jnp.zeros((8, 8, 128), F32)
    for corner in range(4):
        cpool[corner, NONE] = jnp.zeros((8, 128), F32)

    near = (8, 1)
    edge = (1, 8)

    def stage_faces(t):
        for side in (0, 1):
            step = 2 * side - 1
            for j in (0, 1):
                bx_block = jnp.maximum(sl[j, (step + 1) * 3 + 1], 0)
                face = pad[bx_block, edge[side], 1:9, 1:9, :]
                xs[t, side, 64 * j : 64 * j + 64] = face.reshape(64, 128).astype(BF16)
                by_block = jnp.maximum(sl[j, 3 + step + 1], 0)
                face = pad[by_block, 1:9, edge[side], 1:9, :]
                ys[t, side, 64 * j : 64 * j + 64] = face.reshape(64, 128).astype(BF16)
        for sx in (0, 1):
            for sy in (0, 1):
                row = 2 * sx * 3 + 2 * sy
                lines = [pad[jnp.maximum(sl[j, row], 0), edge[sx], edge[sy], 1:9, :] for j in (0, 1)]
                cs[t, 2 * sx + sy] = jnp.concatenate(lines, axis=0).astype(BF16)

    def halo_copies(t):
        out = []
        for sx in (0, 1):
            for sy in (0, 1):
                out.append((cs.at[t, 2 * sx + sy], cr.at[t, 3 - 2 * sx - sy], beside(2 * sx - 1, 2 * sy - 1)))
        for side in (0, 1):
            out.append((ys.at[t, side], yr.at[t, 1 - side], beside(0, 2 * side - 1)))
        for side in (0, 1):
            out.append((xs.at[t, side], xr.at[t, 1 - side], beside(2 * side - 1, 0)))
        return [
            pltpu.make_async_remote_copy(
                src_ref=src, dst_ref=dst, send_sem=halo_send.at[t, n], recv_sem=halo_recv.at[t, n],
                device_id=to, device_id_type=MESH,
            )
            for n, (src, dst, to) in enumerate(out)
        ]

    def local_pools():
        for side in (0, 1):
            for b in (0, 1):
                xpool[side, b] = pad[b, near[side], 1:9, 1:9, :]
                ypool[side, b] = pad[b, 1:9, near[side], 1:9, :]
        for sx in (0, 1):
            for sy in (0, 1):
                for b in (0, 1):
                    cpool[2 * sx + sy, b] = pad[b, near[sx], near[sy], 1:9, :]

    def remote_pools(t):
        for side in (0, 1):
            for j in (0, 1):
                ex, ey = 2 * side * 3 + 1, 3 + 2 * side
                xpool[side, 2 + 2 * ex + j] = xr[t, side, 64 * j : 64 * j + 64].astype(F32).reshape(8, 8, 128)
                ypool[side, 2 + 2 * ey + j] = yr[t, side, 64 * j : 64 * j + 64].astype(F32).reshape(8, 8, 128)
        for sx in (0, 1):
            for sy in (0, 1):
                lines = cr[t, 2 * sx + sy].astype(F32).reshape(2, 8, 128)
                for j in (0, 1):
                    ex, ey, ec = 2 * sx * 3 + 1, 3 + 2 * sy, 2 * sx * 3 + 2 * sy
                    cpool[2 * sx + sy, 2 + 2 * ex + j] = xpool[sx, 2 + 2 * ex + j, near[sy] - 1]
                    cpool[2 * sx + sy, 2 + 2 * ey + j] = ypool[sy, 2 + 2 * ey + j, near[sx] - 1]
                    cpool[2 * sx + sy, 2 + 2 * ec + j] = lines[j]

    def rims():
        def one(b, carry):
            for o1 in (-1, 0, 1):
                for o2 in (-1, 0, 1):
                    for o3 in (-1, 0, 1):
                        if (o1, o2, o3) == (0, 0, 0):
                            continue
                        p = nb[b, offset_index((o1, o2, o3))]
                        x, y, z = [(0, None, 9)[o + 1] for o in (o1, o2, o3)]
                        zs = (8, None, 1)[o3 + 1]
                        if o1 == 0 and o2 == 0:
                            pad[b, 1:9, 1:9, z : z + 1, :] = pad[jnp.minimum(p, 2), 1:9, 1:9, zs : zs + 1, :]
                        elif o2 == 0:
                            s = (o1 + 1) // 2
                            if o3 == 0:
                                pad[b, x, 1:9, 1:9, :] = xpool[s, p]
                            else:
                                pad[b, x, 1:9, z : z + 1, :] = xpool[s, p, :, zs - 1 : zs, :]
                        elif o1 == 0:
                            s = (o2 + 1) // 2
                            if o3 == 0:
                                pad[b, 1:9, y, 1:9, :] = ypool[s, p]
                            else:
                                pad[b, 1:9, y, z : z + 1, :] = ypool[s, p, :, zs - 1 : zs, :]
                        else:
                            s = (o1 + 1) + (o2 + 1) // 2
                            if o3 == 0:
                                pad[b, x, y, 1:9, :] = cpool[s, p]
                            else:
                                pad[b, x, y, z : z + 1, :] = cpool[s, p, zs - 1 : zs, :]
            return carry

        lax.fori_loop(0, 2, one, 0)

    def columns(dst):
        def one(i, carry):
            b, x = i // 10, lax.rem(i, 10)
            for m in range(9):
                o2, o3 = m // 3, m % 3
                cells = pad[b, x, o2 : o2 + 8, o3 : o3 + 8, :]
                dst[i, :, 128 * m : 128 * m + 128] = cells.reshape(64, 128).astype(BF16)
            return carry

        lax.fori_loop(0, 20, one, 0)

    for b in (0, 1):
        for o1 in range(3):
            for x in (8, 9):
                gcat[10 * b + (x + o1) % 10, :, 128 * o1 : 128 * o1 + 128] = jnp.zeros((64, 128), BF16)
    staged["feat"].wait()
    lax.fori_loop(0, 16, fill_interior, 0)
    staged["sl"].wait()
    stage_faces(0)
    staged["cfrom"].wait()
    staged["gcoarse"].wait()

    def row_place(step):
        return lax.rem(at["z"] + step // nx, nz) * nx + lax.rem(at["x"] + lax.rem(step, nx), nx)

    def stage_gcoarse(step, carry):
        to = row_place(step)
        gsend[step] = gcoarse[jnp.where(cfrom[1] == to, 1, 0)]
        return carry

    lax.fori_loop(0, nby, stage_gcoarse, 0)
    gpool[0] = gsend[0]

    pl.semaphore_wait(barrier, len(greeted))
    first = halo_copies(0)
    for copy in first:
        copy.start()

    def start_row(src, dst, send, recv):
        for i, j in others:
            pltpu.make_async_remote_copy(
                src_ref=src.at[i * ring + j], dst_ref=dst.at[i * ring + j], send_sem=send, recv_sem=recv,
                device_id=stepped(("z", i), ("x", j)), device_id_type=MESH,
            ).start()

    def from_row(by):
        return lax.rem(at["z"] - by // nx + nz, nz) * nx + lax.rem(at["x"] - lax.rem(by, nx) + nx, nx)

    def all_of(ref, send, recv):
        return pltpu.make_async_remote_copy(
            src_ref=ref, dst_ref=ref, send_sem=send, recv_sem=recv, device_id=other_core, device_id_type=MESH
        )

    def row_waits(buffer, send, recv):
        return all_of(buffer.at[pl.ds(1, nby - 1)], send, recv)

    start_row(gsend, gpool, g_send, g_recv)
    staged["weight"].wait()
    for k in range(27):
        wback[k // 9, :, 128 * (k % 9) : 128 * (k % 9) + 128] = weight[26 - k]
    for m in range(9):
        for o1 in (0, 1):
            wpair[m, :, 128 * o1 : 128 * o1 + 128] = weight[9 * o1 + m]
    staged["down"].wait()
    for q in range(8):
        wdcat[q // 2, :, 128 * (q % 2) : 128 * (q % 2) + 128] = down[q]
    local_pools()
    staged["nb"].wait()
    misfits = jnp.int32(0)
    for b in (0, 1):
        for offset in OFFSETS:
            good = fits_grid(nb[b, offset_index(offset)], offset[0], offset[1])
            misfits = misfits + jnp.where(good, 0, 1)
    arf[2, 1408:1536] = jnp.full((128, 128), misfits, jnp.int32).astype(F32)
    for copy in first:
        copy.wait_recv()
    remote_pools(0)
    rims()
    columns(col)

    def forward(b, carry):
        rows = col[pl.ds(b * 10, 9)].reshape(576, 1152)
        pair = jnp.dot(rows, wpair[...].reshape(1152, 256), preferred_element_type=F32)
        rows = col[pl.ds(b * 10 + 2, 8)].reshape(512, 1152)
        last = jnp.dot(rows, weight[18:27].reshape(1152, 128), preferred_element_type=F32)
        slope[b] = (pair[:512, :128] + pair[64:, 128:] + last).reshape(8, 64, 128)
        return carry

    lax.fori_loop(0, 2, forward, 0)

    def activate(i, carry):
        b, a1 = i // 4, lax.rem(i, 4)
        for p1 in (0, 1):
            x = 2 * a1 + p1
            pre = slope[b, x]
            g = jax.nn.sigmoid(pre)
            act = (pre * g).astype(BF16)
            hid_out[b, x] = act
            lines = act.astype(F32).reshape(4, 2, 8, 128)
            for p2 in (0, 1):
                at_row = pl.multiple_of(b * 128 + a1 * 32, 32)
                hpart[2 * p1 + p2, pl.ds(at_row, 32), :] = lines[:, p2].reshape(32, 128).astype(BF16)
            slope[b, x] = g * (1.0 + pre * (1.0 - g))
        return carry

    lax.fori_loop(0, 8, activate, 0)

    staged["cdest"].wait()
    staged["gout"].wait()
    row_waits(gpool, g_send, g_recv).wait_recv()
    wide[...] = jnp.zeros((2, 256, 128), F32)
    for b in (0, 1):
        block = gpool[from_row(cdest[b])].astype(F32)
        wide[0, pl.ds(128 * b, 64, stride=2), :] = block
        wide[1, pl.ds(128 * b + 1, 64, stride=2), :] = block
    cgx[:, :128] = wide[0].astype(BF16)
    cgx[:, 128:] = wide[1].astype(BF16)
    for q in range(4):
        up[q] = lax.dot_general(cgx[...], wdcat[q], (((1,), (1,)), ((), ())), preferred_element_type=F32)

    def pre_grad(i, carry):
        b, a1 = i // 4, lax.rem(i, 4)
        for p1 in (0, 1):
            x = 2 * a1 + p1
            at_row = pl.multiple_of(b * 128 + a1 * 32, 32)
            parts = [up[2 * p1 + p2, pl.ds(at_row, 32), :].reshape(4, 8, 128) for p2 in (0, 1)]
            back = jnp.stack(parts, axis=1).reshape(64, 128)
            grad = ((gout[b, x].astype(F32) + back) * slope[b, x]).astype(BF16)
            for o1 in range(3):
                gcat[b * 10 + x + o1, :, 128 * o1 : 128 * o1 + 128] = grad
            pad[b, x + 1, 1:9, 1:9, :] = grad.astype(F32).reshape(8, 8, 128)
        return carry

    lax.fori_loop(0, 8, pre_grad, 0)
    def contracted(left, right):
        return lax.dot_general(left, right, (((0,), (0,)), ((), ())), preferred_element_type=F32)

    def down_grad(q):
        both = contracted(hpart[q], cgx[...])
        for l in (0, 1):
            n = 2 * q + l
            arf[n // 3, 1152 + 128 * (n % 3) : 1280 + 128 * (n % 3)] = both[:, 128 * l : 128 * l + 128]

    my_half = pl.multiple_of(core * HALF_ROWS, HALF_ROWS)
    your_half = pl.multiple_of((1 - core) * HALF_ROWS, HALF_ROWS)

    def core_copy(part):
        return pltpu.make_async_remote_copy(
            src_ref=s0.at[part], dst_ref=r0.at[part], send_sem=core_send.at[0, part], recv_sem=core_recv.at[0, part],
            device_id=other_core, device_id_type=MESH,
        )

    def core_back(part):
        return pltpu.make_async_remote_copy(
            src_ref=fin.at[core, part], dst_ref=fin.at[core, part], send_sem=core_send.at[1, part],
            recv_sem=core_recv.at[1, part], device_id=other_core, device_id_type=MESH,
        )

    plane, chunk = ring * ring, HALF_ROWS // (ring * ring)

    def spot(part):
        a1, a2, _ = ROUTES[part]
        return at[a1] * ring + at[a2]

    def start_copies(back, part):
        a1, a2, _ = ROUTES[part]
        for i, j in others:
            if back:
                src = dst = fin.at[core, part, spot(part)]
            else:
                place = lax.rem(at[a1] + i, ring) * ring + lax.rem(at[a2] + j, ring)
                src, dst = s1.at[part, place], r1.at[part, i * ring + j]
            pltpu.make_async_remote_copy(
                src_ref=src, dst_ref=dst, send_sem=plane_send.at[back, part], recv_sem=plane_recv.at[back, part],
                device_id=stepped((a1, i), (a2, j)), device_id_type=MESH,
            ).start()

    def plane_waits(back, part):
        landed = fin.at[core, part, pl.ds(0, plane - 1)] if back else r1.at[part, pl.ds(1, plane - 1)]
        return all_of(landed, plane_send.at[back, part], plane_recv.at[back, part])

    def axis_copies(part):
        return [
            pltpu.make_async_remote_copy(
                src_ref=r3.at[part, 0], dst_ref=r3.at[part, step], send_sem=axis_send.at[part, step],
                recv_sem=axis_recv.at[part, step], device_id=stepped((ROUTES[part][2], step)), device_id_type=MESH,
            )
            for step in range(1, ring)
        ]

    def weight_grad(part):
        for mm in range(3):
            m = 3 * part + mm
            rows = col[:, :, 128 * m : 128 * m + 128].reshape(1280, 128)
            three = contracted(rows, gcat[...].reshape(1280, 384))
            for o1 in range(3):
                arf[part, 128 * (3 * o1 + mm) : 128 * (3 * o1 + mm) + 128] = three[:, 128 * o1 : 128 * o1 + 128]
        s0[part] = arf[part, pl.ds(your_half, HALF_ROWS), :].astype(BF16)
        core_copy(part).start()

    def start_plane(part):
        core_copy(part).wait_recv()
        hf[part] = arf[part, pl.ds(my_half, HALF_ROWS), :] + r0[part].astype(F32)
        s1[part] = hf[part].astype(BF16).reshape(plane, chunk, 128)
        start_copies(0, part)

    def start_axis(part):
        plane_waits(0, part).wait_recv()
        mine = hf[part, pl.ds(pl.multiple_of(spot(part) * chunk, chunk), chunk), :]
        for step in range(1, plane):
            mine = mine + r1[part, step].astype(F32)
        r3[part, 0] = mine.astype(BF16)
        for copy in axis_copies(part):
            copy.start()

    def start_back(part):
        a3 = ROUTES[part][2]
        for copy in axis_copies(part):
            copy.wait_recv()
        whole = None
        for place in range(ring):
            term = r3[part, lax.rem(at[a3] - place + ring, ring)].astype(F32)
            whole = term if whole is None else whole + term
        fin[core, part, spot(part)] = (whole * (1.0 / (nbx * nby))).astype(BF16)
        start_copies(1, part)

    for part in range(3):
        for q in ((0, 1), (2,), (3,))[part]:
            down_grad(q)
        weight_grad(part)
    for part in range(3):
        start_plane(part)
    stage_faces(1)
    second_halo = halo_copies(1)
    for copy in second_halo:
        copy.start()
    local_pools()

    total = None
    for q in range(4):
        term = jnp.dot(hpart[q], wdcat[q], preferred_element_type=F32)
        total = term if total is None else total + term
    wide[0] = total[:, :128]
    wide[1] = total[:, 128:]
    reduced = wide[0, pl.ds(0, 128, stride=2), :] + wide[1, pl.ds(1, 128, stride=2), :]
    small[...] = reduced.astype(BF16).reshape(2, 64, 128)

    def stage_reduced(step, carry):
        rsend[step] = small[jnp.where(cdest[1] == row_place(step), 1, 0)]
        return carry

    lax.fori_loop(0, nby, stage_reduced, 0)
    rpool[0] = rsend[0]

    for part in range(3):
        start_axis(part)
    start_row(rsend, rpool, c_send, c_recv)
    for copy in first:
        copy.wait_send()
    row_waits(gsend, g_send, g_recv).wait_send()
    for copy in second_halo:
        copy.wait_recv()
    remote_pools(1)
    rims()
    columns(colg)

    def backward(b, carry):
        total = None
        for o1 in range(3):
            rows = colg[pl.ds(b * 10 + o1, 8)].reshape(512, 1152)
            term = lax.dot_general(rows, wback[o1], (((1,), (1,)), ((), ())), preferred_element_type=F32)
            total = term if total is None else total + term
        gfeat_out[b] = total.astype(BF16).reshape(8, 64, 128)
        return carry

    backward(0, 0)
    for part in range(3):
        start_back(part)
    backward(1, 0)
    for copy in second_halo:
        copy.wait_send()
    for part in range(3):
        core_copy(part).wait_send()
        plane_waits(0, part).wait_send()
        for copy in axis_copies(part):
            copy.wait_send()

    row_waits(rpool, c_send, c_recv).wait_recv()
    for m in (0, 1):
        coarse_out[m] = rpool[from_row(cfrom[m])]

    for part in range(3):
        plane_waits(1, part).wait_recv()
        core_back(part).start()
    for part in range(3):
        plane_waits(1, part).wait_send()
    for part in range(3):
        core_back(part).wait_recv()

    row_waits(rsend, c_send, c_recv).wait_send()
    for part in range(3):
        core_back(part).wait_send()


def finish_kernel(hid, coarse, gfeat, fin, hid_out, coarse_out, gfeat_out, gw_out, gd_out, misfits, gw, gd, sem):
    copies = []

    def leave(src, dst):
        copies.append(pltpu.make_async_copy(src, dst, sem.at[len(copies)]))
        copies[-1].start()

    leave(hid, hid_out)
    leave(coarse, coarse_out)
    leave(gfeat, gfeat_out)
    for part in range(3):
        low = fin[0, part].reshape(HALF_ROWS, 128).astype(F32).reshape(6, 128, 128)
        high = fin[1, part].reshape(HALF_ROWS, 128).astype(F32).reshape(6, 128, 128)
        for o1, three in enumerate((low[:3], low[3:], high[:3])):
            at = pl.ds(9 * o1 + 3 * part, 3)
            gw[at] = three
            leave(gw.at[at], gw_out.at[at])
        kept = 3 if part < 2 else 2
        gd[3 * part : 3 * part + kept] = high[3 : 3 + kept]
        leave(gd.at[pl.ds(3 * part, kept)], gd_out.at[pl.ds(3 * part, kept)])
    count = fin[1, 2].reshape(HALF_ROWS, 128)[640:656].astype(F32)
    misfits[0] = (jnp.max(count) > 0).astype(jnp.int32)
    for copy in copies:
        copy.wait()


def grid_path(
    sizes, features, weight, down_weight, grad_out, grad_coarse, neighbours, send_list, coarse_dest, coarse_from
):
    nx, ny, nz = sizes
    nby = nx * nz
    plane, chunk = nx * nx, HALF_ROWS // (nx * nx)
    vmem = pl.BlockSpec(memory_space=pltpu.VMEM)
    hbm, smem = pl.BlockSpec(memory_space=pltpu.HBM), pl.BlockSpec(memory_space=pltpu.SMEM)
    hidden, coarse, grad_features, grads = pl.pallas_call(
        functools.partial(section_kernel, sizes),
        out_shape=[
            jax.ShapeDtypeStruct((2, 8, 64, 128), BF16),
            jax.ShapeDtypeStruct((2, 64, 128), BF16),
            jax.ShapeDtypeStruct((2, 8, 64, 128), BF16),
            jax.ShapeDtypeStruct((2, 3, plane, chunk, 128), BF16),
        ],
        in_specs=[hbm] * 9,
        out_specs=[vmem] * 4,
        scratch_shapes=[
            pltpu.SMEM((2, 27), jnp.int32),
            pltpu.SMEM((2, LISTS), jnp.int32),
            pltpu.SMEM((2,), jnp.int32),
            pltpu.SMEM((2,), jnp.int32),
            pltpu.VMEM((2, 8, 64, 128), BF16),
            pltpu.VMEM((27, 128, 128), BF16),
            pltpu.VMEM((8, 128, 128), BF16),
            pltpu.VMEM((2, 8, 64, 128), BF16),
            pltpu.VMEM((2, 64, 128), BF16),
            pltpu.SemaphoreType.DMA((9,)),
            pltpu.VMEM((3, 10, 10, 16, 128), F32),
            pltpu.VMEM((20, 64, 1152), BF16),
            pltpu.VMEM((20, 64, 1152), BF16),
            pltpu.VMEM((2, 21, 8, 8, 128), F32),
            pltpu.VMEM((2, 21, 8, 8, 128), F32),
            pltpu.VMEM((4, 21, 8, 128), F32),
            pltpu.VMEM((2, 2, 128, 128), BF16),
            pltpu.VMEM((2, 2, 128, 128), BF16),
            pltpu.VMEM((2, 4, 16, 128), BF16),
            pltpu.VMEM((2, 2, 128, 128), BF16),
            pltpu.VMEM((2, 2, 128, 128), BF16),
            pltpu.VMEM((2, 4, 16, 128), BF16),
            pltpu.VMEM((nby, 64, 128), BF16),
            pltpu.VMEM((nby, 64, 128), BF16),
            pltpu.VMEM((nby, 64, 128), BF16),
            pltpu.VMEM((nby, 64, 128), BF16),
            pltpu.VMEM((3, 128, 1152), BF16),
            pltpu.VMEM((9, 128, 256), BF16),
            pltpu.VMEM((4, 128, 256), BF16),
            pltpu.VMEM((2, 64, 128), BF16),
            pltpu.VMEM((2, 8, 64, 128), F32),
            pltpu.VMEM((4, 256, 128), BF16),
            pltpu.VMEM((2, 256, 128), F32),
            pltpu.VMEM((256, 256), BF16),
            pltpu.VMEM((4, 256, 128), F32),
            pltpu.VMEM((20, 64, 384), BF16),
            pltpu.VMEM((3, PART_ROWS, 128), F32),
            pltpu.VMEM((3, HALF_ROWS, 128), BF16),
            pltpu.VMEM((3, HALF_ROWS, 128), BF16),
            pltpu.VMEM((3, HALF_ROWS, 128), F32),
            pltpu.VMEM((3, plane, chunk, 128), BF16),
            pltpu.VMEM((3, plane, chunk, 128), BF16),
            pltpu.VMEM((3, nx, chunk, 128), BF16),
            pltpu.SemaphoreType.DMA((2, 8)),
            pltpu.SemaphoreType.DMA((2, 8)),
            pltpu.SemaphoreType.DMA,
            pltpu.SemaphoreType.DMA,
            pltpu.SemaphoreType.DMA,
            pltpu.SemaphoreType.DMA,
            pltpu.SemaphoreType.DMA((2, 3)),
            pltpu.SemaphoreType.DMA((2, 3)),
            pltpu.SemaphoreType.DMA((3, nx)),
            pltpu.SemaphoreType.DMA((3, nx)),
            pltpu.SemaphoreType.DMA((2, 3)),
            pltpu.SemaphoreType.DMA((2, 3)),
        ],
        compiler_params=pltpu.CompilerParams(
            collective_id=0, has_side_effects=True, vmem_limit_bytes=48 * 2**20
        ),
        cost_estimate=pl.CostEstimate(flops=3 * 10**9, bytes_accessed=6 * 10**6, transcendentals=2**17),
    )(
        neighbours, send_list, coarse_dest, coarse_from,
        features.reshape(2, 8, 64, 128), weight, down_weight, grad_out.reshape(2, 8, 64, 128), grad_coarse,
    )
    hidden, coarse, grad_features, grad_weight, grad_down, misfits = pl.pallas_call(
        finish_kernel,
        out_shape=[
            jax.ShapeDtypeStruct((2, 8, 64, 128), BF16),
            jax.ShapeDtypeStruct((2, 64, 128), BF16),
            jax.ShapeDtypeStruct((2, 8, 64, 128), BF16),
            jax.ShapeDtypeStruct((27, 128, 128), F32),
            jax.ShapeDtypeStruct((8, 128, 128), F32),
            jax.ShapeDtypeStruct((1,), jnp.int32),
        ],
        in_specs=[vmem] * 4,
        out_specs=[hbm] * 5 + [smem],
        scratch_shapes=[
            pltpu.VMEM((27, 128, 128), F32),
            pltpu.VMEM((8, 128, 128), F32),
            pltpu.SemaphoreType.DMA((15,)),
        ],
        compiler_params=pltpu.CompilerParams(vmem_limit_bytes=16 * 2**20),
    )(hidden, coarse, grad_features, grads)
    return (
        (hidden.reshape(features.shape), coarse, grad_features.reshape(features.shape), grad_weight, grad_down),
        misfits[0],
    )


def duplicate_kernel(count, *refs):
    sources, targets, sem = refs[:count], refs[count : 2 * count], refs[2 * count]
    for n in range(count):
        copy = pltpu.make_async_copy(sources[n], targets[n], sem.at[n])
        copy.start()
        copy.wait()


def duplicates(arrays):
    count = len(arrays)
    hbm = pl.BlockSpec(memory_space=pltpu.HBM)
    return pl.pallas_call(
        functools.partial(duplicate_kernel, count),
        out_shape=[jax.ShapeDtypeStruct(array.shape, array.dtype) for array in arrays],
        in_specs=[hbm] * count,
        out_specs=[hbm] * count,
        scratch_shapes=[pltpu.SemaphoreType.DMA((count,))],
        compiler_params=pltpu.CompilerParams(has_side_effects=True),
    )(*arrays)


def per_device(sizes, *operands):
    operands = operands[:6] + (operands[6].T,) + operands[7:]
    results, misfits = grid_path(sizes, *operands)
    _, results = lax.while_loop(
        lambda state: state[0] > 0,
        lambda state: (jnp.zeros((), jnp.int32), tuple(duplicates(general_path(*duplicates(operands))))),
        (misfits, results),
    )
    return results


def solution(mesh):
    nby = mesh.shape["by"]
    nx = {16: 4, 4: 2}[nby]
    sizes = (nx, mesh.shape["bx"] // 2, nby // nx)
    in_specs = (
        P(("bx", "by"), None, None, None, None),
        P(),
        P(),
        P(("bx", "by"), None, None, None, None),
        P(("bx", "by"), None, None),
        P(("bx", "by"), None),
        P(("bx", "by"), None),
        P(("bx", "by")),
        P(("bx", "by")),
    )
    out_specs = (
        P(("bx", "by"), None, None, None, None),
        P(("bx", "by"), None, None),
        P(("bx", "by"), None, None, None, None),
        P(),
        P(),
    )
    return jax.shard_map(
        functools.partial(per_device, sizes), mesh=mesh, in_specs=in_specs, out_specs=out_specs, check_vma=False
    )
```

```python
import functools

import jax
import jax.numpy as jnp
from jax import lax
from jax.experimental import pallas as pl
from jax.experimental.pallas import tpu as pltpu
from jax.sharding import PartitionSpec as P

OFFSETS = [(p, q, w) for p in (-1, 0, 1) for q in (-1, 0, 1) for w in (-1, 0, 1)]


def with_halo(cells, sides, width):
    for axis, dim in sides:
        count = lax.axis_size(axis)
        ends = count - 1
        head = lax.slice_in_dim(cells, 0, width, axis=dim)
        tail = lax.slice_in_dim(cells, cells.shape[dim] - width, cells.shape[dim], axis=dim)
        cells = jnp.concatenate(
            [
                lax.ppermute(tail, axis, [(i, (i + 1) % count) for i in range(ends)]),
                cells,
                lax.ppermute(head, axis, [((i + 1) % count, i) for i in range(ends)]),
            ],
            axis=dim,
        )
    return cells


def offset_index(offset):
    return (offset[0] + 1) * 9 + (offset[1] + 1) * 3 + offset[2] + 1


def span_of(step, edge_len):
    if step == -1:
        return slice(edge_len - 1, edge_len)
    if step == 1:
        return slice(0, 1)
    return slice(0, edge_len)


def assemble(piece_at):
    planes = []
    for step_x in (-1, 0, 1):
        lines = []
        for step_y in (-1, 0, 1):
            cells = [piece_at((step_x, step_y, step_z)) for step_z in (-1, 0, 1)]
            lines.append(jnp.concatenate(cells, axis=3))
        planes.append(jnp.concatenate(lines, axis=2))
    return jnp.concatenate(planes, axis=1)


def window(padded, offset, sign):
    edge_len = padded.shape[1] - 2
    starts = [1 + sign * offset[axis_id] for axis_id in range(3)]
    return padded[
        :,
        starts[0] : starts[0] + edge_len,
        starts[1] : starts[1] + edge_len,
        starts[2] : starts[2] + edge_len,
    ]


def conv_rows(padded, weight, sign):
    channels = padded.shape[-1]
    running = None
    for offset in OFFSETS:
        shifted = window(padded, offset, sign).reshape(-1, channels)
        matrix = weight[offset_index(offset)]
        if sign < 0:
            matrix = matrix.T
        term = jnp.dot(shifted, matrix, preferred_element_type=jnp.float32)
        running = term if running is None else running + term
    return running


def contract(left, right):
    return lax.dot_general(
        left, right, (((0,), (0,)), ((), ())), preferred_element_type=jnp.float32
    )


def children(hidden):
    block_count, edge_len, channels = (hidden.shape[0], hidden.shape[1], hidden.shape[-1])
    half_edge = edge_len // 2
    parted = hidden.reshape(block_count, half_edge, 2, half_edge, 2, half_edge, 2, channels)
    return [
        parted[:, :, i, :, j, :, l, :].reshape(-1, channels)
        for i in (0, 1)
        for j in (0, 1)
        for l in (0, 1)
    ]


def down_blocks(hidden, down_weight):
    block_count, channels = (hidden.shape[0], hidden.shape[-1])
    running = None
    for child_id, rows_in in enumerate(children(hidden)):
        term = jnp.dot(rows_in, down_weight[child_id], preferred_element_type=jnp.float32)
        running = term if running is None else running + term
    return running.reshape(block_count, -1, channels)


def up_blocks(coarse_grad, down_weight, edge_len):
    block_count, channels = (coarse_grad.shape[0], coarse_grad.shape[-1])
    half_edge = edge_len // 2
    flat_grad = coarse_grad.reshape(-1, channels)
    parts_list = [
        jnp.dot(flat_grad, down_weight[child_id].T, preferred_element_type=jnp.float32)
        for child_id in range(8)
    ]
    stacked = jnp.stack(parts_list).reshape(
        2, 2, 2, block_count, half_edge, half_edge, half_edge, channels
    )
    return stacked.transpose(3, 4, 0, 5, 1, 6, 2, 7).reshape(
        block_count, edge_len, edge_len, edge_len, channels
    )


def face_stack(blocks):
    return jnp.stack(
        [
            blocks[:, 0],
            blocks[:, -1],
            blocks[:, :, 0],
            blocks[:, :, -1],
            blocks[:, :, :, 0],
            blocks[:, :, :, -1],
        ],
        axis=1,
    )


def listed_faces(blocks, send_list):
    block_count = blocks.shape[0]
    all_faces = face_stack(blocks)
    zero_face = jnp.zeros((1,) + all_faces.shape[1:], all_faces.dtype)
    extended = jnp.concatenate([all_faces, zero_face], axis=0)
    picked = jnp.take(extended, jnp.where(send_list < 0, block_count, send_list), axis=0)
    return (all_faces, zero_face, picked)


def build_padded(blocks, face_pool, neighbours):
    edge_len = blocks.shape[1]

    def piece_at(offset):
        if offset == (0, 0, 0):
            return blocks
        axis_lead = [axis_id for axis_id in range(3) if offset[axis_id] != 0][0]
        face_id = 2 * axis_lead + (0 if offset[axis_lead] == 1 else 1)
        face_rows = jnp.take(face_pool, neighbours[:, offset_index(offset)] * 6 + face_id, axis=0)
        others = [axis_id for axis_id in range(3) if axis_id != axis_lead]
        face_rows = face_rows[
            :, span_of(offset[others[0]], edge_len), span_of(offset[others[1]], edge_len)
        ]
        return jnp.expand_dims(face_rows, 1 + axis_lead)

    return assemble(piece_at)


def padded_for(blocks, send_list, neighbours):
    slot_cap = send_list.shape[1]
    all_faces, zero_face, picked = listed_faces(blocks, send_list)
    outgoing = picked.reshape((3, 3) + picked.shape[1:])
    padded = with_halo(outgoing, (("bx", 0), ("by", 1)), 1)
    received = padded[::2, ::2]
    face_pool = jnp.concatenate(
        [all_faces, received.reshape((9 * slot_cap,) + all_faces.shape[1:]), zero_face], axis=0
    )
    return build_padded(blocks, face_pool.reshape((-1,) + all_faces.shape[2:]), neighbours)


def row_gathered(blocks):
    count = lax.axis_size("by")
    me = lax.axis_index("by")

    def one(step, state):
        held, gathered = state
        held = lax.ppermute(held, "by", [(i, (i + 1) % count) for i in range(count)])
        return held, gathered.at[lax.rem(me - step + count, count)].set(held)

    gathered = jnp.zeros((count,) + blocks.shape, blocks.dtype).at[me].set(blocks)
    return lax.fori_loop(1, count, one, (blocks, gathered))[1]


def summed(terms):
    for axis in ("bx", "by"):
        count, distance = lax.axis_size(axis), 1
        while distance < count:
            pairs = [(i, i ^ distance) for i in range(count)]
            terms = [term + lax.ppermute(term, axis, pairs) for term in terms]
            distance *= 2
    return terms


def general_path(
    features,
    weight,
    down_weight,
    grad_out,
    grad_coarse,
    neighbours,
    send_list,
    coarse_dest,
    coarse_from,
):
    send_list = send_list.T
    block_count, edge_len, channels = (features.shape[0], features.shape[1], features.shape[-1])
    device_total = lax.axis_size("bx") * lax.axis_size("by")
    padded_in = padded_for(features, send_list, neighbours)
    preact = conv_rows(padded_in, weight, 1).reshape(features.shape)
    hidden = jax.nn.silu(preact).astype(jnp.bfloat16)
    reduced = down_blocks(hidden, down_weight).astype(jnp.bfloat16)
    slots = jnp.arange(block_count)
    coarse = row_gathered(reduced)[coarse_from, slots]
    coarse_grad_here = row_gathered(grad_coarse)[coarse_dest, slots]
    flat_grad = coarse_grad_here.reshape(-1, channels)
    down_terms = jnp.stack([contract(rows_in, flat_grad) for rows_in in children(hidden)])
    sigmoid_pre = jax.nn.sigmoid(preact)
    grad_pre = (
        (grad_out.astype(jnp.float32) + up_blocks(coarse_grad_here, down_weight, edge_len))
        * sigmoid_pre
        * (1.0 + preact * (1.0 - sigmoid_pre))
    ).astype(jnp.bfloat16)
    padded_grad = padded_for(grad_pre, send_list, neighbours)
    grad_features = conv_rows(padded_grad, weight, -1).reshape(features.shape).astype(jnp.bfloat16)
    own_rows = grad_pre.reshape(-1, channels)
    weight_terms = jnp.stack(
        [
            contract(window(padded_in, offset, 1).reshape(-1, channels), own_rows)
            for offset in OFFSETS
        ]
    )
    weight_total, down_total = summed([weight_terms, down_terms])
    return (hidden, coarse, grad_features, weight_total / device_total, down_total / device_total)


F32, BF16 = jnp.float32, jnp.bfloat16
MESH = pl.DeviceIdType.MESH
NONE = 20
LISTS = 9
ROUTES = (("x", "y", "z"), ("y", "z", "x"), ("z", "x", "y"))
HALF_ROWS = 768
GROUPS = (((0, 1), (2, 3), (4, 9)), ((5, 6), (7, 8), (10, 11)))


def farthest_first(ring):
    steps = [(i, j) for i in range(ring) for j in range(ring) if (i, j) != (0, 0)]
    return sorted(steps, key=lambda step: -sum(min(i, ring - i) for i in step))


def fits_grid(p, o1, o2):
    half = p // 2
    good = (half == 0) | (half == NONE // 2)
    for dr in {0, o1}:
        for dc in {0, o2}:
            if (dr, dc) != (0, 0):
                good = good | (half == (dr + 1) * 3 + dc + 2)
    return good


def section_kernel(
    sizes,
    nb_in, sl_in, cdest_in, cfrom_in, feat_in, weight_in, down_in, gout_in, gcoarse_in,
    hid_out, coarse_out, gfeat_out, fin,
    nb, sl, cdest, cfrom, feat, weight, down, gout, gcoarse, in_sem,
    pad, col, colg, xpool, ypool, cpool,
    xs, ys, cs, xr, yr, cr,
    gsend, gpool, rsend, rpool,
    wback, wpair, wdcat, small, slope, hpart, wide, cgx, up, gcat,
    s0, r0, hf, s1, r1, r3,
    halo_send, halo_recv, g_send, g_recv, c_send, c_recv, plane_send, plane_recv, back_recv, axis_send, axis_recv, core_send, core_recv,
):
    nx, ny, nz = sizes
    nby, nbx = nx * nz, 2 * ny
    ring = nx
    others = farthest_first(ring)
    r, c = lax.axis_index("bx"), lax.axis_index("by")
    core, at = lax.rem(r, 2), {"x": lax.rem(c, nx), "y": r // 2, "z": c // nx}
    size = {"x": nx, "y": ny, "z": nz}

    def stepped(*steps):
        to = dict(at)
        for axis, step in steps:
            to[axis] = lax.rem(at[axis] + step, ring)
        return (to["y"] * 2 + core, to["z"] * nx + to["x"])

    other_core = (r + 1 - 2 * core, c)

    def beside(dr, dc):
        return (lax.rem(r + dr + nbx, nbx), lax.rem(c + dc + nby, nby))

    around = [(dr, dc) for dr in (-1, 0, 1) for dc in (-1, 0, 1) if (dr, dc) != (0, 0)]

    barrier = pltpu.get_barrier_semaphore()

    greeted = []
    for i, j in others:
        greeted.append(stepped(("z", i), ("x", j)))
        if i != 0:
            greeted.append(stepped(("y", i), ("z", j)))
        if i != 0 and j != 0:
            greeted.append(stepped(("x", i), ("y", j)))
    greeted = [beside(dr, dc) for dr, dc in around if dr != 0] + greeted
    for device in greeted:
        pl.semaphore_signal(barrier, inc=1, device_id=device, device_id_type=MESH)

    staged = {}
    pairs = (
        ("sl", sl_in, sl), ("feat", feat_in, feat), ("cfrom", cfrom_in, cfrom), ("gcoarse", gcoarse_in, gcoarse),
        ("nb", nb_in, nb), ("down", down_in, down), ("weight", weight_in, weight), ("cdest", cdest_in, cdest),
        ("gout", gout_in, gout),
    )
    for n, (name, src, dst) in enumerate(pairs):
        staged[name] = pltpu.make_async_copy(src, dst, in_sem.at[n])
        staged[name].start()

    def fill_interior(i, carry):
        b, x = i // 8, lax.rem(i, 8)
        pad[b, x + 1, 1:9, 1:9, :] = feat[b, x].astype(F32).reshape(8, 8, 128)
        return carry

    pad[2, 1:9, 1:9] = jnp.zeros((8, 8, 16, 128), F32)
    for side in (0, 1):
        xpool[side, NONE] = jnp.zeros((8, 8, 128), F32)
        ypool[side, NONE] = jnp.zeros((8, 8, 128), F32)
    for corner in range(4):
        cpool[corner, NONE] = jnp.zeros((8, 128), F32)

    near = (8, 1)
    edge = (1, 8)

    def stage_faces(t):
        for side in (0, 1):
            step = 2 * side - 1
            for j in (0, 1):
                bx_block = jnp.maximum(sl[j, (step + 1) * 3 + 1], 0)
                face = pad[bx_block, edge[side], 1:9, 1:9, :]
                xs[t, side, 64 * j : 64 * j + 64] = face.reshape(64, 128).astype(BF16)
                by_block = jnp.maximum(sl[j, 3 + step + 1], 0)
                face = pad[by_block, 1:9, edge[side], 1:9, :]
                ys[t, side, 64 * j : 64 * j + 64] = face.reshape(64, 128).astype(BF16)
        for sx in (0, 1):
            for sy in (0, 1):
                row = 2 * sx * 3 + 2 * sy
                lines = [pad[jnp.maximum(sl[j, row], 0), edge[sx], edge[sy], 1:9, :] for j in (0, 1)]
                cs[t, 2 * sx + sy] = jnp.concatenate(lines, axis=0).astype(BF16)

    def halo_copies(t):
        out = []
        for sx in (0, 1):
            for sy in (0, 1):
                out.append((cs.at[t, 2 * sx + sy], cr.at[t, 3 - 2 * sx - sy], beside(2 * sx - 1, 2 * sy - 1)))
        for side in (0, 1):
            out.append((ys.at[t, side], yr.at[t, 1 - side], beside(0, 2 * side - 1)))
        for side in (0, 1):
            out.append((xs.at[t, side], xr.at[t, 1 - side], beside(2 * side - 1, 0)))
        return [
            pltpu.make_async_remote_copy(
                src_ref=src, dst_ref=dst, send_sem=halo_send.at[t, n], recv_sem=halo_recv.at[t, n],
                device_id=to, device_id_type=MESH,
            )
            for n, (src, dst, to) in enumerate(out)
        ]

    def local_pools():
        for side in (0, 1):
            for b in (0, 1):
                xpool[side, b] = pad[b, near[side], 1:9, 1:9, :]
                ypool[side, b] = pad[b, 1:9, near[side], 1:9, :]
        for sx in (0, 1):
            for sy in (0, 1):
                for b in (0, 1):
                    cpool[2 * sx + sy, b] = pad[b, near[sx], near[sy], 1:9, :]

    def remote_pools(t):
        for side in (0, 1):
            for j in (0, 1):
                ex, ey = 2 * side * 3 + 1, 3 + 2 * side
                xpool[side, 2 + 2 * ex + j] = xr[t, side, 64 * j : 64 * j + 64].astype(F32).reshape(8, 8, 128)
                ypool[side, 2 + 2 * ey + j] = yr[t, side, 64 * j : 64 * j + 64].astype(F32).reshape(8, 8, 128)
        for sx in (0, 1):
            for sy in (0, 1):
                lines = cr[t, 2 * sx + sy].astype(F32).reshape(2, 8, 128)
                for j in (0, 1):
                    ex, ey, ec = 2 * sx * 3 + 1, 3 + 2 * sy, 2 * sx * 3 + 2 * sy
                    cpool[2 * sx + sy, 2 + 2 * ex + j] = xpool[sx, 2 + 2 * ex + j, near[sy] - 1]
                    cpool[2 * sx + sy, 2 + 2 * ey + j] = ypool[sy, 2 + 2 * ey + j, near[sx] - 1]
                    cpool[2 * sx + sy, 2 + 2 * ec + j] = lines[j]

    def rims():
        def one(b, carry):
            for o1 in (-1, 0, 1):
                for o2 in (-1, 0, 1):
                    for o3 in (-1, 0, 1):
                        if (o1, o2, o3) == (0, 0, 0):
                            continue
                        p = nb[b, offset_index((o1, o2, o3))]
                        x, y, z = [(0, None, 9)[o + 1] for o in (o1, o2, o3)]
                        zs = (8, None, 1)[o3 + 1]
                        if o1 == 0 and o2 == 0:
                            pad[b, 1:9, 1:9, z : z + 1, :] = pad[jnp.minimum(p, 2), 1:9, 1:9, zs : zs + 1, :]
                        elif o2 == 0:
                            s = (o1 + 1) // 2
                            if o3 == 0:
                                pad[b, x, 1:9, 1:9, :] = xpool[s, p]
                            else:
                                pad[b, x, 1:9, z : z + 1, :] = xpool[s, p, :, zs - 1 : zs, :]
                        elif o1 == 0:
                            s = (o2 + 1) // 2
                            if o3 == 0:
                                pad[b, 1:9, y, 1:9, :] = ypool[s, p]
                            else:
                                pad[b, 1:9, y, z : z + 1, :] = ypool[s, p, :, zs - 1 : zs, :]
                        else:
                            s = (o1 + 1) + (o2 + 1) // 2
                            if o3 == 0:
                                pad[b, x, y, 1:9, :] = cpool[s, p]
                            else:
                                pad[b, x, y, z : z + 1, :] = cpool[s, p, zs - 1 : zs, :]
            return carry

        lax.fori_loop(0, 2, one, 0)

    def columns(dst):
        def one(i, carry):
            b, x = i // 10, lax.rem(i, 10)
            for m in range(9):
                o2, o3 = m // 3, m % 3
                cells = pad[b, x, o2 : o2 + 8, o3 : o3 + 8, :]
                dst[i, :, 128 * m : 128 * m + 128] = cells.reshape(64, 128).astype(BF16)
            return carry

        lax.fori_loop(0, 20, one, 0)

    for b in (0, 1):
        for o1 in range(3):
            for x in (8, 9):
                gcat[10 * b + (x + o1) % 10, :, 128 * o1 : 128 * o1 + 128] = jnp.zeros((64, 128), BF16)
    staged["feat"].wait()
    lax.fori_loop(0, 16, fill_interior, 0)
    staged["sl"].wait()
    stage_faces(0)
    staged["cfrom"].wait()
    staged["gcoarse"].wait()

    def row_place(step):
        return lax.rem(at["z"] + step // nx, nz) * nx + lax.rem(at["x"] + lax.rem(step, nx), nx)

    def stage_gcoarse(step, carry):
        to = row_place(step)
        gsend[step] = gcoarse[jnp.where(cfrom[1] == to, 1, 0)]
        return carry

    lax.fori_loop(0, nby, stage_gcoarse, 0)
    gpool[0] = gsend[0]

    pl.semaphore_wait(barrier, len(greeted))
    first = halo_copies(0)
    for copy in first:
        copy.start()

    def start_row(src, dst, send, recv):
        for i, j in others:
            pltpu.make_async_remote_copy(
                src_ref=src.at[i * ring + j], dst_ref=dst.at[i * ring + j], send_sem=send, recv_sem=recv,
                device_id=stepped(("z", i), ("x", j)), device_id_type=MESH,
            ).start()

    def from_row(by):
        return lax.rem(at["z"] - by // nx + nz, nz) * nx + lax.rem(at["x"] - lax.rem(by, nx) + nx, nx)

    def all_of(ref, send, recv):
        return pltpu.make_async_remote_copy(
            src_ref=ref, dst_ref=ref, send_sem=send, recv_sem=recv, device_id=other_core, device_id_type=MESH
        )

    def row_waits(buffer, send, recv):
        return all_of(buffer.at[pl.ds(1, nby - 1)], send, recv)

    start_row(gsend, gpool, g_send, g_recv)
    staged["weight"].wait()
    for k in range(27):
        wback[k // 9, :, 128 * (k % 9) : 128 * (k % 9) + 128] = weight[26 - k]
    for m in range(9):
        for o1 in (0, 1):
            wpair[m, :, 128 * o1 : 128 * o1 + 128] = weight[9 * o1 + m]
    staged["down"].wait()
    for q in range(8):
        wdcat[q // 2, :, 128 * (q % 2) : 128 * (q % 2) + 128] = down[q]
    local_pools()
    staged["nb"].wait()
    misfits = jnp.int32(0)
    for b in (0, 1):
        for offset in OFFSETS:
            good = fits_grid(nb[b, offset_index(offset)], offset[0], offset[1])
            misfits = misfits + jnp.where(good, 0, 1)
    for copy in first:
        copy.wait_recv()
    remote_pools(0)
    rims()
    columns(col)

    def forward(b, carry):
        rows = col[pl.ds(b * 10, 9)].reshape(576, 1152)
        pair = jnp.dot(rows, wpair[...].reshape(1152, 256), preferred_element_type=F32)
        rows = col[pl.ds(b * 10 + 2, 8)].reshape(512, 1152)
        last = jnp.dot(rows, weight[18:27].reshape(1152, 128), preferred_element_type=F32)
        slope[b] = (pair[:512, :128] + pair[64:, 128:] + last).reshape(8, 64, 128)
        return carry

    lax.fori_loop(0, 2, forward, 0)

    def activate(i, carry):
        b, a1 = i // 4, lax.rem(i, 4)
        for p1 in (0, 1):
            x = 2 * a1 + p1
            pre = slope[b, x]
            g = jax.nn.sigmoid(pre)
            act = (pre * g).astype(BF16)
            hid_out[b, x] = act
            lines = act.astype(F32).reshape(4, 2, 8, 128)
            for p2 in (0, 1):
                at_row = pl.multiple_of(b * 128 + a1 * 32, 32)
                hpart[2 * p1 + p2, pl.ds(at_row, 32), :] = lines[:, p2].reshape(32, 128).astype(BF16)
            slope[b, x] = g * (1.0 + pre * (1.0 - g))
        return carry

    lax.fori_loop(0, 8, activate, 0)

    staged["cdest"].wait()
    staged["gout"].wait()
    row_waits(gpool, g_send, g_recv).wait_recv()
    wide[...] = jnp.zeros((2, 256, 128), F32)
    for b in (0, 1):
        block = gpool[from_row(cdest[b])].astype(F32)
        wide[0, pl.ds(128 * b, 64, stride=2), :] = block
        wide[1, pl.ds(128 * b + 1, 64, stride=2), :] = block
    cgx[:, :128] = wide[0].astype(BF16)
    cgx[:, 128:] = wide[1].astype(BF16)
    for q in range(4):
        up[q] = lax.dot_general(cgx[...], wdcat[q], (((1,), (1,)), ((), ())), preferred_element_type=F32)

    def pre_grad(i, carry):
        b, a1 = i // 4, lax.rem(i, 4)
        for p1 in (0, 1):
            x = 2 * a1 + p1
            at_row = pl.multiple_of(b * 128 + a1 * 32, 32)
            parts = [up[2 * p1 + p2, pl.ds(at_row, 32), :].reshape(4, 8, 128) for p2 in (0, 1)]
            back = jnp.stack(parts, axis=1).reshape(64, 128)
            grad = ((gout[b, x].astype(F32) + back) * slope[b, x]).astype(BF16)
            for o1 in range(3):
                gcat[b * 10 + x + o1, :, 128 * o1 : 128 * o1 + 128] = grad
            pad[b, x + 1, 1:9, 1:9, :] = grad.astype(F32).reshape(8, 8, 128)
        return carry

    lax.fori_loop(0, 8, pre_grad, 0)
    def contracted(left, right):
        return lax.dot_general(left, right, (((0,), (0,)), ((), ())), preferred_element_type=F32)

    def core_copy(part):
        return pltpu.make_async_remote_copy(
            src_ref=s0.at[part], dst_ref=r0.at[part], send_sem=core_send.at[0, part], recv_sem=core_recv.at[0, part],
            device_id=other_core, device_id_type=MESH,
        )

    def core_back(part, place):
        done = fin.at[core, part, place]
        return pltpu.make_async_remote_copy(
            src_ref=done, dst_ref=done, send_sem=core_send.at[1, part], recv_sem=core_recv.at[1, part],
            device_id=other_core, device_id_type=MESH,
        )

    def core_back_waits(part):
        return all_of(fin.at[1 - core, part], core_send.at[1, part], core_recv.at[1, part])

    plane, chunk = ring * ring, HALF_ROWS // (ring * ring)

    def spot(part):
        a1, a2, _ = ROUTES[part]
        return at[a1] * ring + at[a2]

    def start_apart(part):
        a1, a2, _ = ROUTES[part]
        for i, j in others:
            place = lax.rem(at[a1] + i, ring) * ring + lax.rem(at[a2] + j, ring)
            pltpu.make_async_remote_copy(
                src_ref=s1.at[part, place], dst_ref=r1.at[part, i * ring + j], send_sem=plane_send.at[0, part],
                recv_sem=plane_recv.at[part], device_id=stepped((a1, i), (a2, j)), device_id_type=MESH,
            ).start()

    def apart_waits(part):
        return all_of(r1.at[part, pl.ds(1, plane - 1)], plane_send.at[0, part], plane_recv.at[part])

    def back_copy(part, i, j, place):
        a1, a2, _ = ROUTES[part]
        return pltpu.make_async_remote_copy(
            src_ref=fin.at[core, part, place], dst_ref=fin.at[core, part, place], send_sem=plane_send.at[1, part],
            recv_sem=back_recv.at[part, i * ring + j], device_id=stepped((a1, i), (a2, j)), device_id_type=MESH,
        )

    def pass_on(part, i, j):
        a1, a2, _ = ROUTES[part]
        place = lax.rem(at[a1] - i + ring, ring) * ring + lax.rem(at[a2] - j + ring, ring)
        back_copy(part, i, j, place).wait_recv()
        core_back(part, place).start()

    def axis_copies(part):
        return [
            pltpu.make_async_remote_copy(
                src_ref=r3.at[part, 0], dst_ref=r3.at[part, step], send_sem=axis_send.at[part, step],
                recv_sem=axis_recv.at[part, step], device_id=stepped((ROUTES[part][2], step)), device_id_type=MESH,
            )
            for step in sorted(range(1, ring), key=lambda step: -min(step, ring - step))
        ]

    def own_terms(half, part):
        groups = GROUPS[half][part]
        count = sum(group < 9 for group in groups)
        if count:
            rows = col[:, :, 128 * groups[0] : 128 * (groups[0] + count)].reshape(1280, 128 * count)
            three = contracted(rows, gcat[...].reshape(1280, 384))
        for place, group in enumerate(groups):
            for i in range(3):
                n = 3 * (group - 9) + i
                if group < 9:
                    term = three[128 * place : 128 * place + 128, 128 * i : 128 * i + 128]
                elif n < 8:
                    term = contracted(hpart[n // 2], cgx[:, 128 * (n % 2) : 128 * (n % 2) + 128])
                else:
                    term = jnp.full((128, 128), misfits, jnp.int32).astype(F32)
                yield slice(384 * place + 128 * i, 384 * place + 128 * i + 128), term

    def terms_to_send(part):
        for half in (0, 1):
            @pl.when(core != half)
            def _(half=half):
                for at_rows, term in own_terms(half, part):
                    s0[part, at_rows] = term.astype(BF16)
        core_copy(part).start()

    def terms_to_keep(part):
        for half in (0, 1):
            @pl.when(core == half)
            def _(half=half):
                for at_rows, term in own_terms(half, part):
                    hf[part, at_rows] = term

    def start_plane(part):
        core_copy(part).wait_recv()
        hf[part] = hf[part] + r0[part].astype(F32)
        s1[part] = hf[part].astype(BF16).reshape(plane, chunk, 128)
        start_apart(part)

    def start_axis(part):
        apart_waits(part).wait_recv()
        mine = hf[part, pl.ds(pl.multiple_of(spot(part) * chunk, chunk), chunk), :]
        for step in range(1, plane):
            mine = mine + r1[part, step].astype(F32)
        r3[part, 0] = mine.astype(BF16)
        for copy in axis_copies(part):
            copy.start()

    def start_back(part):
        a3 = ROUTES[part][2]
        for copy in axis_copies(part):
            copy.wait_recv()
        whole = None
        for place in range(ring):
            term = r3[part, lax.rem(at[a3] - place + ring, ring)].astype(F32)
            whole = term if whole is None else whole + term
        fin[core, part, spot(part)] = (whole * (1.0 / (nbx * nby))).astype(BF16)
        for i, j in others:
            back_copy(part, i, j, spot(part)).start()
        core_back(part, spot(part)).start()

    for part in range(3):
        terms_to_send(part)
    for part in range(3):
        terms_to_keep(part)
        start_plane(part)
    stage_faces(1)
    second_halo = halo_copies(1)
    for copy in second_halo:
        copy.start()
    local_pools()

    total = None
    for q in range(4):
        term = jnp.dot(hpart[q], wdcat[q], preferred_element_type=F32)
        total = term if total is None else total + term
    wide[0] = total[:, :128]
    wide[1] = total[:, 128:]
    reduced = wide[0, pl.ds(0, 128, stride=2), :] + wide[1, pl.ds(1, 128, stride=2), :]
    small[...] = reduced.astype(BF16).reshape(2, 64, 128)

    def stage_reduced(step, carry):
        rsend[step] = small[jnp.where(cdest[1] == row_place(step), 1, 0)]
        return carry

    lax.fori_loop(0, nby, stage_reduced, 0)
    rpool[0] = rsend[0]

    for part in range(3):
        start_axis(part)
    start_row(rsend, rpool, c_send, c_recv)
    for copy in first:
        copy.wait_send()
    row_waits(gsend, g_send, g_recv).wait_send()
    for copy in second_halo:
        copy.wait_recv()
    remote_pools(1)
    rims()
    columns(colg)

    def backward(b, carry):
        total = None
        for o1 in range(3):
            rows = colg[pl.ds(b * 10 + o1, 8)].reshape(512, 1152)
            term = lax.dot_general(rows, wback[o1], (((1,), (1,)), ((), ())), preferred_element_type=F32)
            total = term if total is None else total + term
        gfeat_out[b] = total.astype(BF16).reshape(8, 64, 128)
        return carry

    backward(0, 0)
    for part in range(3):
        start_back(part)
    backward(1, 0)
    for copy in second_halo:
        copy.wait_send()
    for part in range(3):
        core_copy(part).wait_send()
        apart_waits(part).wait_send()
        for copy in axis_copies(part):
            copy.wait_send()

    row_waits(rpool, c_send, c_recv).wait_recv()
    for m in (0, 1):
        coarse_out[m] = rpool[from_row(cfrom[m])]

    for i, j in reversed(others):
        for part in range(3):
            pass_on(part, i, j)
    row_waits(rsend, c_send, c_recv).wait_send()
    for part in range(3):
        all_of(fin.at[core, part, pl.ds(0, plane - 1)], plane_send.at[1, part], plane_recv.at[part]).wait_send()
    for part in range(3):
        core_back_waits(part).wait_recv()
        core_back_waits(part).wait_send()


def finish_kernel(hid, coarse, gfeat, fin, hid_out, coarse_out, gfeat_out, gw_out, gd_out, misfits, gw, gd, sem):
    copies = []

    def leave(src, dst):
        copies.append(pltpu.make_async_copy(src, dst, sem.at[len(copies)]))
        copies[-1].start()

    leave(hid, hid_out)
    leave(coarse, coarse_out)
    leave(gfeat, gfeat_out)
    for part in range(3):
        for half in (0, 1):
            six = fin[half, part].reshape(HALF_ROWS, 128).astype(F32).reshape(6, 128, 128)
            first, second = GROUPS[half][part]
            if second < 9:
                for i in range(3):
                    gw[9 * i + first] = six[i]
                    gw[9 * i + second] = six[3 + i]
                    leave(gw.at[pl.ds(9 * i + first, 2)], gw_out.at[pl.ds(9 * i + first, 2)])
            elif first < 9:
                for i in range(3):
                    gw[9 * i + first] = six[i]
                    leave(gw.at[9 * i + first], gw_out.at[9 * i + first])
                gd[0:3] = six[3:]
                leave(gd.at[pl.ds(0, 3)], gd_out.at[pl.ds(0, 3)])
            else:
                gd[3:8] = six[:5]
                leave(gd.at[pl.ds(3, 5)], gd_out.at[pl.ds(3, 5)])
    count = fin[1, 2].reshape(HALF_ROWS, 128)[640:656].astype(F32)
    misfits[0] = (jnp.max(count) > 0).astype(jnp.int32)
    for copy in copies:
        copy.wait()


def grid_path(
    sizes, features, weight, down_weight, grad_out, grad_coarse, neighbours, send_list, coarse_dest, coarse_from
):
    nx, ny, nz = sizes
    nby = nx * nz
    plane, chunk = nx * nx, HALF_ROWS // (nx * nx)
    vmem = pl.BlockSpec(memory_space=pltpu.VMEM)
    hbm, smem = pl.BlockSpec(memory_space=pltpu.HBM), pl.BlockSpec(memory_space=pltpu.SMEM)
    hidden, coarse, grad_features, grads = pl.pallas_call(
        functools.partial(section_kernel, sizes),
        out_shape=[
            jax.ShapeDtypeStruct((2, 8, 64, 128), BF16),
            jax.ShapeDtypeStruct((2, 64, 128), BF16),
            jax.ShapeDtypeStruct((2, 8, 64, 128), BF16),
            jax.ShapeDtypeStruct((2, 3, plane, chunk, 128), BF16),
        ],
        in_specs=[hbm] * 9,
        out_specs=[vmem] * 4,
        scratch_shapes=[
            pltpu.SMEM((2, 27), jnp.int32),
            pltpu.SMEM((2, LISTS), jnp.int32),
            pltpu.SMEM((2,), jnp.int32),
            pltpu.SMEM((2,), jnp.int32),
            pltpu.VMEM((2, 8, 64, 128), BF16),
            pltpu.VMEM((27, 128, 128), BF16),
            pltpu.VMEM((8, 128, 128), BF16),
            pltpu.VMEM((2, 8, 64, 128), BF16),
            pltpu.VMEM((2, 64, 128), BF16),
            pltpu.SemaphoreType.DMA((9,)),
            pltpu.VMEM((3, 10, 10, 16, 128), F32),
            pltpu.VMEM((20, 64, 1152), BF16),
            pltpu.VMEM((20, 64, 1152), BF16),
            pltpu.VMEM((2, 21, 8, 8, 128), F32),
            pltpu.VMEM((2, 21, 8, 8, 128), F32),
            pltpu.VMEM((4, 21, 8, 128), F32),
            pltpu.VMEM((2, 2, 128, 128), BF16),
            pltpu.VMEM((2, 2, 128, 128), BF16),
            pltpu.VMEM((2, 4, 16, 128), BF16),
            pltpu.VMEM((2, 2, 128, 128), BF16),
            pltpu.VMEM((2, 2, 128, 128), BF16),
            pltpu.VMEM((2, 4, 16, 128), BF16),
            pltpu.VMEM((nby, 64, 128), BF16),
            pltpu.VMEM((nby, 64, 128), BF16),
            pltpu.VMEM((nby, 64, 128), BF16),
            pltpu.VMEM((nby, 64, 128), BF16),
            pltpu.VMEM((3, 128, 1152), BF16),
            pltpu.VMEM((9, 128, 256), BF16),
            pltpu.VMEM((4, 128, 256), BF16),
            pltpu.VMEM((2, 64, 128), BF16),
            pltpu.VMEM((2, 8, 64, 128), F32),
            pltpu.VMEM((4, 256, 128), BF16),
            pltpu.VMEM((2, 256, 128), F32),
            pltpu.VMEM((256, 256), BF16),
            pltpu.VMEM((4, 256, 128), F32),
            pltpu.VMEM((20, 64, 384), BF16),
            pltpu.VMEM((3, HALF_ROWS, 128), BF16),
            pltpu.VMEM((3, HALF_ROWS, 128), BF16),
            pltpu.VMEM((3, HALF_ROWS, 128), F32),
            pltpu.VMEM((3, plane, chunk, 128), BF16),
            pltpu.VMEM((3, plane, chunk, 128), BF16),
            pltpu.VMEM((3, nx, chunk, 128), BF16),
            pltpu.SemaphoreType.DMA((2, 8)),
            pltpu.SemaphoreType.DMA((2, 8)),
            pltpu.SemaphoreType.DMA,
            pltpu.SemaphoreType.DMA,
            pltpu.SemaphoreType.DMA,
            pltpu.SemaphoreType.DMA,
            pltpu.SemaphoreType.DMA((2, 3)),
            pltpu.SemaphoreType.DMA((3,)),
            pltpu.SemaphoreType.DMA((3, plane)),
            pltpu.SemaphoreType.DMA((3, nx)),
            pltpu.SemaphoreType.DMA((3, nx)),
            pltpu.SemaphoreType.DMA((2, 3)),
            pltpu.SemaphoreType.DMA((2, 3)),
        ],
        compiler_params=pltpu.CompilerParams(
            collective_id=0, has_side_effects=True, vmem_limit_bytes=48 * 2**20
        ),
        cost_estimate=pl.CostEstimate(flops=3 * 10**9, bytes_accessed=6 * 10**6, transcendentals=2**17),
    )(
        neighbours, send_list, coarse_dest, coarse_from,
        features.reshape(2, 8, 64, 128), weight, down_weight, grad_out.reshape(2, 8, 64, 128), grad_coarse,
    )
    hidden, coarse, grad_features, grad_weight, grad_down, misfits = pl.pallas_call(
        finish_kernel,
        out_shape=[
            jax.ShapeDtypeStruct((2, 8, 64, 128), BF16),
            jax.ShapeDtypeStruct((2, 64, 128), BF16),
            jax.ShapeDtypeStruct((2, 8, 64, 128), BF16),
            jax.ShapeDtypeStruct((27, 128, 128), F32),
            jax.ShapeDtypeStruct((8, 128, 128), F32),
            jax.ShapeDtypeStruct((1,), jnp.int32),
        ],
        in_specs=[vmem] * 4,
        out_specs=[hbm] * 5 + [smem],
        scratch_shapes=[
            pltpu.VMEM((27, 128, 128), F32),
            pltpu.VMEM((8, 128, 128), F32),
            pltpu.SemaphoreType.DMA((20,)),
        ],
        compiler_params=pltpu.CompilerParams(vmem_limit_bytes=16 * 2**20),
    )(hidden, coarse, grad_features, grads)
    return (
        (hidden.reshape(features.shape), coarse, grad_features.reshape(features.shape), grad_weight, grad_down),
        misfits[0],
    )


def duplicate_kernel(count, *refs):
    sources, targets, sem = refs[:count], refs[count : 2 * count], refs[2 * count]
    for n in range(count):
        copy = pltpu.make_async_copy(sources[n], targets[n], sem.at[n])
        copy.start()
        copy.wait()


def duplicates(arrays):
    count = len(arrays)
    hbm = pl.BlockSpec(memory_space=pltpu.HBM)
    return pl.pallas_call(
        functools.partial(duplicate_kernel, count),
        out_shape=[jax.ShapeDtypeStruct(array.shape, array.dtype) for array in arrays],
        in_specs=[hbm] * count,
        out_specs=[hbm] * count,
        scratch_shapes=[pltpu.SemaphoreType.DMA((count,))],
        compiler_params=pltpu.CompilerParams(has_side_effects=True),
    )(*arrays)


def per_device(sizes, *operands):
    operands = operands[:6] + (operands[6].T,) + operands[7:]
    results, misfits = grid_path(sizes, *operands)
    _, results = lax.while_loop(
        lambda state: state[0] > 0,
        lambda state: (jnp.zeros((), jnp.int32), tuple(duplicates(general_path(*duplicates(operands))))),
        (misfits, results),
    )
    return results


def solution(mesh):
    nby = mesh.shape["by"]
    nx = {16: 4, 4: 2}[nby]
    sizes = (nx, mesh.shape["bx"] // 2, nby // nx)
    in_specs = (
        P(("bx", "by"), None, None, None, None),
        P(),
        P(),
        P(("bx", "by"), None, None, None, None),
        P(("bx", "by"), None, None),
        P(("bx", "by"), None),
        P(("bx", "by"), None),
        P(("bx", "by")),
        P(("bx", "by")),
    )
    out_specs = (
        P(("bx", "by"), None, None, None, None),
        P(("bx", "by"), None, None),
        P(("bx", "by"), None, None, None, None),
        P(),
        P(),
    )
    return jax.shard_map(
        functools.partial(per_device, sizes), mesh=mesh, in_specs=in_specs, out_specs=out_specs, check_vma=False
    )
```
